32 devices in a mesh: dp: 8 (over z, y), sp: 4 (over x, core).
Axes of the slice: x: 2, y: 2, z: 4, core: 2. Of those that a mesh axis runs over, the one named last changes fastest.
Arguments:
- inputs: bfloat16 [8, 512, 1024], P('dp', 'sp'), may hold values from -6 to 6
- qkv_weight: bfloat16 [1024, 3072], P('dp'), may hold values from -0.1875 to 0.1875
- out_weight: bfloat16 [1024, 1024], P('dp'), may hold values from -1 to 1
- in_weight: bfloat16 [1024, 4096], P('dp'), may hold values from -0.1875 to 0.1875
- down_weight: bfloat16 [4096, 1024], P('dp'), may hold values from -0.09375 to 0.09375
- norm_gain: float32 [2, 1024], replicated, may hold values from 0.5 to 1.5
- norm_shift: float32 [2, 1024], replicated, may hold values from -1.8 to 1.8
- bias_table: float32 [16, 32], replicated, may hold values from -4 to 4
- segment_ids: int32 [8, 512], P('dp'), may hold values from 0 to 2, as said below
- bucket_index: int32 [512], replicated, may hold values from 0 to 31, as said below
- cotangent: bfloat16 [8, 512, 1024], P('dp', 'sp'), may hold values from -6 to 6
Outputs:
- output: bfloat16 [8, 512, 1024], P('dp', 'sp')
- input_grad: float32 [8, 512, 1024], P('dp', 'sp')
- query_key_value_gradient: float32 [1024, 3072], P('dp')
- out_grad: float32 [1024, 1024], P('dp')
- in_grad: float32 [1024, 4096], P('dp')
- down_grad: float32 [4096, 1024], P('dp')
- gain_grad: float32 [2, 1024], P(None, 'dp')
- shift_grad: float32 [2, 1024], P(None, 'dp')
- table_grad: float32 [512], P('dp')
The draws below stay inside these ranges and needn't reach their ends.
Inputs may be any that keep to these rules, and one draw needn't show every extreme that they name: `segment_ids`: in each group the item ids never fall along the sequence, and item 1 begins before position 128 and ends at or after position 384. `bucket_index`: never falls as the distance grows; equals the distance below 16.
All inputs are finite; a program needn't handle non-finite values.
Results may differ from the reference program's by a relative error of at most 0.014.
Values may be sent and summed in bfloat16 or wider, within the bound.
No kernel may reach another device: no remote copies, remote signals or barrier semaphores. Data moves between devices by JAX's collectives and lax.ppermute only.
A program may use at most 384 MiB of HBM per device.

```python
import jax
import jax.numpy as jnp
from jax import lax

D = 1024
HEADS = 16
HEAD_DIM = 64
FF = 4096
BUCKETS = 32
TOK_DEV = 128
QBLOCK = 512
SEQ = 512
GROUPS = 8


def draw_segment_ids(key, part):
    key = jax.random.fold_in(key, 11)
    first_key, second_key = jax.random.split(key)
    first_cut = jax.random.randint(first_key, (GROUPS, 1), 1, TOK_DEV)
    second_cut = jax.random.randint(second_key, (GROUPS, 1), SEQ - TOK_DEV + 1, SEQ)
    positions = jnp.arange(SEQ, dtype=jnp.int32)[None, :]
    return ((positions >= first_cut).astype(jnp.int32) + (positions >= second_cut).astype(jnp.int32)).astype(jnp.int32)


def draw_bucket_index(key, part):
    key = jax.random.fold_in(key, 23)
    exact_count = BUCKETS // 2
    breaks = jax.random.permutation(key, SEQ - exact_count - 1)[:BUCKETS - exact_count - 1].astype(jnp.int32) + exact_count + 1
    distance = jnp.arange(SEQ, dtype=jnp.int32)
    counted = jnp.sum((distance[:, None] >= breaks[None, :]).astype(jnp.int32), axis=1)
    return jnp.where(distance < exact_count, distance, exact_count + counted).astype(jnp.int32)


def block_scale(key, extent, cuts, smallest, largest):
    level, own = 1.0, jax.random.fold_in(key, 6)
    for axis_at, blocks in cuts:
        steps = jnp.exp(jax.random.uniform(jax.random.fold_in(own, axis_at), (blocks,), jnp.float32, smallest / len(cuts), largest / len(cuts)))
        level = level * jnp.repeat(steps, extent[axis_at] // blocks).reshape([-1 if axis == axis_at else 1 for axis in range(len(extent))])
    return level


def bell_draw(stream_key, dims, scale, bound, cuts=(), kind=jnp.bfloat16):
    values = scale * jax.random.normal(stream_key, dims, jnp.float32)
    if cuts:
        values = values * block_scale(stream_key, dims, cuts, -0.22, 0.18)
    return jnp.clip(values, -bound, bound).astype(kind)


def setup_inputs(seed: int = 0) -> dict:
    key_of = jax.random.split(jax.random.key(seed), 12)
    return {
        "inputs": bell_draw(key_of[0], (GROUPS, SEQ, D), 1.0, 6.0, ((0, 8), (1, 4))),
        "qkv_weight": bell_draw(key_of[1], (D, 3 * D), D ** -0.5, 0.1875, ((0, 8),)),
        "out_weight": bell_draw(key_of[2], (D, D), (D // 32) ** -0.5, 1.0, ((0, 8),)),
        "in_weight": bell_draw(key_of[3], (D, FF), D ** -0.5, 0.1875, ((0, 8),)),
        "down_weight": bell_draw(key_of[4], (FF, D), FF ** -0.5, 0.09375, ((0, 8),)),
        "norm_gain": jnp.clip(1.0 + 0.1 * jax.random.normal(key_of[5], (2, D), jnp.float32), 0.5, 1.5),
        "norm_shift": bell_draw(key_of[6], (2, D), 0.3, 1.8, (), jnp.float32),
        "bias_table": bell_draw(key_of[7], (HEADS, BUCKETS), 1.0, 4.0, (), jnp.float32),
        "segment_ids": draw_segment_ids(jax.random.fold_in(key_of[11], 71), 0),
        "bucket_index": draw_bucket_index(jax.random.fold_in(key_of[11], 71), 0),
        "cotangent": bell_draw(key_of[10], (GROUPS, SEQ, D), 1.0, 6.0, ((0, 8), (1, 4))),
    }


largest_score = lax.Precision.HIGHEST

@jax.custom_vjp
def low(v):
    return lax.optimization_barrier(v.astype(jnp.bfloat16)).astype(jnp.float32)

@jax.custom_vjp
def low_back(v):
    return v

def low_keep(v):
    return (low(v), None)

def low_pass(kept, grad):
    return (grad,)

def back_keep(v):
    return (v, None)

def back_low(kept, grad):
    return (low(grad),)
low.defvjp(low_keep, low_pass)
low_back.defvjp(back_keep, back_low)

def layer_norm(values, gain, shift):
    average = lax.optimization_barrier(jnp.mean(values, axis=-1, keepdims=True))
    centred = values - average
    variance = lax.optimization_barrier(jnp.mean(centred * centred, axis=-1, keepdims=True))
    return centred * lax.rsqrt(variance + 1e-05) * gain + shift

def matmul(left, right):
    return jnp.dot(left, right, precision=largest_score)

def group_forward(tokens, qkv_weight, out_weight, in_weight, down_weight, norm_gain, norm_shift, bias_table, seg_all, bucket_index):
    seq_len = tokens.shape[0]
    first_activation = low(layer_norm(tokens, norm_gain[0], norm_shift[0]))
    qkv_rows = low_back(low(matmul(first_activation, qkv_weight)))
    query_heads = qkv_rows[:, :D].reshape(seq_len, HEADS, HEAD_DIM)
    key_heads = qkv_rows[:, D:2 * D].reshape(seq_len, HEADS, HEAD_DIM)
    value_heads = qkv_rows[:, 2 * D:].reshape(seq_len, HEADS, HEAD_DIM)
    bias_rows = jnp.take(bias_table, bucket_index, axis=1)
    scale = HEAD_DIM ** (-0.5)
    columns = jnp.arange(seq_len, dtype=jnp.int32)

    def attend(block_start):
        positions = block_start + jnp.arange(QBLOCK, dtype=jnp.int32)
        distance = positions[:, None] - columns[None, :]
        seg_rows = lax.dynamic_slice_in_dim(seg_all, block_start, QBLOCK, 0)
        allowed = (distance >= 0) & (seg_rows[:, None] == seg_all[None, :])
        bias_block = jnp.take(bias_rows, jnp.maximum(distance, 0), axis=1)
        query_block = lax.dynamic_slice_in_dim(query_heads, block_start, QBLOCK, 0)
        raw_scores = low_back(jnp.einsum('qhd,khd->hqk', query_block, key_heads, precision=largest_score))
        scores = jnp.where(allowed[None], raw_scores * scale + bias_block, -1e+30)
        probs = low(jax.nn.softmax(scores, axis=-1))
        return jnp.einsum('hqk,khd->qhd', probs, value_heads, precision=largest_score)
    block_starts = jnp.arange(seq_len // QBLOCK, dtype=jnp.int32) * QBLOCK
    mixed = lax.map(jax.checkpoint(attend), block_starts).reshape(seq_len, D)
    attn_rows = low_back(low(mixed))
    residual = tokens + low_back(matmul(attn_rows, out_weight))
    act_two = low(layer_norm(residual, norm_gain[1], norm_shift[1]))
    hidden = low_back(matmul(act_two, in_weight))
    fed_rows = low(jax.nn.gelu(hidden))
    return residual + low_back(matmul(fed_rows, down_weight))

def reference(inputs, qkv_weight, out_weight, in_weight, down_weight, norm_gain, norm_shift, bias_table, segment_ids, bucket_index, cotangent):
    params = (qkv_weight.astype(jnp.float32), out_weight.astype(jnp.float32), in_weight.astype(jnp.float32), down_weight.astype(jnp.float32), norm_gain, norm_shift, bias_table)

    def per_group(totals, group_data):
        tokens, seg_all, upstream = group_data

        def apply_layer(tokens_in, *weights_in):
            return group_forward(tokens_in, *weights_in, seg_all, bucket_index)
        result, pullback = jax.vjp(apply_layer, tokens.astype(jnp.float32), *params)
        gradients = pullback(upstream.astype(jnp.float32))
        totals = tuple((total_one + grad_one for total_one, grad_one in zip(totals, gradients[1:])))
        return (totals, (result.astype(jnp.bfloat16), gradients[0]))
    zero_sums = tuple((jnp.zeros(param.shape, jnp.float32) for param in params))
    totals, outputs = lax.scan(per_group, zero_sums, (inputs, segment_ids, cotangent))
    output, input_grad = outputs
    return (output, input_grad, totals[0], totals[1], totals[2], totals[3], totals[4], totals[5], totals[6].reshape(-1))
```

```python
import functools

import jax
import jax.numpy as jnp
import numpy as np
from jax import lax
from jax.experimental import pallas as pl
from jax.experimental.pallas import tpu as pltpu
from jax.sharding import PartitionSpec as P

BLOCK = 128
NEG = -1e30
BF16 = jnp.bfloat16
F32 = jnp.float32


def dot(left, right, left_dim=1, right_dim=0):
    return lax.dot_general(
        left, right, (((left_dim,), (right_dim,)), ((), ())), preferred_element_type=F32
    )


def layer_norm(values, gain, shift):
    average = jnp.mean(values, axis=-1, keepdims=True)
    centred = values - average
    inverse = lax.rsqrt(jnp.mean(centred * centred, axis=-1, keepdims=True) + 1e-05)
    normed = centred * inverse
    return (normed * gain + shift, normed, inverse)


def norm_back(upstream, normed, inverse, gain):
    scaled = upstream * gain
    centre_term = jnp.mean(scaled, axis=-1, keepdims=True)
    slope_term = jnp.mean(scaled * normed, axis=-1, keepdims=True)
    return inverse * (scaled - centre_term - normed * slope_term)


def rank_at(position, count):
    position = lax.rem(position + 2 * count, count)
    return jnp.where(position < count // 2, 2 * position, 2 * (count - 1 - position) + 1)


def position_of(rank, count):
    return jnp.where(rank % 2 == 0, rank // 2, count - 1 - rank // 2)


def ring_pairs(count):
    order = list(range(0, count, 2)) + list(range(count - 1, 0, -2))
    forward = [(order[i], order[(i + 1) % count]) for i in range(count)]
    return forward, [(b, a) for a, b in forward]


def gather_dp(shard, count):
    if count != 8:
        return lax.all_gather(shard, "dp", axis=0)
    forward, backward = ring_pairs(count)
    me = lax.axis_index("dp")
    at = position_of(me, count)
    half = shard.shape[0] // 2
    whole = jnp.zeros((count,) + shard.shape, shard.dtype)
    whole = lax.dynamic_update_index_in_dim(whole, shard, me, 0)
    up = down = shard
    for step in range(1, count // 2):
        up = lax.ppermute(up, "dp", forward)
        down = lax.ppermute(down, "dp", backward)
        whole = lax.dynamic_update_index_in_dim(whole, up, rank_at(at - step, count), 0)
        whole = lax.dynamic_update_index_in_dim(whole, down, rank_at(at + step, count), 0)
    up = lax.ppermute(up[:half], "dp", forward)
    down = lax.ppermute(down[half:], "dp", backward)
    last = rank_at(at + count // 2, count)
    whole = lax.dynamic_update_slice(whole, up[None], (last, 0, 0))
    return lax.dynamic_update_slice(whole, down[None], (last, half, 0))


def scatter_dp(parts, count):
    if count != 8:
        return lax.psum_scatter(parts.astype(BF16), "dp", scatter_dimension=0).astype(F32)
    forward, backward = ring_pairs(count)
    me = lax.axis_index("dp")
    at = position_of(me, count)
    half = parts.shape[1] // 2

    def own(position):
        return lax.dynamic_index_in_dim(parts, rank_at(position, count), 0, keepdims=False).astype(F32)

    far = own(at + count // 2)
    up = lax.ppermute(far[:half].astype(BF16), "dp", forward)
    down = lax.ppermute(far[half:].astype(BF16), "dp", backward)
    for step in range(count // 2 - 1, 0, -1):
        for_up, for_down = own(at + step), own(at - step)
        if step == count // 2 - 1:
            for_up = for_up.at[:half].add(up.astype(F32))
            for_down = for_down.at[half:].add(down.astype(F32))
        else:
            for_up = for_up + up.astype(F32)
            for_down = for_down + down.astype(F32)
        up = lax.ppermute(for_up.astype(BF16), "dp", forward)
        down = lax.ppermute(for_down.astype(BF16), "dp", backward)
    return own(at) + up.astype(F32) + down.astype(F32)


def swap(values, bit):
    count = lax.axis_size("sp")
    return lax.ppermute(values, "sp", [(i, i ^ bit) for i in range(count)])


def gather_sp(piece):
    near = swap(piece, 1)
    far = swap(piece, 2)
    return [piece, near, far, swap(far, 1)]


def ordered(pieces):
    me = lax.axis_index("sp")
    whole = jnp.zeros((len(pieces),) + pieces[0].shape, pieces[0].dtype)
    for step, piece in enumerate(pieces):
        whole = lax.dynamic_update_index_in_dim(whole, piece, me ^ step, 0)
    return whole


def pick(stacked, step):
    return lax.dynamic_index_in_dim(stacked, lax.axis_index("sp") ^ step, 0, keepdims=False)


def exchange_sp(stacked):
    return ordered([pick(stacked, 0)] + [swap(pick(stacked, step), step) for step in (1, 2, 3)])


def reduce_sp(pieces):
    near = [swap(pieces[1].astype(BF16), 1), swap(pieces[3].astype(BF16), 1)]
    own = pieces[0] + near[0].astype(F32)
    far = pieces[2] + near[1].astype(F32)
    return own + swap(far.astype(BF16), 2).astype(F32)


def bias_kernel(reversed_ref, bias_ref):
    heads, diagonals, width = reversed_ref.shape
    for head in range(heads):
        for diagonal in range(diagonals):
            row = reversed_ref[head, diagonal : diagonal + 1, :]
            spread = jnp.broadcast_to(row, (BLOCK, width))
            rolled = pltpu.roll(spread, 0, 1, stride=1, stride_axis=0)
            bias_ref[head, diagonal] = rolled[:, :BLOCK]


def bias_blocks(reversed_rows):
    heads, diagonals, _ = reversed_rows.shape
    return pl.pallas_call(
        bias_kernel, out_shape=jax.ShapeDtypeStruct((heads, diagonals, BLOCK, BLOCK), F32)
    )(reversed_rows)


def mask_rows(index, seg_col_ref, seg_row_ref):
    width = (index + 1) * BLOCK
    same = seg_col_ref[index * BLOCK : width, :] == seg_row_ref[:, :width]
    row = index * BLOCK + lax.broadcasted_iota(jnp.int32, (BLOCK, width), 0)
    column = lax.broadcasted_iota(jnp.int32, (BLOCK, width), 1)
    return jnp.where(same & (row >= column), 0.0, NEG).astype(F32)


def half_mask(side):
    lane = lax.broadcasted_iota(jnp.int32, (1, BLOCK), 1)
    return (lane // (BLOCK // 2) == side).astype(F32).astype(BF16)


def score_rows(query, keys, bias_ref, head, index, mask):
    raw = dot(query, keys, 1, 1)
    bias = jnp.concatenate([bias_ref[head, index - block] for block in range(index + 1)], axis=1)
    return raw + bias + mask


def attend_kernel(scale, qkv_ref, bias_ref, seg_col_ref, seg_row_ref, attn_ref, log_ref):
    seq_len = qkv_ref.shape[0]
    columns = qkv_ref.shape[1] // 3
    lane = lax.broadcasted_iota(jnp.int32, (1, BLOCK), 1)
    for index in range(seq_len // BLOCK):
        rows = slice(index * BLOCK, (index + 1) * BLOCK)
        width = (index + 1) * BLOCK
        mask = mask_rows(index, seg_col_ref, seg_row_ref)
        logs = jnp.zeros((BLOCK, BLOCK), F32)
        for pair in range(columns // BLOCK):
            lanes = slice(pair * BLOCK, (pair + 1) * BLOCK)
            query = qkv_ref[rows, lanes] * scale
            keys = qkv_ref[:width, columns + pair * BLOCK : columns + (pair + 1) * BLOCK]
            values = qkv_ref[:width, 2 * columns + pair * BLOCK : 2 * columns + (pair + 1) * BLOCK]
            mixed = []
            for side in range(2):
                head = 2 * pair + side
                scores = score_rows(query * half_mask(side), keys, bias_ref, head, index, mask)
                largest = jnp.max(scores, axis=1, keepdims=True)
                weights = jnp.exp(scores - largest)
                total = jnp.sum(weights, axis=1, keepdims=True)
                mixed.append(dot(weights.astype(BF16), values) / total)
                logs = jnp.where(lane == head, largest + jnp.log(total), logs)
            attn_ref[rows, lanes] = jnp.where(lane < BLOCK // 2, mixed[0], mixed[1]).astype(BF16)
        log_ref[rows, :] = logs


def attend(qkv, bias, seg_col, seg_row, scale):
    seq_len = qkv.shape[0]
    return pl.pallas_call(
        functools.partial(attend_kernel, scale),
        out_shape=(
            jax.ShapeDtypeStruct((seq_len, qkv.shape[1] // 3), BF16),
            jax.ShapeDtypeStruct((seq_len, BLOCK), F32),
        ),
        compiler_params=pltpu.CompilerParams(vmem_limit_bytes=48 * 1024 * 1024),
    )(qkv, bias, seg_col, seg_row)


def attend_back_kernel(
    scale,
    qkv_ref,
    grad_ref,
    log_ref,
    bias_ref,
    seg_col_ref,
    seg_row_ref,
    grad_qkv_ref,
    sums_ref,
    key_acc,
    value_acc,
    diagonal_acc,
):
    seq_len = qkv_ref.shape[0]
    columns = qkv_ref.shape[1] // 3
    heads, diagonals = diagonal_acc.shape[:2]
    key_acc[...] = jnp.zeros_like(key_acc)
    value_acc[...] = jnp.zeros_like(value_acc)
    diagonal_acc[...] = jnp.zeros_like(diagonal_acc)
    for index in range(seq_len // BLOCK):
        rows = slice(index * BLOCK, (index + 1) * BLOCK)
        width = (index + 1) * BLOCK
        mask = mask_rows(index, seg_col_ref, seg_row_ref)
        for pair in range(columns // BLOCK):
            lanes = slice(pair * BLOCK, (pair + 1) * BLOCK)
            query = qkv_ref[rows, lanes] * scale
            keys = qkv_ref[:width, columns + pair * BLOCK : columns + (pair + 1) * BLOCK]
            values = qkv_ref[:width, 2 * columns + pair * BLOCK : 2 * columns + (pair + 1) * BLOCK]
            grad_rows = grad_ref[rows, lanes]
            grad_query = jnp.zeros((BLOCK, BLOCK), F32)
            for side in range(2):
                head = 2 * pair + side
                query_one = query * half_mask(side)
                grad_one = grad_rows * half_mask(side)
                scores = score_rows(query_one, keys, bias_ref, head, index, mask)
                probs = jnp.exp(scores - log_ref[rows, head : head + 1])
                grad_probs = dot(grad_one, values, 1, 1)
                row_term = jnp.sum(probs * grad_probs, axis=1, keepdims=True)
                grad_scores = probs * (grad_probs - row_term)
                for block in range(index + 1):
                    diagonal_acc[head, index - block] += grad_scores[
                        :, block * BLOCK : (block + 1) * BLOCK
                    ]
                grad_raw = grad_scores.astype(BF16)
                grad_query += dot(grad_raw, keys * half_mask(side))
                key_acc[:width, lanes] += dot(grad_raw, query_one, 0, 0)
                value_acc[:width, lanes] += dot(probs.astype(BF16), grad_one, 0, 0)
            grad_qkv_ref[rows, lanes] = (grad_query * scale).astype(BF16)
    grad_qkv_ref[:, columns : 2 * columns] = key_acc[...].astype(BF16)
    grad_qkv_ref[:, 2 * columns :] = value_acc[...].astype(BF16)
    row = lax.broadcasted_iota(jnp.int32, (BLOCK, BLOCK), 0)
    column = lax.broadcasted_iota(jnp.int32, (BLOCK, BLOCK), 1)
    flip = (row + column == BLOCK - 1).astype(F32)
    for head in range(heads):
        for diagonal in range(diagonals):
            block = lax.dot_general(
                diagonal_acc[head, diagonal],
                flip,
                (((1,), (0,)), ((), ())),
                precision=lax.Precision.HIGHEST,
                preferred_element_type=F32,
            )
            wide = jnp.concatenate([block, jnp.zeros_like(block)], axis=1)
            rolled = pltpu.roll(wide, 0, 1, stride=1, stride_axis=0)
            sums_ref[head, diagonal : diagonal + 1, :] = jnp.sum(rolled, axis=0, keepdims=True)


def attend_back(qkv, grad_heads, logs, bias, seg_col, seg_row, scale):
    seq_len = qkv.shape[0]
    columns = qkv.shape[1] // 3
    heads, diagonals = bias.shape[:2]
    return pl.pallas_call(
        functools.partial(attend_back_kernel, scale),
        out_shape=(
            jax.ShapeDtypeStruct(qkv.shape, BF16),
            jax.ShapeDtypeStruct((heads, diagonals, 2 * BLOCK), F32),
        ),
        scratch_shapes=[
            pltpu.VMEM((seq_len, columns), F32),
            pltpu.VMEM((seq_len, columns), F32),
            pltpu.VMEM((heads, diagonals, BLOCK, BLOCK), F32),
        ],
        compiler_params=pltpu.CompilerParams(vmem_limit_bytes=48 * 1024 * 1024),
    )(qkv, grad_heads, logs, bias, seg_col, seg_row)


def on_device(
    inputs,
    qkv_weight,
    out_weight,
    in_weight,
    down_weight,
    norm_gain,
    norm_shift,
    bias_table,
    segment_ids,
    bucket_index,
    cotangent,
):
    dp_count, sp_count = lax.axis_size("dp"), lax.axis_size("sp")
    me_sp = lax.axis_index("sp")
    tok_count, width = inputs.shape[1:]
    head_total, bucket_count = bias_table.shape
    heads_here = head_total // sp_count
    head_dim = width // head_total
    scale = head_dim ** (-0.5)
    seq_len = segment_ids.shape[1]
    rows_here = qkv_weight.shape[0]
    ff = in_weight.shape[1]
    ff_rows = ff // dp_count // sp_count
    part = width // sp_count

    def own_sp(stacked, axis):
        return lax.dynamic_index_in_dim(stacked, me_sp, axis, keepdims=False)

    qkv_part = own_sp(qkv_weight.reshape(rows_here, 3, sp_count, part), 2).reshape(rows_here, 3 * part)
    out_part = own_sp(out_weight.reshape(rows_here, sp_count, part), 1)
    in_part = own_sp(in_weight.reshape(rows_here, dp_count, sp_count, ff_rows), 2).reshape(
        rows_here, ff // sp_count
    )
    down_part = own_sp(down_weight.reshape(sp_count, ff_rows, width), 0)
    full_qkv = gather_dp(qkv_part, dp_count).reshape(width, 3 * part)
    in_out = gather_dp(jnp.concatenate([out_part, in_part], axis=1), dp_count).reshape(width, -1)
    out_columns, full_in = in_out[:, :part], in_out[:, part:]
    full_down = gather_dp(down_part, dp_count).reshape(ff // sp_count, width)
    full_out = jnp.moveaxis(ordered(gather_sp(out_columns)), 0, 1).reshape(width, width)

    diagonals = seq_len // BLOCK
    place = np.arange(2 * BLOCK)
    distance = BLOCK * np.arange(diagonals)[:, None] + np.where(place <= BLOCK, -place, 2 * BLOCK - place)
    bucket_rows = bucket_index[np.clip(distance, 0, seq_len - 1)]
    summed = BLOCK * np.arange(diagonals)[:, None] + place - (BLOCK - 1)
    sum_buckets = bucket_index[np.clip(summed, 0, seq_len - 1)]
    sum_onehot = (sum_buckets[..., None] == jnp.arange(bucket_count)).astype(F32)
    table_here = lax.dynamic_slice_in_dim(bias_table, me_sp * heads_here, heads_here, 0)
    onehot = (bucket_rows[..., None] == jnp.arange(bucket_count)).astype(F32)
    reversed_rows = jnp.sum(table_here[:, None, None, :] * onehot[None], axis=-1)
    bias = bias_blocks(reversed_rows)
    seg_row = segment_ids
    seg_col = segment_ids.reshape(seq_len, 1)

    tokens_all = ordered(gather_sp(inputs[0])).reshape(seq_len, width).astype(F32)
    normed_out_one, normed_one, inverse_one = layer_norm(tokens_all, norm_gain[0], norm_shift[0])
    act_one = normed_out_one.astype(BF16)
    tokens = inputs[0].astype(F32)
    upstream = cotangent[0].astype(F32)
    upstream_all = jnp.concatenate(gather_sp(cotangent[0]), axis=0)
    qkv = dot(act_one, full_qkv).astype(BF16)
    attn, logs = attend(qkv, bias, seg_col, seg_row, scale)
    attn_all = ordered(gather_sp(attn))
    attn_rows = lax.dynamic_slice_in_dim(attn_all, me_sp * tok_count, tok_count, 1)
    attn_rows = jnp.moveaxis(attn_rows, 0, 1).reshape(tok_count, width)
    residual = tokens + dot(attn_rows, full_out)
    normed_out_two, normed_two, inverse_two = layer_norm(residual, norm_gain[1], norm_shift[1])
    act_two = jnp.concatenate(gather_sp(normed_out_two.astype(BF16)), axis=0)
    hidden = dot(act_two, full_in)
    activated, gelu_back = jax.vjp(jax.nn.gelu, hidden)
    fed = activated.astype(BF16)

    grad_fed = dot(upstream_all, full_down, 1, 1)
    grad_hidden = gelu_back(grad_fed)[0].astype(BF16)
    grad_act_two = reduce_sp(list(dot(grad_hidden, full_in, 1, 1).reshape(sp_count, tok_count, width)))
    grad_down = dot(fed, upstream_all, 0, 0)
    grad_in = dot(act_two, grad_hidden, 0, 0)
    output = residual + reduce_sp(list(dot(fed, full_down).reshape(sp_count, tok_count, width)))

    gain_two = jnp.sum(grad_act_two * normed_two, axis=0)
    shift_two = jnp.sum(grad_act_two, axis=0)
    grad_resid = upstream + norm_back(grad_act_two, normed_two, inverse_two, norm_gain[1])
    grad_branch = grad_resid.astype(BF16)
    grad_attn_rows = dot(grad_branch, full_out, 1, 1).astype(BF16)
    grad_heads = exchange_sp(
        jnp.moveaxis(grad_attn_rows.reshape(tok_count, sp_count, part), 1, 0)
    ).reshape(seq_len, part)
    grad_branch_columns = exchange_sp(
        jnp.moveaxis(grad_branch.reshape(tok_count, sp_count, part), 1, 0)
    ).reshape(seq_len, part)
    grad_out = jnp.concatenate(
        [dot(attn_all[step], grad_branch_columns, 0, 0) for step in range(sp_count)], axis=0
    )
    grad_qkv_here, diagonal_sums = attend_back(qkv, grad_heads, logs, bias, seg_col, seg_row, scale)
    table_here_grad = lax.dot_general(
        diagonal_sums, sum_onehot, (((1, 2), (0, 1)), ((), ())), precision=lax.Precision.HIGHEST
    )
    grad_qkv = dot(act_one, grad_qkv_here, 0, 0)
    partial_one = dot(grad_qkv_here, full_qkv, 1, 1)
    gain_one = jnp.sum(partial_one * normed_one, axis=0)
    shift_one = jnp.sum(partial_one, axis=0)
    stacked_one = partial_one.reshape(sp_count, tok_count, width)
    grad_act_one = reduce_sp([pick(stacked_one, step) for step in range(sp_count)])

    def mine(values):
        return lax.dynamic_slice_in_dim(values, me_sp * tok_count, tok_count, 0)

    grad_input = grad_resid + norm_back(
        grad_act_one, mine(normed_one), mine(inverse_one), norm_gain[0]
    )

    table_whole = lax.dynamic_update_slice_in_dim(
        jnp.zeros((head_total, bucket_count), F32), table_here_grad, me_sp * heads_here, 0
    )
    small = jnp.concatenate(
        [
            value.reshape(dp_count, -1)
            for value in (gain_one, gain_two, shift_one, shift_two, table_whole)
        ],
        axis=1,
    )
    small_count = small.shape[1]
    small = jnp.pad(small, ((0, 0), (0, 16 * 4 * part - small_count))).reshape(dp_count, 16, 4 * part)
    sum_down = scatter_dp(grad_down.reshape(dp_count, ff_rows, width), dp_count)
    sum_in = scatter_dp(grad_in.reshape(dp_count, rows_here, ff // sp_count), dp_count)
    last = jnp.concatenate(
        [
            jnp.concatenate([grad_qkv, grad_out], axis=1).reshape(dp_count, rows_here, 4 * part),
            small,
        ],
        axis=1,
    )
    sum_last = scatter_dp(last, dp_count)

    all_down = ordered(gather_sp(sum_down.astype(BF16))).astype(F32)
    all_in = ordered(gather_sp(sum_in.astype(BF16))).astype(F32)
    all_last = ordered(gather_sp(sum_last.astype(BF16))).astype(F32)
    out_down = all_down.reshape(sp_count * ff_rows, width)
    out_in = jnp.moveaxis(all_in.reshape(sp_count, rows_here, dp_count, ff_rows), 0, 2).reshape(
        rows_here, ff
    )
    out_qkv = jnp.moveaxis(
        all_last[:, :rows_here, : 3 * part].reshape(sp_count, rows_here, 3, part), 0, 2
    ).reshape(rows_here, 3 * width)
    out_out = jnp.moveaxis(all_last[:, :rows_here, 3 * part :], 0, 1).reshape(rows_here, width)
    small_sum = jnp.sum(all_last[:, rows_here:], axis=0).reshape(-1)
    piece = width // dp_count
    gains = small_sum[: 2 * piece].reshape(2, piece)
    shifts = small_sum[2 * piece : 4 * piece].reshape(2, piece)
    tables = small_sum[4 * piece : small_count]
    return (
        output.astype(BF16)[None],
        grad_input[None],
        out_qkv,
        out_out,
        out_in,
        out_down,
        gains,
        shifts,
        tables,
    )


def solution(mesh):
    in_specs = (
        P("dp", "sp", None),
        P("dp", None),
        P("dp", None),
        P("dp", None),
        P("dp", None),
        P(),
        P(),
        P(),
        P("dp", None),
        P(),
        P("dp", "sp", None),
    )
    out_specs = (
        P("dp", "sp", None),
        P("dp", "sp", None),
        P("dp", None),
        P("dp", None),
        P("dp", None),
        P("dp", None),
        P(None, "dp"),
        P(None, "dp"),
        P("dp"),
    )
    return jax.shard_map(
        on_device, mesh=mesh, in_specs=in_specs, out_specs=out_specs, check_vma=False
    )
```

```python
import functools

import jax
import jax.numpy as jnp
from jax import lax
from jax.experimental import pallas as pl
from jax.experimental.pallas import tpu as pltpu
from jax.sharding import PartitionSpec as P

BLOCK = 128
SMALL_ROWS = 16
NEG = -1e30
BF16 = jnp.bfloat16
F32 = jnp.float32
VMEM_LIMIT = 56 * 1024 * 1024
ROOT = 0.7978845608028654
CUBE = 0.044715


def dot(left, right, left_dim=1, right_dim=0):
    return lax.dot_general(
        left, right, (((left_dim,), (right_dim,)), ((), ())), preferred_element_type=F32
    )


def layer_norm(values):
    average = jnp.mean(values, axis=-1, keepdims=True)
    centred = values - average
    inverse = lax.rsqrt(jnp.mean(centred * centred, axis=-1, keepdims=True) + 1e-05)
    return centred * inverse, inverse


def norm_back(upstream, normed, inverse, gain):
    scaled = upstream * gain
    centre_term = jnp.mean(scaled, axis=-1, keepdims=True)
    slope_term = jnp.mean(scaled * normed, axis=-1, keepdims=True)
    return inverse * (scaled - centre_term - normed * slope_term)


def shaped(shape, dtype):
    return jax.ShapeDtypeStruct(tuple(shape), dtype)


def call(kernel, outs, args, any_args=(), smem_args=(), scratch=(), cost=(0, 0)):
    specs = [pl.BlockSpec(memory_space=pltpu.VMEM)] * len(args)
    specs += [pl.BlockSpec(memory_space=pl.ANY)] * len(any_args)
    specs += [pl.BlockSpec(memory_space=pltpu.SMEM)] * len(smem_args)
    return pl.pallas_call(
        kernel,
        out_shape=tuple(outs),
        in_specs=specs,
        out_specs=tuple(pl.BlockSpec(memory_space=pltpu.VMEM) for _ in outs),
        scratch_shapes=list(scratch),
        compiler_params=pltpu.CompilerParams(vmem_limit_bytes=VMEM_LIMIT),
        cost_estimate=pl.CostEstimate(flops=cost[0], bytes_accessed=cost[1], transcendentals=0),
    )(*args, *any_args, *smem_args)


def rank_at(position, count):
    position = lax.rem(position + 2 * count, count)
    return jnp.where(position < count // 2, 2 * position, 2 * (count - 1 - position) + 1)


def position_of(rank, count):
    return jnp.where(rank % 2 == 0, rank // 2, count - 1 - rank // 2)


def ring_pairs(count):
    order = list(range(0, count, 2)) + list(range(count - 1, 0, -2))
    forward = [(order[i], order[(i + 1) % count]) for i in range(count)]
    return forward, [(b, a) for a, b in forward]


def half_rows(rows):
    return rows // 2 // 16 * 16


def gather_offsets(rows, count):
    if count != 8:
        return jnp.zeros((1,), jnp.int32)
    at = position_of(lax.axis_index("dp"), count)
    steps = [0, -1, 1, -2, 2, -3, 3, 4]
    places = [rank_at(at + step, count) * rows for step in steps]
    return jnp.stack(places + [places[-1] + half_rows(rows)]).astype(jnp.int32)


def gather_dp(shard, count):
    if count != 8:
        return [lax.all_gather(shard, "dp", axis=0, tiled=True)]
    forward, backward = ring_pairs(count)
    half = half_rows(shard.shape[0])
    pieces = [shard]
    up = down = shard
    for step in range(1, count // 2):
        up = lax.ppermute(up, "dp", forward)
        down = lax.ppermute(down, "dp", backward)
        pieces += [up, down]
    up = lax.ppermute(up[:half], "dp", forward)
    down = lax.ppermute(down[half:], "dp", backward)
    return pieces + [up, down]


def scatter_dp(parts, count):
    if count != 8:
        return lax.psum_scatter(parts, "dp", scatter_dimension=0)
    forward, backward = ring_pairs(count)
    at = position_of(lax.axis_index("dp"), count)
    half = half_rows(parts.shape[1])

    def own(position):
        return lax.dynamic_index_in_dim(parts, rank_at(position, count), 0, keepdims=False)

    far = own(at + count // 2)
    up = lax.ppermute(far[:half], "dp", forward)
    down = lax.ppermute(far[half:], "dp", backward)
    for step in range(count // 2 - 1, 0, -1):
        for_up, for_down = own(at + step).astype(F32), own(at - step).astype(F32)
        if step == count // 2 - 1:
            up = jnp.pad(up, ((0, parts.shape[1] - half), (0, 0)))
            down = jnp.pad(down, ((half, 0), (0, 0)))
        up = lax.ppermute((for_up + up.astype(F32)).astype(BF16), "dp", forward)
        down = lax.ppermute((for_down + down.astype(F32)).astype(BF16), "dp", backward)
    return (own(at).astype(F32) + up.astype(F32) + down.astype(F32)).astype(BF16)


def swap(values, bit):
    count = lax.axis_size("sp")
    return lax.ppermute(values, "sp", [(i, i ^ bit) for i in range(count)])


def gather_sp(piece):
    far = swap(piece, 2)
    near = swap(piece, 1)
    return [piece, near, far, swap(far, 1)]


def reduce_sp(far, send):
    near = swap(send, 1)
    tok = far.shape[0]
    return near, swap((far + near[tok:].astype(F32)).astype(BF16), 2)


def place(step, size, me_ref):
    return pl.multiple_of((me_ref[0] ^ step) * size, size)


def load(pieces, offsets_ref, target, sems, lanes=slice(None)):
    copies = []
    for at, piece in enumerate(pieces):
        rows = pl.ds(pl.multiple_of(offsets_ref[at], 16), piece.shape[0])
        copies.append(pltpu.make_async_copy(piece.at[:, lanes], target.at[rows, :], sems.at[at]))
    for copy in copies:
        copy.start()
    return copies


def finish(copies):
    for copy in copies:
        copy.wait()


def share_kernel(plan, refs):
    *sources, me_ref, target, sems = refs
    copies = []
    for at, (source, axis, start, step, size, to) in enumerate(plan):
        start = pl.multiple_of(start + step * me_ref[0], step)
        block = sources[source]
        if axis == 1:
            block = block.at[:, pl.ds(start, size)]
        else:
            block = block.at[pl.ds(start, size), :]
        copies.append(pltpu.make_async_copy(block, target.at[:, to : to + size if axis else None], sems.at[at]))
    for copy in copies:
        copy.start()
    finish(copies)


def share(sources, me, plan, rows):
    columns = sum(size if axis else sources[source].shape[1] for source, axis, _, _, size, _ in plan)

    def kernel(*refs):
        share_kernel(plan, refs)

    return call(
        kernel,
        [shaped((rows, columns), BF16)],
        [],
        sources,
        [me],
        [pltpu.SemaphoreType.DMA((len(plan),))],
        (0, 4 * rows * columns),
    )[0]


def bias_kernel(table_ref, bucket_ref, bias_ref):
    heads, diagonals = bias_ref.shape[:2]
    wide = bucket_ref.shape[1]
    bucket = lax.broadcasted_iota(jnp.int32, (table_ref.shape[1], wide), 0)
    chosen = (bucket == bucket_ref[...]).astype(F32)
    rows = lax.dot_general(
        table_ref[...],
        chosen,
        (((1,), (0,)), ((), ())),
        precision=lax.Precision.HIGHEST,
        preferred_element_type=F32,
    )
    for head in range(heads):
        for diagonal in range(diagonals):
            start = wide - (diagonal + 2) * BLOCK
            row = rows[head : head + 1, start : start + 2 * BLOCK]
            spread = jnp.broadcast_to(row, (BLOCK, 2 * BLOCK))
            rolled = pltpu.roll(spread, BLOCK, 1, stride=1, stride_axis=0)
            bias_ref[head, diagonal] = rolled[:, :BLOCK]


def norm_kernel(*refs):
    *pieces, gain_ref, shift_ref, me_ref, act_ref, normed_ref = refs
    for step, piece in enumerate(pieces):
        rows = pl.ds(place(step, piece.shape[0], me_ref), piece.shape[0])
        normed, _ = layer_norm(piece[...].astype(F32))
        act_ref[rows, :] = (normed * gain_ref[0:1, :] + shift_ref[0:1, :]).astype(BF16)
        normed_ref[rows, :] = normed.astype(BF16)


def mask_rows(index, seg_col_ref, seg_row_ref):
    width = (index + 1) * BLOCK
    same = seg_col_ref[index * BLOCK : width, :] == seg_row_ref[:, :width]
    row = index * BLOCK + lax.broadcasted_iota(jnp.int32, (BLOCK, width), 0)
    column = lax.broadcasted_iota(jnp.int32, (BLOCK, width), 1)
    return jnp.where(same & (row >= column), 0.0, NEG).astype(F32)


def half_mask(side):
    lane = lax.broadcasted_iota(jnp.int32, (1, BLOCK), 1)
    return (lane // (BLOCK // 2) == side).astype(F32).astype(BF16)


def score_rows(query, keys, bias_ref, head, index, mask):
    raw = dot(query, keys, 1, 1)
    bias = jnp.concatenate([bias_ref[head, index - block] for block in range(index + 1)], axis=1)
    return raw + bias + mask


def attend_kernel(scale, count, *refs):
    act_ref, bias_ref, seg_col_ref, seg_row_ref = refs[:4]
    pieces, offsets_ref = refs[4 : 4 + count], refs[4 + count]
    qkv_ref, attn_ref, log_ref, weight, sems = refs[5 + count :]
    copies = load(pieces, offsets_ref, weight, sems)
    seq_len = qkv_ref.shape[0]
    columns = qkv_ref.shape[1] // 3
    lane = lax.broadcasted_iota(jnp.int32, (1, BLOCK), 1)
    finish(copies)
    for index in range(seq_len // BLOCK):
        rows = slice(index * BLOCK, (index + 1) * BLOCK)
        qkv_ref[rows, :] = dot(act_ref[rows, :], weight[...]).astype(BF16)
    for index in range(seq_len // BLOCK):
        rows = slice(index * BLOCK, (index + 1) * BLOCK)
        width = (index + 1) * BLOCK
        mask = mask_rows(index, seg_col_ref, seg_row_ref)
        logs = jnp.zeros((BLOCK, BLOCK), F32)
        for pair in range(columns // BLOCK):
            lanes = slice(pair * BLOCK, (pair + 1) * BLOCK)
            query = qkv_ref[rows, lanes] * scale
            keys = qkv_ref[:width, columns + pair * BLOCK : columns + (pair + 1) * BLOCK]
            values = qkv_ref[:width, 2 * columns + pair * BLOCK : 2 * columns + (pair + 1) * BLOCK]
            mixed = []
            for side in range(2):
                head = 2 * pair + side
                scores = score_rows(query * half_mask(side), keys, bias_ref, head, index, mask)
                largest = jnp.max(scores, axis=1, keepdims=True)
                weights = jnp.exp(scores - largest)
                total = jnp.sum(weights, axis=1, keepdims=True)
                mixed.append(dot(weights.astype(BF16), values) / total)
                logs = jnp.where(lane == head, largest + jnp.log(total), logs)
            attn_ref[rows, lanes] = jnp.where(lane < BLOCK // 2, mixed[0], mixed[1]).astype(BF16)
        log_ref[rows, :] = logs


def branch_kernel(*refs):
    attn_refs, weight_refs = refs[:4], refs[4:8]
    tokens_ref, gain_ref, shift_ref, me_ref, resid_ref, act_ref, own = refs[8:]
    tok = tokens_ref.shape[0]
    part = weight_refs[0].shape[1]
    for step, attn in enumerate(attn_refs):
        own[:, pl.ds(place(step, part, me_ref), part)] = attn[pl.ds(place(0, tok, me_ref), tok), :]
    for step, weight in enumerate(weight_refs):
        columns = pl.ds(place(step, part, me_ref), part)
        resid_ref[:, columns] = tokens_ref[:, columns].astype(F32) + dot(own[...], weight[...])
    normed, _ = layer_norm(resid_ref[...])
    act_ref[...] = (normed * gain_ref[1:2, :] + shift_ref[1:2, :]).astype(BF16)


def feed_kernel(count, part, *refs):
    act_refs, up_refs, pieces = refs[:4], refs[4:8], refs[8 : 8 + count]
    offsets_ref, fed_ref, slope_ref, grad_ref, weight, upstream, sems = refs[8 + count :]
    copies = load(pieces, offsets_ref, weight, sems, slice(part, None))
    tok = act_refs[0].shape[0]
    for step, up in enumerate(up_refs):
        upstream[step * tok : (step + 1) * tok, :] = up[...]
    finish(copies)
    for step, act in enumerate(act_refs):
        rows = slice(step * tok, (step + 1) * tok)
        hidden = dot(act[...], weight[...])
        square = hidden * hidden
        bend = jnp.tanh(ROOT * hidden * (1.0 + CUBE * square))
        fed_ref[rows, :] = (0.5 * hidden * (1.0 + bend)).astype(BF16)
        slope_ref[rows, :] = 0.5 * (1.0 + bend) + 0.5 * hidden * (1.0 - bend * bend) * ROOT * (
            1.0 + 3.0 * CUBE * square
        )
    width = grad_ref.shape[0]
    for start in range(0, width, 2 * BLOCK):
        rows = slice(start, start + 2 * BLOCK)
        grad_ref[rows, :] = dot(fed_ref[:, rows], upstream[...], 0, 0).astype(BF16)


def feed_back_kernel(count, part, *refs):
    slope_ref, up_refs = refs[0], refs[1:5]
    down_refs, in_refs = refs[5 : 5 + count], refs[5 + count : 5 + 2 * count]
    down_at, in_at = refs[5 + 2 * count : 7 + 2 * count]
    hidden_ref, own_ref, far_ref, send_ref, down, weight, down_sems, in_sems = refs[7 + 2 * count :]
    down_copies = load(down_refs, down_at, down, down_sems)
    in_copies = load(in_refs, in_at, weight, in_sems, slice(part, None))
    tok = up_refs[0].shape[0]
    finish(down_copies)
    finish(in_copies)
    for step, up in enumerate(up_refs):
        rows = slice(step * tok, (step + 1) * tok)
        grad = (dot(up[...], down[...], 1, 1) * slope_ref[rows, :]).astype(BF16)
        hidden_ref[rows, :] = grad
        share_of = dot(grad, weight[...], 1, 1)
        if step == 0:
            own_ref[...] = share_of
        elif step == 2:
            far_ref[...] = share_of
        else:
            send_ref[(step // 2) * tok : (step // 2 + 1) * tok, :] = share_of.astype(BF16)


def feed_rest_kernel(count, *refs):
    fed_ref, hidden_ref, act_refs, down_refs = refs[0], refs[1], refs[2:6], refs[6 : 6 + count]
    down_at, grad_ref, own_ref, far_ref, send_ref, act_all, down, sems = refs[6 + count :]
    copies = load(down_refs, down_at, down, sems)
    tok = act_refs[0].shape[0]
    for step, act in enumerate(act_refs):
        act_all[step * tok : (step + 1) * tok, :] = act[...]
    for start in range(0, grad_ref.shape[0], 2 * BLOCK):
        rows = slice(start, start + 2 * BLOCK)
        grad_ref[rows, :] = dot(act_all[:, rows], hidden_ref[...], 0, 0).astype(BF16)
    finish(copies)
    for step in range(4):
        share_of = dot(fed_ref[step * tok : (step + 1) * tok, :], down[...])
        if step == 0:
            own_ref[...] = share_of
        elif step == 2:
            far_ref[...] = share_of
        else:
            send_ref[(step // 2) * tok : (step // 2 + 1) * tok, :] = share_of.astype(BF16)


def branch_back_kernel(*refs):
    own_ref, near_ref, far_ref, resid_ref, up_ref, gain_ref = refs[:6]
    weight_refs, me_ref, grad_ref, sums_ref = refs[6:10], refs[10], refs[11], refs[12]
    send_refs, branch, grad_attn = refs[13:17], refs[17], refs[18]
    tok = up_ref.shape[0]
    part = weight_refs[0].shape[1]
    upstream = own_ref[...] + near_ref[:tok, :].astype(F32) + far_ref[...].astype(F32)
    normed, inverse = layer_norm(resid_ref[...])
    sums_ref[0:1, :] = jnp.sum(upstream * normed, axis=0, keepdims=True)
    sums_ref[1:2, :] = jnp.sum(upstream, axis=0, keepdims=True)
    sums_ref[2:, :] = jnp.zeros_like(sums_ref[2:, :])
    grad = up_ref[...].astype(F32) + norm_back(upstream, normed, inverse, gain_ref[1:2, :])
    grad_ref[...] = grad
    branch[...] = grad.astype(BF16)
    total = jnp.zeros(grad.shape, F32)
    for step, weight in enumerate(weight_refs):
        total += dot(branch[:, pl.ds(place(step, part, me_ref), part)], weight[...], 1, 1)
    grad_attn[...] = total.astype(BF16)
    for step, send in enumerate(send_refs):
        columns = pl.ds(place(step, part, me_ref), part)
        send[:, :part] = grad_attn[:, columns]
        send[:, part:] = branch[:, columns]


def attend_back_kernel(scale, count, *refs):
    qkv_ref, log_ref, bias_ref, seg_col_ref, seg_row_ref, act_ref, normed_ref, sums_ref, bucket_ref = refs[:9]
    attn_refs, grad_refs = refs[9:13], refs[13:17]
    pieces, offsets_ref, me_ref = refs[17 : 17 + count], refs[17 + count], refs[18 + count]
    last_ref, small_ref, own_ref, far_ref, send_ref = refs[19 + count : 24 + count]
    weight, grads, branch, grad_qkv, key_acc, value_acc, diagonal_acc, stacked, sems = refs[24 + count :]
    copies = load(pieces, offsets_ref, weight, sems)
    seq_len = qkv_ref.shape[0]
    columns = qkv_ref.shape[1] // 3
    heads, diagonals = diagonal_acc.shape[:2]
    tok = grad_refs[0].shape[0]
    for step, grad in enumerate(grad_refs):
        rows = pl.ds(place(step, tok, me_ref), tok)
        grads[rows, :] = grad[:, :columns]
        branch[rows, :] = grad[:, columns:]
    key_acc[...] = jnp.zeros_like(key_acc)
    value_acc[...] = jnp.zeros_like(value_acc)
    diagonal_acc[...] = jnp.zeros_like(diagonal_acc)
    for index in range(seq_len // BLOCK):
        rows = slice(index * BLOCK, (index + 1) * BLOCK)
        width = (index + 1) * BLOCK
        mask = mask_rows(index, seg_col_ref, seg_row_ref)
        for pair in range(columns // BLOCK):
            lanes = slice(pair * BLOCK, (pair + 1) * BLOCK)
            query = qkv_ref[rows, lanes] * scale
            keys = qkv_ref[:width, columns + pair * BLOCK : columns + (pair + 1) * BLOCK]
            values = qkv_ref[:width, 2 * columns + pair * BLOCK : 2 * columns + (pair + 1) * BLOCK]
            grad_rows = grads[rows, lanes]
            grad_query = jnp.zeros((BLOCK, BLOCK), F32)
            for side in range(2):
                head = 2 * pair + side
                query_one = query * half_mask(side)
                grad_one = grad_rows * half_mask(side)
                scores = score_rows(query_one, keys, bias_ref, head, index, mask)
                probs = jnp.exp(scores - log_ref[rows, head : head + 1])
                grad_probs = dot(grad_one, values, 1, 1)
                row_term = jnp.sum(probs * grad_probs, axis=1, keepdims=True)
                grad_scores = probs * (grad_probs - row_term)
                for block in range(index + 1):
                    diagonal_acc[head, index - block] += grad_scores[
                        :, block * BLOCK : (block + 1) * BLOCK
                    ]
                grad_raw = grad_scores.astype(BF16)
                grad_query += dot(grad_raw, keys * half_mask(side))
                key_acc[:width, lanes] += dot(grad_raw, query_one, 0, 0)
                value_acc[:width, lanes] += dot(probs.astype(BF16), grad_one, 0, 0)
            grad_qkv[rows, lanes] = (grad_query * scale).astype(BF16)
    grad_qkv[:, columns : 2 * columns] = key_acc[...].astype(BF16)
    grad_qkv[:, 2 * columns :] = value_acc[...].astype(BF16)

    finish(copies)
    gain_sum = jnp.zeros((1, act_ref.shape[1]), F32)
    shift_sum = jnp.zeros((1, act_ref.shape[1]), F32)
    for step in range(4):
        rows = pl.ds(place(step, tok, me_ref), tok)
        share_of = dot(grad_qkv[rows, :], weight[...], 1, 1)
        gain_sum += jnp.sum(share_of * normed_ref[rows, :].astype(F32), axis=0, keepdims=True)
        shift_sum += jnp.sum(share_of, axis=0, keepdims=True)
        if step == 0:
            own_ref[...] = share_of
        elif step == 2:
            far_ref[...] = share_of
        else:
            send_ref[(step // 2) * tok : (step // 2 + 1) * tok, :] = share_of.astype(BF16)

    parts, last_rows = last_ref.shape[:2]
    rows_here = act_ref.shape[1] // parts
    for start in range(0, act_ref.shape[1], 2 * BLOCK):
        block = dot(act_ref[:, start : start + 2 * BLOCK], grad_qkv[...], 0, 0).astype(BF16)
        for sub in range(2 * BLOCK // rows_here):
            part = start // rows_here + sub
            last_ref[part, :rows_here, : 3 * columns] = block[sub * rows_here : (sub + 1) * rows_here, :]
    for step, attn in enumerate(attn_refs):
        block = dot(attn[...], branch[...], 0, 0).astype(BF16)
        for sub in range(columns // rows_here):
            part = (me_ref[0] ^ step) * (columns // rows_here) + sub
            last_ref[part, :rows_here, 3 * columns :] = block[sub * rows_here : (sub + 1) * rows_here, :]

    row = lax.broadcasted_iota(jnp.int32, (BLOCK, BLOCK), 0)
    column = lax.broadcasted_iota(jnp.int32, (BLOCK, BLOCK), 1)
    flip = (row + column == BLOCK - 1).astype(F32)
    stacked[...] = jnp.zeros_like(stacked)
    for head in range(heads):
        for diagonal in range(diagonals):
            block = lax.dot_general(
                diagonal_acc[head, diagonal],
                flip,
                (((1,), (0,)), ((), ())),
                precision=lax.Precision.HIGHEST,
                preferred_element_type=F32,
            )
            wide = jnp.concatenate([block, jnp.zeros_like(block)], axis=1)
            rolled = pltpu.roll(wide, 0, 1, stride=1, stride_axis=0)
            at = slice(diagonal * BLOCK, (diagonal + 2) * BLOCK)
            stacked[head : head + 1, at] += jnp.sum(rolled, axis=0, keepdims=True)
    buckets = BLOCK // heads
    bucket = lax.broadcasted_iota(jnp.int32, (BLOCK, bucket_ref.shape[1]), 0) % buckets
    chosen = (bucket == bucket_ref[...]).astype(F32)
    by_head = lax.dot_general(
        stacked[...],
        chosen,
        (((1,), (1,)), ((), ())),
        precision=lax.Precision.HIGHEST,
        preferred_element_type=F32,
    )
    row = lax.broadcasted_iota(jnp.int32, by_head.shape, 0)
    column = lax.broadcasted_iota(jnp.int32, by_head.shape, 1)
    table = jnp.sum(jnp.where(column // buckets == row, by_head, 0.0), axis=0, keepdims=True)
    small = [gain_sum, sums_ref[0:1, :], shift_sum, sums_ref[1:2, :]]
    for at, value in enumerate(small):
        small_ref[at : at + 1, :] = value
    small_ref[4:5, :BLOCK] = table
    if last_rows > rows_here:
        last_ref[:, rows_here:, :] = jnp.zeros_like(last_ref[:, rows_here:, :])
        for part in range(parts):
            for at, value in enumerate(small):
                last_ref[part, rows_here : rows_here + 1, at * rows_here : (at + 1) * rows_here] = value[
                    :, part * rows_here : (part + 1) * rows_here
                ].astype(BF16)
            per = parts // 4
            turned = table if part % per == 0 else pltpu.roll(table, BLOCK - part % per * (BLOCK // per), 1)
            turned = jnp.where(me_ref[0] == part // per, turned, 0.0)
            last_ref[part, rows_here : rows_here + 1, 4 * rows_here : 4 * rows_here + BLOCK] = turned.astype(BF16)


def norm_back_kernel(own_ref, near_ref, far_ref, tokens_ref, resid_ref, gain_ref, grad_ref):
    tok = own_ref.shape[0]
    upstream = own_ref[...] + near_ref[:tok, :].astype(F32) + far_ref[...].astype(F32)
    normed, inverse = layer_norm(tokens_ref[...].astype(F32))
    grad_ref[...] = resid_ref[...] + norm_back(upstream, normed, inverse, gain_ref[0:1, :])


def wide_feed_kernel(*refs):
    in_refs, down_refs, me_ref, in_ref, down_ref = refs[:4], refs[4:8], refs[8], refs[9], refs[10]
    rows = down_refs[0].shape[0]
    for step in range(4):
        down_ref[pl.ds(place(step, rows, me_ref), rows), :] = down_refs[step][...].astype(F32)
        for start in range(0, in_refs[step].shape[1], rows):
            at = pl.multiple_of(4 * start + (me_ref[0] ^ step) * rows, rows)
            in_ref[:, pl.ds(at, rows)] = in_refs[step][:, start : start + rows].astype(F32)


def wide_last_kernel(part, *refs):
    last_refs, me_ref, qkv_ref, out_ref, small_ref = refs[:4], refs[4], refs[5], refs[6], refs[7]
    rows = qkv_ref.shape[0]
    small = jnp.zeros(small_ref.shape, F32)
    for step, last in enumerate(last_refs):
        for third in range(3):
            at = pl.multiple_of(4 * third * part + (me_ref[0] ^ step) * part, part)
            qkv_ref[:, pl.ds(at, part)] = last[:rows, third * part : (third + 1) * part].astype(F32)
        out_ref[:, pl.ds(place(step, part, me_ref), part)] = last[:rows, 3 * part :].astype(F32)
        small += last[rows:, :].astype(F32)
    small_ref[...] = small


def stacked_sp(pieces):
    me = lax.axis_index("sp")
    whole = jnp.zeros((len(pieces),) + pieces[0].shape, pieces[0].dtype)
    for step, piece in enumerate(pieces):
        whole = lax.dynamic_update_index_in_dim(whole, piece, me ^ step, 0)
    return whole


def on_device(
    inputs,
    qkv_weight,
    out_weight,
    in_weight,
    down_weight,
    norm_gain,
    norm_shift,
    bias_table,
    segment_ids,
    bucket_index,
    cotangent,
):
    dp_count, sp_count = lax.axis_size("dp"), lax.axis_size("sp")
    me_sp = lax.axis_index("sp")
    me = me_sp.astype(jnp.int32).reshape(1)
    tok, width = inputs.shape[1:]
    head_total, bucket_count = bias_table.shape
    heads = head_total // sp_count
    scale = (width // head_total) ** (-0.5)
    seq_len = segment_ids.shape[1]
    rows_here = qkv_weight.shape[0]
    ff = in_weight.shape[1]
    ff_rows = ff // dp_count // sp_count
    ff_part = ff // sp_count
    part = width // sp_count
    diagonals = seq_len // BLOCK
    aligned = ff_rows % BLOCK == 0 and rows_here % BLOCK == 0

    if aligned:
        qkv_part = share(
            [qkv_weight], me, [(0, 1, third * width, part, part, third * part) for third in range(3)], rows_here
        )
        plan = [(0, 1, 0, part, part, 0)]
        plan += [
            (1, 1, index * sp_count * ff_rows, ff_rows, ff_rows, part + index * ff_rows)
            for index in range(dp_count)
        ]
        both_part = share([out_weight, in_weight], me, plan, rows_here)
    else:

        def own_sp(stacked, axis):
            return lax.dynamic_index_in_dim(stacked, me_sp, axis, keepdims=False)

        qkv_part = own_sp(qkv_weight.reshape(rows_here, 3, sp_count, part), 2).reshape(rows_here, 3 * part)
        out_part = own_sp(out_weight.reshape(rows_here, sp_count, part), 1)
        in_part = own_sp(in_weight.reshape(rows_here, dp_count, sp_count, ff_rows), 2)
        both_part = jnp.concatenate([out_part, in_part.reshape(rows_here, ff_part)], axis=1)
    down_part = lax.dynamic_slice_in_dim(down_weight, me_sp * ff_rows, ff_rows, 0)
    at_rows = gather_offsets(rows_here, dp_count)
    at_ff = gather_offsets(ff_rows, dp_count)
    qkv_pieces = gather_dp(qkv_part, dp_count)
    both_pieces = gather_dp(both_part, dp_count)
    down_pieces = gather_dp(down_part, dp_count)
    count = len(qkv_pieces)
    sems = pltpu.SemaphoreType.DMA((count,))

    table_here = lax.dynamic_slice_in_dim(bias_table, me_sp * heads, heads, 0)
    reversed_buckets = jnp.pad(bucket_index[::-1], (1, BLOCK - 1))[None]
    padded_buckets = jnp.pad(bucket_index, (BLOCK - 1, 1), constant_values=-1)[None]
    (bias,) = call(
        bias_kernel, [shaped((heads, diagonals, BLOCK, BLOCK), F32)], [table_here, reversed_buckets]
    )
    seg_row = segment_ids
    seg_col = segment_ids.reshape(seq_len, 1)

    tokens = inputs[0]
    token_pieces = gather_sp(tokens)
    up_pieces = gather_sp(cotangent[0])
    act_one, normed_one = call(
        norm_kernel,
        [shaped((seq_len, width), BF16)] * 2,
        [*token_pieces, norm_gain, norm_shift],
        (),
        [me],
        (),
        (20 * seq_len * width, 6 * seq_len * width),
    )
    qkv, attn, logs = call(
        functools.partial(attend_kernel, scale, count),
        [shaped((seq_len, 3 * part), BF16), shaped((seq_len, part), BF16), shaped((seq_len, BLOCK), F32)],
        [act_one, bias, seg_col, seg_row],
        qkv_pieces,
        [at_rows],
        [pltpu.VMEM((width, 3 * part), BF16), sems],
        (2 * seq_len * width * 3 * part, 8 * seq_len * width),
    )
    attn_pieces = gather_sp(attn)
    if count == 1:
        out_columns = both_pieces[0][:, :part]
    else:

        def assemble(*refs):
            finish(load(refs[:count], refs[count], refs[count + 1], refs[count + 2], slice(0, part)))

        (out_columns,) = call(
            assemble, [shaped((width, part), BF16)], [], both_pieces, [at_rows], [sems], (0, 4 * width * part)
        )
    out_pieces = gather_sp(out_columns)
    resid, act_two = call(
        branch_kernel,
        [shaped((tok, width), F32), shaped((tok, width), BF16)],
        [*attn_pieces, *out_pieces, tokens, norm_gain, norm_shift],
        (),
        [me],
        [pltpu.VMEM((tok, width), BF16)],
        (2 * tok * width * width, 4 * width * width),
    )
    act_pieces = gather_sp(act_two)
    fed, slope, grad_down = call(
        functools.partial(feed_kernel, count, part),
        [shaped((seq_len, ff_part), BF16), shaped((seq_len, ff_part), F32), shaped((ff_part, width), BF16)],
        [*act_pieces, *up_pieces],
        both_pieces,
        [at_rows],
        [pltpu.VMEM((width, ff_part), BF16), pltpu.VMEM((seq_len, width), BF16), sems],
        (4 * seq_len * width * ff_part, 12 * seq_len * width),
    )

    share_shapes = [shaped((tok, width), F32), shaped((tok, width), F32), shaped((2 * tok, width), BF16)]
    grad_hidden, own_two, far_two, send_two = call(
        functools.partial(feed_back_kernel, count, part),
        [shaped((seq_len, ff_part), BF16)] + share_shapes,
        [slope, *up_pieces],
        [*down_pieces, *both_pieces],
        [at_ff, at_rows],
        [pltpu.VMEM((ff_part, width), BF16), pltpu.VMEM((width, ff_part), BF16), sems, sems],
        (4 * seq_len * width * ff_part, 12 * seq_len * width),
    )
    near_two, last_two = reduce_sp(far_two, send_two)
    grad_in, own_out, far_out, send_out = call(
        functools.partial(feed_rest_kernel, count),
        [shaped((width, ff_part), BF16)] + share_shapes,
        [fed, grad_hidden, *act_pieces],
        down_pieces,
        [at_ff],
        [pltpu.VMEM((seq_len, width), BF16), pltpu.VMEM((ff_part, width), BF16), sems],
        (4 * seq_len * width * ff_part, 12 * seq_len * width),
    )
    near_out, last_out = reduce_sp(far_out, send_out)
    output = (resid + own_out + near_out[:tok].astype(F32) + last_out.astype(F32)).astype(BF16)

    grad_resid, sums_two, *sends = call(
        branch_back_kernel,
        [shaped((tok, width), F32), shaped((8, width), F32)] + [shaped((tok, 2 * part), BF16)] * 4,
        [own_two, near_two, last_two, resid, cotangent[0], norm_gain, *out_pieces],
        (),
        [me],
        [pltpu.VMEM((tok, width), BF16), pltpu.VMEM((tok, width), BF16)],
        (2 * tok * width * width, 4 * width * width),
    )
    grad_pieces = [sends[0]] + [swap(sends[step], step) for step in (1, 2, 3)]
    last_rows = rows_here + SMALL_ROWS if aligned else rows_here
    last, small, own_one, far_one, send_one = call(
        functools.partial(attend_back_kernel, scale, count),
        [shaped((dp_count, last_rows, 4 * part), BF16), shaped((8, width), F32)] + share_shapes,
        [qkv, logs, bias, seg_col, seg_row, act_one, normed_one, sums_two, padded_buckets]
        + [*attn_pieces, *grad_pieces],
        qkv_pieces,
        [at_rows, me],
        [
            pltpu.VMEM((width, 3 * part), BF16),
            pltpu.VMEM((seq_len, part), BF16),
            pltpu.VMEM((seq_len, part), BF16),
            pltpu.VMEM((seq_len, 3 * part), BF16),
            pltpu.VMEM((seq_len, part), F32),
            pltpu.VMEM((seq_len, part), F32),
            pltpu.VMEM((heads, diagonals, BLOCK, BLOCK), F32),
            pltpu.VMEM((heads, seq_len + BLOCK), F32),
            sems,
        ],
        (4 * seq_len * width * 4 * part, 16 * seq_len * width),
    )
    near_one, last_one = reduce_sp(far_one, send_one)
    (grad_input,) = call(
        norm_back_kernel,
        [shaped((tok, width), F32)],
        [own_one, near_one, last_one, tokens, grad_resid, norm_gain],
        cost=(20 * tok * width, 20 * tok * width),
    )

    sum_down = scatter_dp(grad_down.reshape(dp_count, ff_rows, width), dp_count)
    sum_in = scatter_dp(grad_in.reshape(dp_count, rows_here, ff_part), dp_count)
    if not aligned:
        table = jnp.zeros((head_total * bucket_count,), F32)
        table = lax.dynamic_update_slice_in_dim(table, small[4, :BLOCK], me_sp * BLOCK, 0)
        packed = [small[at].reshape(dp_count, -1) for at in range(4)] + [table.reshape(dp_count, -1)]
        packed = jnp.concatenate(packed, axis=1).astype(BF16)
        packed = jnp.pad(packed, ((0, 0), (0, 4 * part - packed.shape[1])))
        packed = jnp.pad(packed[:, None], ((0, 0), (0, SMALL_ROWS - 1), (0, 0)))
        last = jnp.concatenate([last, packed], axis=1)
    sum_last = scatter_dp(last, dp_count)
    in_pieces, down_sums, last_pieces = gather_sp(sum_in), gather_sp(sum_down), gather_sp(sum_last)
    if aligned:
        out_in, out_down = call(
            wide_feed_kernel,
            [shaped((rows_here, ff), F32), shaped((sp_count * ff_rows, width), F32)],
            [*in_pieces, *down_sums],
            (),
            [me],
            (),
            (0, 6 * rows_here * ff),
        )
        out_qkv, out_out, small_sum = call(
            functools.partial(wide_last_kernel, part),
            [
                shaped((rows_here, 3 * width), F32),
                shaped((rows_here, width), F32),
                shaped((SMALL_ROWS, 4 * part), F32),
            ],
            last_pieces,
            (),
            [me],
            (),
            (0, 24 * rows_here * width),
        )
    else:
        out_down = stacked_sp(down_sums).astype(F32).reshape(sp_count * ff_rows, width)
        all_in = stacked_sp(in_pieces).astype(F32).reshape(sp_count, rows_here, dp_count, ff_rows)
        out_in = jnp.moveaxis(all_in, 0, 2).reshape(rows_here, ff)
        all_last = stacked_sp(last_pieces).astype(F32)
        all_qkv = all_last[:, :rows_here, : 3 * part].reshape(sp_count, rows_here, 3, part)
        out_qkv = jnp.moveaxis(all_qkv, 0, 2).reshape(rows_here, 3 * width)
        out_out = jnp.moveaxis(all_last[:, :rows_here, 3 * part :], 0, 1).reshape(rows_here, width)
        small_sum = jnp.sum(all_last[:, rows_here:], axis=0)
    piece = width // dp_count
    small_row = small_sum[0]
    gains = small_row[: 2 * piece].reshape(2, piece)
    shifts = small_row[2 * piece : 4 * piece].reshape(2, piece)
    tables = small_row[4 * piece : 4 * piece + head_total * bucket_count // dp_count]
    return (output[None], grad_input[None], out_qkv, out_out, out_in, out_down, gains, shifts, tables)


def solution(mesh):
    in_specs = (
        P("dp", "sp", None),
        P("dp", None),
        P("dp", None),
        P("dp", None),
        P("dp", None),
        P(),
        P(),
        P(),
        P("dp", None),
        P(),
        P("dp", "sp", None),
    )
    out_specs = (
        P("dp", "sp", None),
        P("dp", "sp", None),
        P("dp", None),
        P("dp", None),
        P("dp", None),
        P("dp", None),
        P(None, "dp"),
        P(None, "dp"),
        P("dp"),
    )
    return jax.shard_map(
        on_device, mesh=mesh, in_specs=in_specs, out_specs=out_specs, check_vma=False
    )
```

```python
import functools

import jax
import jax.numpy as jnp
from jax import lax
from jax.experimental import pallas as pl
from jax.experimental.pallas import tpu as pltpu
from jax.sharding import PartitionSpec as P

BLOCK = 128
SMALL_ROWS = 16
NEG = -1e30
BF16 = jnp.bfloat16
F32 = jnp.float32
VMEM_LIMIT = 24 * 1024 * 1024
ROOT = 0.7978845608028654
CUBE = 0.044715


def dot(left, right, left_dim=1, right_dim=0):
    return lax.dot_general(
        left, right, (((left_dim,), (right_dim,)), ((), ())), preferred_element_type=F32
    )


def exact_dot(left, right, left_dim=1, right_dim=0):
    return lax.dot_general(
        left,
        right,
        (((left_dim,), (right_dim,)), ((), ())),
        precision=lax.Precision.HIGHEST,
        preferred_element_type=F32,
    )


def layer_norm(values):
    average = jnp.mean(values, axis=-1, keepdims=True)
    centred = values - average
    inverse = lax.rsqrt(jnp.mean(centred * centred, axis=-1, keepdims=True) + 1e-05)
    return centred * inverse, inverse


def norm_back(upstream, normed, inverse, gain):
    scaled = upstream * gain
    centre_term = jnp.mean(scaled, axis=-1, keepdims=True)
    slope_term = jnp.mean(scaled * normed, axis=-1, keepdims=True)
    return inverse * (scaled - centre_term - normed * slope_term)


def shaped(shape, dtype):
    return jax.ShapeDtypeStruct(tuple(shape), dtype)


def call(kernel, outs, args=(), hbm_args=(), smem_args=(), scratch=(), hbm_outs=(), micros=1):
    specs = [pl.BlockSpec(memory_space=pltpu.VMEM)] * len(args)
    specs += [pl.BlockSpec(memory_space=pltpu.HBM)] * len(hbm_args)
    specs += [pl.BlockSpec(memory_space=pltpu.SMEM)] * len(smem_args)
    out_specs = [pl.BlockSpec(memory_space=pltpu.VMEM)] * len(outs)
    out_specs += [pl.BlockSpec(memory_space=pltpu.HBM)] * len(hbm_outs)
    return pl.pallas_call(
        kernel,
        out_shape=(*outs, *hbm_outs),
        in_specs=specs,
        out_specs=tuple(out_specs),
        scratch_shapes=list(scratch),
        compiler_params=pltpu.CompilerParams(vmem_limit_bytes=VMEM_LIMIT),
        cost_estimate=pl.CostEstimate(flops=0, bytes_accessed=int(micros * 3.3e6), transcendentals=0),
    )(*args, *hbm_args, *smem_args)


def rank_at(position, count):
    position = lax.rem(position + 2 * count, count)
    return jnp.where(position < count // 2, 2 * position, 2 * (count - 1 - position) + 1)


def position_of(rank, count):
    return jnp.where(lax.rem(rank, 2) == 0, lax.div(rank, 2), count - 1 - lax.div(rank, 2))


def ring_pairs(count):
    order = list(range(0, count, 2)) + list(range(count - 1, 0, -2))
    forward = [(order[i], order[(i + 1) % count]) for i in range(count)]
    return forward, [(b, a) for a, b in forward]


def half_rows(rows):
    return rows // 2 // 16 * 16


def hold(value, *others):
    return lax.optimization_barrier((value, others))[0] if others else value


def halves(up, down):
    rows, columns = up.shape
    half = half_rows(rows)

    def kernel(up_ref, down_ref, upper_ref, lower_ref, sems):
        copies = [
            pltpu.make_async_copy(up_ref.at[:half, :], upper_ref, sems.at[0]),
            pltpu.make_async_copy(down_ref.at[half:, :], lower_ref, sems.at[1]),
        ]
        finish(start_all(copies))

    outs = [shaped((half, columns), up.dtype), shaped((rows - half, columns), up.dtype)]
    return call(kernel, outs, [], [up, down], scratch=[dma(2)])


class GatherRing:
    def __init__(self, shard, count):
        self.shard, self.count, self.at = shard, count, 0
        self.up = self.down = shard
        self.pieces, self.held = [shard], (shard, shard)

    def step(self, *others):
        self.at += 1
        if self.count != 8:
            if self.at == 1:
                self.up = self.down = lax.all_gather(self.shard, "dp", axis=0, tiled=True)
                self.pieces = [self.up]
            return
        forward, backward = ring_pairs(self.count)
        up, down = self.up, self.down
        if self.at == self.count // 2:
            up, down = halves(up, down)
        self.held = up, down
        up, down, *_ = lax.optimization_barrier((up, down, *others))
        self.up = lax.ppermute(up, "dp", forward)
        self.down = lax.ppermute(down, "dp", backward)
        self.pieces += [self.up, self.down]


def ring_add_kernel(count, step, *refs):
    parts, up_ref, down_ref, me_ref = refs[:4]
    *outs, mine, up, down, sems = refs[4:]
    rows = parts.shape[1]
    half = half_rows(rows)
    at = position_of(me_ref[1], count)
    up_rows, down_rows = (slice(0, half), slice(half, rows)) if step == 1 else (slice(0, rows),) * 2
    copies = [
        pltpu.make_async_copy(up_ref, up.at[up_rows, :], sems.at[0]),
        pltpu.make_async_copy(down_ref, down.at[down_rows, :], sems.at[1]),
        pltpu.make_async_copy(parts.at[rank_at(at + count // 2 - step, count)], mine.at[0], sems.at[2]),
    ]
    if step < count // 2:
        copies.append(
            pltpu.make_async_copy(parts.at[rank_at(at - count // 2 + step, count)], mine.at[1], sems.at[3])
        )
    finish(start_all(copies))
    if step == count // 2:
        total = mine[0].astype(F32) + up[...].astype(F32) + down[...].astype(F32)
        outs[0][...] = total.astype(BF16)
        return
    for target, own, arrived, where in zip(outs, (mine.at[0], mine.at[1]), (up, down), (up_rows, down_rows)):
        if step == 1:
            target[...] = own[...]
        target[where, :] = (own[where, :].astype(F32) + arrived[where, :].astype(F32)).astype(BF16)


class ScatterRing:
    def __init__(self, parts, me, count):
        self.parts, self.me, self.count, self.at = parts, me, count, 0
        self.total = None

    def step(self, *others):
        self.at += 1
        if self.count != 8:
            return
        forward, backward = ring_pairs(self.count)
        rows = self.parts.shape[1]
        half = half_rows(rows)
        if self.at == 1:
            me = position_of(lax.axis_index("dp"), self.count)
            far = rank_at(me + self.count // 2, self.count)
            far = lax.dynamic_index_in_dim(self.parts, far, 0, keepdims=False)
            up, down = far[:half], far[half:]
        else:
            up, down = self.add(self.at - 1, 2, *others)
        self.added = up, down
        self.up = lax.ppermute(up, "dp", forward)
        self.down = lax.ppermute(down, "dp", backward)

    def sent(self):
        return (self.up, self.down) if self.count == 8 else ()

    def sums(self):
        return self.added if self.count == 8 else ()

    def add(self, step, outs, *others):
        rows, columns = self.parts.shape[1:]
        up = hold(self.up, *others)
        return call(
            functools.partial(ring_add_kernel, self.count, step),
            [shaped((rows, columns), BF16)] * outs,
            [],
            [self.parts, up, self.down],
            [self.me],
            [pltpu.VMEM((2, rows, columns), BF16)] + [pltpu.VMEM((rows, columns), BF16)] * 2 + [dma(4)],
        )

    def finish(self, *others):
        if self.count != 8:
            return lax.psum_scatter(self.parts, "dp", scatter_dimension=0)
        return self.add(self.count // 2, 1, *others)[0]


def swap(values, bit):
    count = lax.axis_size("sp")
    return lax.ppermute(values, "sp", [(i, i ^ bit) for i in range(count)])


def gather_sp(piece):
    far = swap(piece, 2)
    near = swap(piece, 1)
    return [piece, near, far, swap(far, 1)]


def exchange_sp(sends):
    return [swap(send, step) for step, send in enumerate(sends, 1)]


def place(step, size, me_ref):
    return pl.multiple_of((me_ref[0] ^ step) * size, size)


def in_hbm(pieces):
    return [pltpu.with_memory_space_constraint(piece, pltpu.HBM) for piece in pieces]


def start_all(copies):
    for copy in copies:
        copy.start()
    return copies


def finish(copies):
    for copy in copies:
        copy.wait()


def load(pieces, me_ref, count, target, sems, lanes=slice(None)):
    if len(pieces) == 1:
        starts = [0]
    else:
        at = position_of(me_ref[1], count)
        rows = pieces[0].shape[0]
        starts = [rank_at(at + step, count) * rows for step in (0, -1, 1, -2, 2, -3, 3, 4)]
        starts.append(starts[-1] + half_rows(rows))
    copies = []
    for at, (start, piece) in enumerate(zip(starts, pieces)):
        rows = pl.ds(pl.multiple_of(start, 16), piece.shape[0])
        copies.append(pltpu.make_async_copy(piece.at[:, lanes], target.at[rows, :], sems.at[at]))
    return start_all(copies)


def load_rows(pieces, target, sems, me_ref=None, rows=slice(None), lanes=slice(None)):
    copies = []
    for step, piece in enumerate(pieces):
        block = piece.at[rows, lanes]
        size = block.shape[0]
        start = step * size if me_ref is None else place(step, size, me_ref)
        copies.append(pltpu.make_async_copy(block, target.at[pl.ds(start, size), :], sems.at[step]))
    return start_all(copies)


def dma(count):
    return pltpu.SemaphoreType.DMA((count,))


def share(sources, me, plan, rows):
    columns = sum(size for _, _, size, _ in plan)

    def kernel(*refs):
        *inputs, me_ref, target, sems = refs
        copies = []
        for at, (source, start, size, to) in enumerate(plan):
            if start is None:
                block = inputs[source].at[pl.ds(place(0, rows, me_ref), rows), :]
            else:
                block = inputs[source].at[:, pl.ds(start + place(0, size, me_ref), size)]
            copies.append(pltpu.make_async_copy(block, target.at[:, to : to + size], sems.at[at]))
        finish(start_all(copies))

    return call(
        kernel,
        [pltpu.VMEM((rows, columns), BF16)],
        [],
        [pltpu.with_memory_space_constraint(source, pltpu.HBM) for source in sources],
        [me],
        [dma(len(plan))],
    )[0]


def bias_kernel(table_ref, bucket_ref, seg_ref, me_ref, bias_ref, mask_ref):
    heads, diagonals = bias_ref.shape[:2]
    wide = bucket_ref.shape[1]
    bucket = lax.broadcasted_iota(jnp.int32, (table_ref.shape[1], wide), 0)
    chosen = (bucket == bucket_ref[...]).astype(F32)
    rows = exact_dot(table_ref[...], chosen)
    row = lax.broadcasted_iota(jnp.int32, rows.shape, 0)
    for head in range(heads):
        mine = jnp.sum(jnp.where(row == me_ref[0] * heads + head, rows, 0.0), axis=0, keepdims=True)
        for diagonal in range(diagonals):
            part = mine[:, diagonal * BLOCK : (diagonal + 2) * BLOCK]
            spread = jnp.broadcast_to(part, (BLOCK, 2 * BLOCK))
            rolled = pltpu.roll(spread, BLOCK, 1, stride=1, stride_axis=0)
            bias_ref[head, diagonal] = rolled[:, :BLOCK]
    segments = seg_ref[...].astype(F32)
    key = lax.broadcasted_iota(jnp.int32, (BLOCK, BLOCK), 0)
    query = lax.broadcasted_iota(jnp.int32, (BLOCK, BLOCK), 1)
    for block in range(diagonals):
        rows = slice(block * BLOCK, (block + 1) * BLOCK)
        keys = jnp.broadcast_to(segments[:, rows], (BLOCK, BLOCK)).T
        for index in range(block, diagonals):
            same = keys == segments[:, index * BLOCK : (index + 1) * BLOCK]
            if index == block:
                same = same & (query >= key)
            mask_ref[index, rows, :] = jnp.where(same, 0.0, NEG).astype(F32)


def norm_kernel(*refs):
    pieces, (gain_ref, shift_ref), me_ref = refs[2:6], refs[:2], refs[6]
    act_ref, normed_ref, up_ref, tokens, sems, up_sems = refs[7:]
    tok = up_ref.shape[0] // 4
    copies = load_rows(pieces, tokens, sems, me_ref, slice(0, tok))
    up_copies = load_rows(pieces, up_ref, up_sems, None, slice(tok, 2 * tok))
    finish(copies)
    for start in range(0, tokens.shape[0], BLOCK):
        rows = slice(start, start + BLOCK)
        normed, _ = layer_norm(tokens[rows, :].astype(F32))
        act_ref[rows, :] = (normed * gain_ref[0:1, :] + shift_ref[0:1, :]).astype(BF16)
        normed_ref[rows, :] = normed.astype(BF16)
    finish(up_copies)


def split_heads(rows):
    lane = lax.broadcasted_iota(jnp.int32, (1, BLOCK), 1)
    low = (lane < BLOCK // 2).astype(F32).astype(BF16)
    return jnp.concatenate([rows * low, rows * (1 - low)], axis=0)


def join_heads(both):
    half = BLOCK // 2
    return jnp.concatenate([both[:half, :BLOCK], both[half:, BLOCK:]], axis=0).T


def score_block(raw, bias_ref, mask_ref, pair, index, block):
    rows = slice(block * BLOCK, (block + 1) * BLOCK)
    mask = mask_ref[index, rows, :]
    return jnp.concatenate(
        [
            raw[rows, side * BLOCK : (side + 1) * BLOCK] + bias_ref[2 * pair + side, index - block] + mask
            for side in range(2)
        ],
        axis=1,
    )


def attend_kernel(scale, parts, count, *refs):
    act_ref, bias_ref, mask_ref = refs[:3]
    pieces, me_ref = refs[3 : 3 + count], refs[3 + count]
    qkv_ref, attn_ref, log_ref, weight, sems = refs[4 + count :]
    columns = attn_ref.shape[1]
    copies = load(pieces, me_ref, parts, weight, sems, slice(0, 3 * columns))
    finish(copies)
    for start in range(0, 3 * columns, columns):
        lanes = slice(start, start + columns)
        qkv_ref[:, lanes] = dot(act_ref[...], weight[:, lanes]).astype(BF16)
    for index in range(qkv_ref.shape[0] // BLOCK):
        rows = slice(index * BLOCK, (index + 1) * BLOCK)
        width = (index + 1) * BLOCK
        for pair in range(columns // BLOCK):
            lanes = slice(pair * BLOCK, (pair + 1) * BLOCK)
            queries = split_heads(qkv_ref[rows, lanes] * scale)
            keys = qkv_ref[:width, columns + pair * BLOCK : columns + (pair + 1) * BLOCK]
            values = qkv_ref[:width, 2 * columns + pair * BLOCK : 2 * columns + (pair + 1) * BLOCK]
            raw = dot(keys, queries, 1, 1)
            scores = [score_block(raw, bias_ref, mask_ref, pair, index, block) for block in range(index + 1)]
            largest = functools.reduce(
                jnp.maximum, [jnp.max(score, axis=0, keepdims=True) for score in scores]
            )
            weights = [jnp.exp(score - largest) for score in scores]
            total = functools.reduce(jnp.add, [jnp.sum(one, axis=0, keepdims=True) for one in weights])
            mixed = dot(values, jnp.concatenate([one.astype(BF16) for one in weights], axis=0), 0, 0)
            attn_ref[rows, lanes] = join_heads(mixed / total).astype(BF16)
            at = index * (columns // BLOCK) + pair
            log_ref[at : at + 1, :] = largest + jnp.log(total)


def branch_kernel(*refs):
    tokens_ref, gain_ref, shift_ref, attn_refs, weight_refs, me_ref = (*refs[:3], refs[3:7], refs[7:11], refs[11])
    resid_ref, act_ref, weight, own, sems, weight_sems = refs[12:]
    tok = tokens_ref.shape[0]
    part = weight_refs[0].shape[1]
    copies = []
    for step in range(4):
        columns = pl.ds(place(step, part, me_ref), part)
        rows = pl.ds(place(0, tok, me_ref), tok)
        copies.append(pltpu.make_async_copy(attn_refs[step].at[rows, :], own.at[:, columns], sems.at[step]))
        copies.append(pltpu.make_async_copy(weight_refs[step], weight.at[:, columns], weight_sems.at[step]))
    finish(start_all(copies))
    resid = tokens_ref[...].astype(F32) + dot(own[...], weight[...])
    resid_ref[...] = resid
    normed, _ = layer_norm(resid)
    act_ref[...] = (normed * gain_ref[1:2, :] + shift_ref[1:2, :]).astype(BF16)


def outer(left, right, grad_ref):
    parts, rows_here, _ = grad_ref.shape
    for start in range(0, parts * rows_here, 2 * BLOCK):
        block = dot(left[:, start : start + 2 * BLOCK], right[...], 0, 0).astype(BF16)
        for sub in range(2 * BLOCK // rows_here):
            grad_ref[start // rows_here + sub] = block[sub * rows_here : (sub + 1) * rows_here]


def store_shares(total, own_ref, send_refs, columns):
    tok = own_ref.shape[0]
    own_ref[:, columns] = total[:tok]
    for step, send in enumerate(send_refs, 1):
        send[:, columns] = total[step * tok : (step + 1) * tok].astype(BF16)


def feed_kernel(parts, count, *refs):
    up_from, act_refs, pieces, me_ref = refs[0], refs[1:5], refs[5 : 5 + count], refs[5 + count]
    fed_ref, grad_ref, own_ref, *send_refs = refs[6 + count : 12 + count]
    act, up_ref, weight, down, slope, hidden, act_sems, up_sems, sems, down_sems = refs[12 + count :]
    width = weight.shape[1]
    copies = load(pieces, me_ref, parts, weight, sems, slice(0, width)) + load_rows(act_refs, act, act_sems)
    late = load(pieces, me_ref, parts, down, down_sems, slice(width, None))
    late += start_all([pltpu.make_async_copy(up_from, up_ref, up_sems.at[0])])
    finish(copies)
    for start in range(0, width, 2 * BLOCK):
        columns = slice(start, start + 2 * BLOCK)
        units = dot(act[...], weight[:, columns])
        square = units * units
        bend = jnp.tanh(ROOT * units * (1.0 + CUBE * square))
        fed_ref[:, columns] = (0.5 * units * (1.0 + bend)).astype(BF16)
        slope[:, columns] = 0.5 * (1.0 + bend) + 0.5 * units * (1.0 - bend * bend) * ROOT * (
            1.0 + 3.0 * CUBE * square
        )
    finish(late)
    for start in range(0, width, 2 * BLOCK):
        rows = slice(start, start + 2 * BLOCK)
        hidden[:, rows] = (dot(up_ref[...], down[rows, :], 1, 1) * slope[:, rows]).astype(BF16)
    for start in range(0, weight.shape[0], 2 * BLOCK):
        rows = slice(start, start + 2 * BLOCK)
        store_shares(dot(hidden[...], weight[rows, :], 1, 1), own_ref, send_refs, rows)
    rows_here = grad_ref.shape[1]
    for at, (left, right) in enumerate([(act, hidden), (fed_ref, up_ref)]):
        lanes = slice(at * width, (at + 1) * width)
        for start in range(0, parts * rows_here, 2 * BLOCK):
            block = dot(left[:, start : start + 2 * BLOCK], right[...], 0, 0).astype(BF16)
            for sub in range(2 * BLOCK // rows_here):
                grad_ref[start // rows_here + sub, :, lanes] = block[sub * rows_here : (sub + 1) * rows_here]


def feed_out_kernel(parts, count, *refs):
    fed_ref, pieces, me_ref = refs[0], refs[1 : 1 + count], refs[1 + count]
    own_ref, *send_refs, down, sems = refs[2 + count :]
    width = down.shape[1]
    finish(load(pieces, me_ref, parts, down, sems, slice(width, None)))
    for start in range(0, width, 2 * BLOCK):
        columns = slice(start, start + 2 * BLOCK)
        store_shares(dot(fed_ref[...], down[:, columns]), own_ref, send_refs, columns)


def out_kernel(own_ref, resid_ref, *refs):
    sent, out_ref, rest, sems = refs[:3], refs[3], refs[4], refs[5]
    finish(load_rows(sent, rest, sems))
    tok = own_ref.shape[0]
    total = resid_ref[...] + own_ref[...]
    for step in range(3):
        total += rest[step * tok : (step + 1) * tok, :].astype(F32)
    out_ref[...] = total.astype(BF16)


def branch_back_kernel(*refs):
    own_ref, resid_ref, up_ref, gain_ref, sent, weight_refs, me_ref = (*refs[:4], refs[4:7], refs[7:11], refs[11])
    grad_ref, sums_ref, *send_refs, branch, grad_attn, rest, weight, sems, weight_sems = refs[12:]
    tok = up_ref.shape[0]
    part = send_refs[0].shape[1] // 2
    copies = load_rows(sent, rest, sems)
    late = []
    for step in range(4):
        columns = pl.ds(place(step, part, me_ref), part)
        late.append(pltpu.make_async_copy(weight_refs[step], weight.at[:, columns], weight_sems.at[step]))
    start_all(late)
    normed, inverse = layer_norm(resid_ref[...])
    finish(copies)
    upstream = own_ref[...]
    for step in range(3):
        upstream += rest[step * tok : (step + 1) * tok, :].astype(F32)
    sums_ref[0:1, :] = jnp.sum(upstream * normed, axis=0, keepdims=True)
    sums_ref[1:2, :] = jnp.sum(upstream, axis=0, keepdims=True)
    sums_ref[2:, :] = jnp.zeros_like(sums_ref[2:, :])
    grad = up_ref[...].astype(F32) + norm_back(upstream, normed, inverse, gain_ref[1:2, :])
    grad_ref[...] = grad
    branch[...] = grad.astype(BF16)
    finish(late)
    grad_attn[...] = dot(branch[...], weight[...], 1, 1).astype(BF16)
    for step, send in enumerate(send_refs):
        columns = pl.ds(place(step, part, me_ref), part)
        send[:, :part] = grad_attn[:, columns]
        send[:, part:] = branch[:, columns]


def attend_back_kernel(scale, dp_count, count, *refs):
    qkv_ref, log_ref, bias_ref, mask_ref, act_ref, normed_ref, sums_ref, bucket_ref = refs[:8]
    attn_refs, grad_refs, pieces, me_ref = refs[8:12], refs[12:16], refs[16 : 16 + count], refs[16 + count]
    last_ref, small_ref, own_ref, *send_refs = refs[17 + count : 23 + count]
    grads, branch, attn, grad_qkv, key_acc, value_acc, diagonal_acc, stacked, shares, weight_ref = refs[
        23 + count : 33 + count
    ]
    grad_sems, branch_sems, attn_sems, sems = refs[33 + count :]
    seq_len = qkv_ref.shape[0]
    columns = qkv_ref.shape[1] // 3
    heads, diagonals = bias_ref.shape[:2]
    tok = own_ref.shape[0]
    copies = load_rows(grad_refs, grads, grad_sems, me_ref, lanes=slice(0, columns))
    late = load_rows(grad_refs, branch, branch_sems, me_ref, lanes=slice(columns, 2 * columns))
    late += load_rows(attn_refs, attn, attn_sems)
    late += load(pieces, me_ref, dp_count, weight_ref, sems, slice(0, 3 * columns))
    key_acc[...] = jnp.zeros_like(key_acc)
    value_acc[...] = jnp.zeros_like(value_acc)
    diagonal_acc[...] = jnp.zeros_like(diagonal_acc)
    finish(copies)
    for pair in range(columns // BLOCK):
        lanes = slice(pair * BLOCK, (pair + 1) * BLOCK)
        all_keys = qkv_ref[:, columns + pair * BLOCK : columns + (pair + 1) * BLOCK]
        for index in range(seq_len // BLOCK):
            rows = slice(index * BLOCK, (index + 1) * BLOCK)
            width = (index + 1) * BLOCK
            queries = split_heads(qkv_ref[rows, lanes] * scale)
            grad_rows = split_heads(grads[rows, lanes])
            keys = all_keys[:width]
            values = qkv_ref[:width, 2 * columns + pair * BLOCK : 2 * columns + (pair + 1) * BLOCK]
            at = index * (columns // BLOCK) + pair
            logs = log_ref[at : at + 1, :]
            raw = dot(keys, queries, 1, 1)
            grad_probs = dot(values, grad_rows, 1, 1)
            probs = [
                jnp.exp(score_block(raw, bias_ref, mask_ref, pair, index, block) - logs)
                for block in range(index + 1)
            ]
            products = [
                one * grad_probs[block * BLOCK : (block + 1) * BLOCK] for block, one in enumerate(probs)
            ]
            row_term = functools.reduce(jnp.add, [jnp.sum(one, axis=0, keepdims=True) for one in products])
            grad_scores = [product - one * row_term for product, one in zip(products, probs)]
            for block, one in enumerate(grad_scores):
                diagonal_acc[pair, index - block] += one
            grad_raw = jnp.concatenate([one.astype(BF16) for one in grad_scores], axis=0)
            probs_all = jnp.concatenate([one.astype(BF16) for one in probs], axis=0)
            grad_qkv[rows, lanes] = (join_heads(dot(keys, grad_raw, 0, 0)) * scale).astype(BF16)
            key_acc[:width, lanes] += dot(grad_raw, queries)
            value_acc[:width, lanes] += dot(probs_all, grad_rows)
    grad_qkv[:, columns : 2 * columns] = key_acc[...].astype(BF16)
    grad_qkv[:, 2 * columns :] = value_acc[...].astype(BF16)

    parts, last_rows = last_ref.shape[:2]
    width = act_ref.shape[1]
    rows_here = width // parts
    for start in range(0, width, 2 * BLOCK):
        block = dot(act_ref[:, start : start + 2 * BLOCK], grad_qkv[...], 0, 0).astype(BF16)
        for sub in range(2 * BLOCK // rows_here):
            last_ref[start // rows_here + sub, :rows_here, : 3 * columns] = block[
                sub * rows_here : (sub + 1) * rows_here
            ]
    finish(late)
    for step in range(4):
        block = dot(attn[step * seq_len : (step + 1) * seq_len, :], branch[...], 0, 0).astype(BF16)
        for sub in range(columns // rows_here):
            part = (me_ref[0] ^ step) * (columns // rows_here) + sub
            last_ref[part, :rows_here, 3 * columns :] = block[sub * rows_here : (sub + 1) * rows_here]

    for start in range(0, width, 2 * BLOCK):
        lanes = slice(start, start + 2 * BLOCK)
        share_of = dot(grad_qkv[...], weight_ref[lanes, :], 1, 1)
        small_ref[0:1, lanes] = jnp.sum(share_of * normed_ref[:, lanes].astype(F32), axis=0, keepdims=True)
        small_ref[2:3, lanes] = jnp.sum(share_of, axis=0, keepdims=True)
        shares[:, lanes] = share_of
    for step, target in enumerate([own_ref, *send_refs]):
        rows = pl.ds(place(step, tok, me_ref), tok)
        target[...] = shares[rows, :].astype(target.dtype)
    small_ref[1:2, :] = sums_ref[0:1, :]
    small_ref[3:4, :] = sums_ref[1:2, :]

    row = lax.broadcasted_iota(jnp.int32, (BLOCK, BLOCK), 0)
    column = lax.broadcasted_iota(jnp.int32, (BLOCK, BLOCK), 1)
    flip = (row + column == BLOCK - 1).astype(F32)
    stacked[...] = jnp.zeros_like(stacked)
    for pair in range(heads // 2):
        for diagonal in range(diagonals):
            both = exact_dot(flip, diagonal_acc[pair, diagonal])
            at = slice(diagonal * BLOCK, (diagonal + 2) * BLOCK)
            for side in range(2):
                block = both[:, side * BLOCK : (side + 1) * BLOCK]
                wide = jnp.concatenate([block, jnp.zeros_like(block)], axis=1)
                rolled = pltpu.roll(wide, 1, 1, stride=1, stride_axis=0)
                head = 2 * pair + side
                stacked[head : head + 1, at] += jnp.sum(rolled, axis=0, keepdims=True)
    buckets = BLOCK // heads
    bucket = lax.rem(lax.broadcasted_iota(jnp.int32, (BLOCK, bucket_ref.shape[1]), 0), buckets)
    chosen = (bucket == bucket_ref[...]).astype(F32)
    by_head = exact_dot(stacked[...], chosen, 1, 1)
    row = lax.broadcasted_iota(jnp.int32, by_head.shape, 0)
    column = lax.broadcasted_iota(jnp.int32, by_head.shape, 1)
    table = jnp.sum(jnp.where(lax.div(column, buckets) == row, by_head, 0.0), axis=0, keepdims=True)
    small_ref[4:5, :BLOCK] = table
    if last_rows > rows_here:
        last_ref[:, rows_here:, :] = jnp.zeros_like(last_ref[:, rows_here:, :])
        per = parts // 4
        for part in range(parts):
            for at in range(4):
                last_ref[part, rows_here : rows_here + 1, at * rows_here : (at + 1) * rows_here] = small_ref[
                    at : at + 1, part * rows_here : (part + 1) * rows_here
                ].astype(BF16)
            turned = table if part % per == 0 else pltpu.roll(table, BLOCK - part % per * (BLOCK // per), 1)
            turned = jnp.where(me_ref[0] == part // per, turned, 0.0)
            last_ref[part, rows_here : rows_here + 1, 4 * rows_here : 4 * rows_here + BLOCK] = turned.astype(BF16)


def norm_back_kernel(own_ref, tokens_ref, resid_ref, gain_ref, *refs):
    sent, grad_ref, rest, sems = refs[:3], refs[3], refs[4], refs[5]
    copies = load_rows(sent, rest, sems)
    tok = own_ref.shape[0]
    normed, inverse = layer_norm(tokens_ref[...].astype(F32))
    finish(copies)
    upstream = own_ref[...]
    for step in range(3):
        upstream += rest[step * tok : (step + 1) * tok, :].astype(F32)
    grad_ref[...] = resid_ref[...] + norm_back(upstream, normed, inverse, gain_ref[0:1, :])


def wide_feed_kernel(*refs):
    pieces, me_ref, in_ref, down_ref, both, sems = refs[:4], refs[4], refs[5], refs[6], refs[7], refs[8]
    finish(load_rows(pieces, both, sems))
    rows = in_ref.shape[0]
    width = down_ref.shape[1]
    for step in range(4):
        mine = slice(step * rows, (step + 1) * rows)
        down_ref[pl.ds(place(step, rows, me_ref), rows), :] = both[mine, width:].astype(F32)
        for start in range(0, width, rows):
            at = pl.multiple_of(4 * start + (me_ref[0] ^ step) * rows, rows)
            in_ref[:, pl.ds(at, rows)] = both[mine, start : start + rows].astype(F32)


def wide_last_kernel(*refs):
    pieces, me_ref = refs[:4], refs[4]
    qkv_ref, out_ref, gain_ref, shift_ref, table_ref, last, sems = refs[5:]
    finish(load_rows(pieces, last, sems))
    rows, width = out_ref.shape
    part = width // 4
    whole = rows + SMALL_ROWS
    small = jnp.zeros((1, width), F32)
    for step in range(4):
        start = step * whole
        mine = slice(start, start + rows)
        for third in range(3):
            at = pl.multiple_of(third * width + (me_ref[0] ^ step) * part, part)
            qkv_ref[:, pl.ds(at, part)] = last[mine, third * part : (third + 1) * part].astype(F32)
        out_ref[:, pl.ds(place(step, part, me_ref), part)] = last[mine, 3 * part :].astype(F32)
        small += last[start + rows : start + whole, :].astype(F32)[0:1]
    for at in range(2):
        gain_ref[at : at + 1, :] = small[:, at * rows : (at + 1) * rows]
        shift_ref[at : at + 1, :] = small[:, (2 + at) * rows : (3 + at) * rows]
    table_ref[...] = small[:, 4 * rows : 4 * rows + table_ref.shape[1]]


def stacked_sp(pieces):
    me = lax.axis_index("sp")
    whole = jnp.zeros((len(pieces),) + pieces[0].shape, pieces[0].dtype)
    for step, piece in enumerate(pieces):
        whole = lax.dynamic_update_index_in_dim(whole, piece, me ^ step, 0)
    return whole


def on_device(
    inputs,
    qkv_weight,
    out_weight,
    in_weight,
    down_weight,
    norm_gain,
    norm_shift,
    bias_table,
    segment_ids,
    bucket_index,
    cotangent,
):
    dp_count, sp_count = lax.axis_size("dp"), lax.axis_size("sp")
    me_sp = lax.axis_index("sp")
    me = jnp.stack([me_sp, lax.axis_index("dp")]).astype(jnp.int32)
    tok, width = inputs.shape[1:]
    head_total, bucket_count = bias_table.shape
    heads = head_total // sp_count
    scale = (width // head_total) ** (-0.5)
    seq_len = segment_ids.shape[1]
    rows_here = qkv_weight.shape[0]
    ff = in_weight.shape[1]
    ff_rows = ff // dp_count // sp_count
    ff_part = ff // sp_count
    part = width // sp_count
    diagonals = seq_len // BLOCK
    aligned = ff_rows % BLOCK == 0 and rows_here % BLOCK == 0

    if aligned:
        plan = [(0, third * width, part, third * part) for third in range(3)] + [(1, 0, part, 3 * part)]
        first_part = share([qkv_weight, out_weight], me, plan, rows_here)
        step = sp_count * ff_rows
        plan = [(0, index * step, ff_rows, index * ff_rows) for index in range(dp_count)]
        plan.append((1, None, width, ff_part))
        rest_part = share([hold(in_weight, first_part), down_weight], me, plan, rows_here)
    else:

        def own_sp(stacked, axis):
            return lax.dynamic_index_in_dim(stacked, me_sp, axis, keepdims=False)

        first_part = own_sp(qkv_weight.reshape(rows_here, 3, sp_count, part), 2).reshape(rows_here, 3 * part)
        out_part = own_sp(out_weight.reshape(rows_here, sp_count, part), 1)
        first_part = jnp.concatenate([first_part, out_part], axis=1)
        in_part = own_sp(in_weight.reshape(rows_here, dp_count, sp_count, ff_rows), 2)
        in_part = in_part.reshape(rows_here, ff_part)
        down_part = lax.dynamic_slice_in_dim(down_weight, me_sp * ff_rows, ff_rows, 0)
        rest_part = jnp.concatenate([in_part, down_part], axis=1)
    first_ring = GatherRing(first_part, dp_count)
    rest_ring = GatherRing(rest_part, dp_count)

    tokens = inputs[0]
    first_ring.step()

    buckets = jnp.pad(bucket_index, (BLOCK, 0), constant_values=-1)[None]
    bias, mask = call(
        bias_kernel,
        [shaped((heads, diagonals, BLOCK, BLOCK), F32), shaped((diagonals, seq_len, BLOCK), F32)],
        [bias_table, hold(buckets, first_part), segment_ids],
        (),
        [me],
        micros=1.2,
    )
    both = jnp.concatenate([hold(tokens, bias), cotangent[0]], axis=0)
    token_far, token_near = swap(both, 2), swap(both, 1)
    first_ring.step(bias, rest_part)
    token_last = swap(token_far, 1)
    first_ring.step(token_far)
    act_one, normed_one, up_all = call(
        norm_kernel,
        [shaped((seq_len, width), BF16)] * 3,
        [hold(norm_gain, *first_ring.held), norm_shift],
        [both, token_near, token_far, token_last],
        [me],
        [pltpu.VMEM((seq_len, width), BF16), dma(4), dma(4)],
        micros=2.4,
    )
    first_ring.step()
    rest_ring.step(first_ring.up, first_ring.down)
    first_pieces = first_ring.pieces
    count = len(first_pieces)
    if count == 1:
        out_columns = first_pieces[0][:, 3 * part :]
    else:

        def assemble(*refs):
            *pieces, me_ref, target, sems = refs
            finish(load(pieces, me_ref, dp_count, target, sems, slice(3 * part, 4 * part)))

        (out_columns,) = call(
            assemble, [], [], first_pieces, [me], [dma(count)], [shaped((width, part), BF16)]
        )
    out_far, out_near = swap(out_columns, 2), swap(out_columns, 1)
    pairs = heads // 2
    qkv, attn, logs = call(
        functools.partial(attend_kernel, scale, dp_count, count),
        [
            shaped((seq_len, 3 * part), BF16),
            shaped((seq_len, part), BF16),
            shaped((diagonals * pairs, 2 * BLOCK), F32),
        ],
        [hold(act_one, out_columns), bias, mask],
        first_pieces,
        [me],
        [pltpu.VMEM((width, 3 * part), BF16), dma(count)],
        micros=5,
    )
    attn = hold(attn, rest_ring.up, rest_ring.down)
    attn_far, attn_near = swap(attn, 2), swap(attn, 1)
    rest_ring.step(attn)
    attn_last = swap(attn_far, 1)
    out_last = swap(out_far, 1)
    resid, act_two = call(
        branch_kernel,
        [shaped((tok, width), F32), shaped((tok, width), BF16)],
        [tokens, norm_gain, norm_shift],
        [attn, attn_near, attn_far, attn_last, out_columns, out_near, out_far, out_last],
        [me],
        [pltpu.VMEM((width, width), BF16), pltpu.VMEM((tok, width), BF16), dma(4), dma(4)],
        micros=2.4,
    )
    act_two = hold(act_two, rest_ring.up, rest_ring.down)
    act_far, act_near = swap(act_two, 2), swap(act_two, 1)
    rest_ring.step(act_two)
    act_last = swap(act_far, 1)
    rest_ring.step(act_last)
    shares = [shaped((tok, width), F32)] + [shaped((tok, width), BF16)] * 3
    fed, grad_feed, own_two, *sends = call(
        functools.partial(feed_kernel, dp_count, count),
        [shaped((seq_len, ff_part), BF16), shaped((dp_count, rows_here, 2 * width), BF16)] + shares,
        [],
        in_hbm([up_all, act_two, act_near, act_far, act_last, *rest_ring.pieces]),
        [me],
        [
            pltpu.VMEM((seq_len, width), BF16),
            pltpu.VMEM((seq_len, width), BF16),
            pltpu.VMEM((width, ff_part), BF16),
            pltpu.VMEM((ff_part, width), BF16),
            pltpu.VMEM((seq_len, ff_part), F32),
            pltpu.VMEM((seq_len, ff_part), BF16),
            dma(4),
            dma(1),
            dma(count),
            dma(count),
        ],
        micros=9,
    )

    sent_two = exchange_sp(sends)
    feed_grads = ScatterRing(grad_feed, me, dp_count)
    feed_grads.step()
    feed_grads.step(*sent_two)
    own_out, *out_sends = call(
        functools.partial(feed_out_kernel, dp_count, count),
        shares,
        [fed],
        in_hbm(rest_ring.pieces),
        [me],
        [pltpu.VMEM((ff_part, width), BF16), dma(count)],
        micros=3,
    )
    grad_resid, sums_two, *sends = call(
        branch_back_kernel,
        [shaped((tok, width), F32), shaped((8, width), F32)] + [shaped((tok, 2 * part), BF16)] * 4,
        [hold(own_two, own_out, *feed_grads.sums()), resid, cotangent[0], norm_gain],
        [*sent_two, out_columns, out_near, out_far, out_last],
        [me],
        [
            pltpu.VMEM((tok, width), BF16),
            pltpu.VMEM((tok, width), BF16),
            pltpu.VMEM((3 * tok, width), BF16),
            pltpu.VMEM((width, width), BF16),
            dma(3),
            dma(4),
        ],
        micros=2.5,
    )
    grad_pieces = [sends[0]] + exchange_sp(sends[1:])
    feed_grads.step(*grad_pieces[1:])
    last_rows = rows_here + SMALL_ROWS if aligned else rows_here
    last, small, own_one, *sends = call(
        functools.partial(attend_back_kernel, scale, dp_count, count),
        [shaped((dp_count, last_rows, 4 * part), BF16), shaped((8, width), F32)] + shares,
        [hold(qkv, *feed_grads.sums()), logs, bias, mask, act_one, normed_one, sums_two, buckets],
        [attn, attn_near, attn_far, attn_last, *grad_pieces, *first_pieces],
        [me],
        [
            pltpu.VMEM((seq_len, part), BF16),
            pltpu.VMEM((seq_len, part), BF16),
            pltpu.VMEM((4 * seq_len, part), BF16),
            pltpu.VMEM((seq_len, 3 * part), BF16),
            pltpu.VMEM((seq_len, part), F32),
            pltpu.VMEM((seq_len, part), F32),
            pltpu.VMEM((pairs, diagonals, BLOCK, 2 * BLOCK), F32),
            pltpu.VMEM((heads, seq_len + BLOCK), F32),
            pltpu.VMEM((seq_len, width), F32),
            pltpu.VMEM((width, 3 * part), BF16),
            dma(4),
            dma(4),
            dma(4),
            dma(count),
        ],
        micros=9.4,
    )
    if not aligned:
        table = jnp.zeros((head_total * bucket_count,), F32)
        table = lax.dynamic_update_slice_in_dim(table, small[4, :BLOCK], me_sp * BLOCK, 0)
        packed = [small[at].reshape(dp_count, -1) for at in range(4)] + [table.reshape(dp_count, -1)]
        packed = jnp.concatenate(packed, axis=1).astype(BF16)
        packed = jnp.pad(packed, ((0, 0), (0, 4 * part - packed.shape[1])))
        packed = jnp.pad(packed[:, None], ((0, 0), (0, SMALL_ROWS - 1), (0, 0)))
        last = jnp.concatenate([last, packed], axis=1)
    last_grads = ScatterRing(last, me, dp_count)
    last_grads.step()
    feed_grads.step(small)
    last_grads.step(*feed_grads.sums())
    sent_out = exchange_sp([hold(send, small) for send in out_sends])
    sent_one = exchange_sp([hold(send, *sent_out, *last_grads.sums()) for send in sends])
    last_grads.step()
    (grad_input,) = call(
        norm_back_kernel,
        [shaped((tok, width), F32)],
        [hold(own_one, *last_grads.sums()), tokens, grad_resid, norm_gain],
        sent_one,
        (),
        [pltpu.VMEM((3 * tok, width), BF16), dma(3)],
        micros=1.4,
    )

    sum_feed = feed_grads.finish(grad_input)
    last_grads.step(grad_input, sum_feed)
    feed_pieces = gather_sp(hold(sum_feed, *last_grads.sums()))
    (output,) = call(
        out_kernel,
        [shaped((tok, width), BF16)],
        [hold(own_out, *last_grads.sums()), resid],
        sent_out,
        (),
        [pltpu.VMEM((3 * tok, width), BF16), dma(3)],
    )

    sum_last = last_grads.finish()
    last_pieces = gather_sp(sum_last)
    piece = width // dp_count
    table_here = head_total * bucket_count // dp_count
    if aligned:
        out_in, out_down = call(
            wide_feed_kernel,
            [shaped((rows_here, ff), F32), shaped((sp_count * ff_rows, width), F32)],
            [],
            feed_pieces,
            [me],
            [pltpu.VMEM((sp_count * rows_here, 2 * width), BF16), dma(4)],
        micros=3,
    )
        out_qkv, out_out, gains, shifts, tables = call(
            wide_last_kernel,
            [
                shaped((rows_here, 3 * width), F32),
                shaped((rows_here, width), F32),
                shaped((2, piece), F32),
                shaped((2, piece), F32),
                shaped((1, table_here), F32),
            ],
            [],
            last_pieces,
            [me],
            [pltpu.VMEM((sp_count * (rows_here + SMALL_ROWS), width), BF16), dma(4)],
        micros=2.3,
    )
        tables = tables[0]
    else:
        all_feed = stacked_sp(feed_pieces).astype(F32)
        out_down = all_feed[:, :, width:].reshape(sp_count * ff_rows, width)
        all_in = all_feed[:, :, :width].reshape(sp_count, rows_here, dp_count, ff_rows)
        out_in = jnp.moveaxis(all_in, 0, 2).reshape(rows_here, ff)
        all_last = stacked_sp(last_pieces).astype(F32)
        all_qkv = all_last[:, :rows_here, : 3 * part].reshape(sp_count, rows_here, 3, part)
        out_qkv = jnp.moveaxis(all_qkv, 0, 2).reshape(rows_here, 3 * width)
        out_out = jnp.moveaxis(all_last[:, :rows_here, 3 * part :], 0, 1).reshape(rows_here, width)
        small_row = jnp.sum(all_last[:, rows_here:], axis=0)[0]
        gains = small_row[: 2 * piece].reshape(2, piece)
        shifts = small_row[2 * piece : 4 * piece].reshape(2, piece)
        tables = small_row[4 * piece : 4 * piece + table_here]
    return (output[None], grad_input[None], out_qkv, out_out, out_in, out_down, gains, shifts, tables)


def solution(mesh):
    in_specs = (
        P("dp", "sp", None),
        P("dp", None),
        P("dp", None),
        P("dp", None),
        P("dp", None),
        P(),
        P(),
        P(),
        P("dp", None),
        P(),
        P("dp", "sp", None),
    )
    out_specs = (
        P("dp", "sp", None),
        P("dp", "sp", None),
        P("dp", None),
        P("dp", None),
        P("dp", None),
        P("dp", None),
        P(None, "dp"),
        P(None, "dp"),
        P("dp"),
    )
    return jax.shard_map(
        on_device, mesh=mesh, in_specs=in_specs, out_specs=out_specs, check_vma=False
    )
```

```python
import functools

import jax
import jax.numpy as jnp
from jax import lax
from jax.experimental import pallas as pl
from jax.experimental.pallas import tpu as pltpu
from jax.sharding import PartitionSpec as P

BLOCK = 128
SMALL_ROWS = 16
NEG = -1e30
BF16 = jnp.bfloat16
F32 = jnp.float32
VMEM_LIMIT = 24 * 1024 * 1024
ROOT = 0.7978845608028654
CUBE = 0.044715


def dot(left, right, left_dim=1, right_dim=0):
    return lax.dot_general(
        left, right, (((left_dim,), (right_dim,)), ((), ())), preferred_element_type=F32
    )


def exact_dot(left, right, left_dim=1, right_dim=0):
    return lax.dot_general(
        left,
        right,
        (((left_dim,), (right_dim,)), ((), ())),
        precision=lax.Precision.HIGHEST,
        preferred_element_type=F32,
    )


def layer_norm(values):
    average = jnp.mean(values, axis=-1, keepdims=True)
    centred = values - average
    inverse = lax.rsqrt(jnp.mean(centred * centred, axis=-1, keepdims=True) + 1e-05)
    return centred * inverse, inverse


def norm_back(upstream, normed, inverse, gain):
    scaled = upstream * gain
    centre_term = jnp.mean(scaled, axis=-1, keepdims=True)
    slope_term = jnp.mean(scaled * normed, axis=-1, keepdims=True)
    return inverse * (scaled - centre_term - normed * slope_term)


def shaped(shape, dtype):
    return jax.ShapeDtypeStruct(tuple(shape), dtype)


def call(kernel, outs, args=(), hbm_args=(), smem_args=(), scratch=(), hbm_outs=(), micros=1):
    specs = [pl.BlockSpec(memory_space=pltpu.VMEM)] * len(args)
    specs += [pl.BlockSpec(memory_space=pltpu.HBM)] * len(hbm_args)
    specs += [pl.BlockSpec(memory_space=pltpu.SMEM)] * len(smem_args)
    out_specs = [pl.BlockSpec(memory_space=pltpu.VMEM)] * len(outs)
    out_specs += [pl.BlockSpec(memory_space=pltpu.HBM)] * len(hbm_outs)
    return pl.pallas_call(
        kernel,
        out_shape=(*outs, *hbm_outs),
        in_specs=specs,
        out_specs=tuple(out_specs),
        scratch_shapes=list(scratch),
        compiler_params=pltpu.CompilerParams(vmem_limit_bytes=VMEM_LIMIT),
        cost_estimate=pl.CostEstimate(flops=0, bytes_accessed=int(micros * 3.3e6), transcendentals=0),
    )(*args, *hbm_args, *smem_args)


def rank_at(position, count):
    position = lax.rem(position + 2 * count, count)
    return jnp.where(position < count // 2, 2 * position, 2 * (count - 1 - position) + 1)


def position_of(rank, count):
    return jnp.where(lax.rem(rank, 2) == 0, lax.div(rank, 2), count - 1 - lax.div(rank, 2))


def ring_pairs(count):
    order = list(range(0, count, 2)) + list(range(count - 1, 0, -2))
    forward = [(order[i], order[(i + 1) % count]) for i in range(count)]
    return forward, [(b, a) for a, b in forward]


def half_rows(rows):
    return rows // 2 // 16 * 16


def hold(value, *others):
    return lax.optimization_barrier((value, others))[0] if others else value


def halves(up, down):
    rows, columns = up.shape
    half = half_rows(rows)

    def kernel(up_ref, down_ref, upper_ref, lower_ref, sems):
        copies = [
            pltpu.make_async_copy(up_ref.at[:half, :], upper_ref, sems.at[0]),
            pltpu.make_async_copy(down_ref.at[half:, :], lower_ref, sems.at[1]),
        ]
        finish(start_all(copies))

    outs = [shaped((half, columns), up.dtype), shaped((rows - half, columns), up.dtype)]
    return call(kernel, outs, [], [up, down], scratch=[dma(2)])


class GatherRing:
    def __init__(self, shard, count):
        self.shard, self.count, self.at = shard, count, 0
        self.up = self.down = shard
        self.pieces, self.held = [shard], (shard, shard)

    def step(self, *others):
        self.at += 1
        if self.count != 8:
            if self.at == 1:
                self.up = self.down = lax.all_gather(self.shard, "dp", axis=0, tiled=True)
                self.pieces = [self.up]
            return
        forward, backward = ring_pairs(self.count)
        up, down = self.up, self.down
        if self.at == self.count // 2:
            up, down = halves(up, down)
        self.held = up, down
        up, down, *_ = lax.optimization_barrier((up, down, *others))
        self.up = lax.ppermute(up, "dp", forward)
        self.down = lax.ppermute(down, "dp", backward)
        self.pieces += [self.up, self.down]


def target_rows(parts, me_ref, count, step):
    at = position_of(me_ref[1], count)
    near, far = count // 2 - step, count // 2 + 1 - step
    middle = parts.shape[2] // 2
    left, right = slice(0, middle), slice(middle, 2 * middle)
    up = parts.at[rank_at(at + far, count), :, left], parts.at[rank_at(at + near, count), :, right]
    down = parts.at[rank_at(at - near, count), :, left], parts.at[rank_at(at - far, count), :, right]
    return up, down


def store_first(parts, me_ref, up_ref, down_ref):
    middle = parts.shape[2] // 2
    for target, (left, right) in zip((up_ref, down_ref), target_rows(parts, me_ref, parts.shape[0], 1)):
        target[:, :middle] = left[...]
        target[:, middle:] = right[...]


def ring_add_kernel(count, step, *refs):
    parts, up_ref, down_ref, me_ref = refs[:4]
    up_out, down_out, mine, up, down, sems = refs[4:]
    middle = parts.shape[2] // 2
    left, right = slice(0, middle), slice(middle, 2 * middle)
    (up_left, up_right), (down_left, down_right) = target_rows(parts, me_ref, count, step)
    last = step == count // 2
    copies = [
        pltpu.make_async_copy(up_ref.at[:, left if last else slice(None)], up.at[:, left if last else slice(None)], sems.at[0]),
        pltpu.make_async_copy(down_ref.at[:, right if last else slice(None)], down.at[:, right if last else slice(None)], sems.at[1]),
        pltpu.make_async_copy(up_left, mine.at[0, :, left], sems.at[2]),
        pltpu.make_async_copy(down_right, mine.at[1, :, right], sems.at[3]),
    ]
    if not last:
        copies.append(pltpu.make_async_copy(up_right, mine.at[0, :, right], sems.at[4]))
        copies.append(pltpu.make_async_copy(down_left, mine.at[1, :, left], sems.at[5]))
    finish(start_all(copies))
    up_lanes, down_lanes = (left, right) if last else (slice(None), slice(None))
    up_out[...] = (mine[0, :, up_lanes].astype(F32) + up[:, up_lanes].astype(F32)).astype(BF16)
    down_out[...] = (mine[1, :, down_lanes].astype(F32) + down[:, down_lanes].astype(F32)).astype(BF16)


def ring_total_kernel(count, parts, up_ref, down_ref, last_up_ref, last_down_ref, me_ref, out_ref, mine, first, last, sems):
    middle = parts.shape[2] // 2
    left, right = slice(0, middle), slice(middle, 2 * middle)
    copies = [
        pltpu.make_async_copy(parts.at[me_ref[1]], mine, sems.at[0]),
        pltpu.make_async_copy(down_ref.at[:, left], first.at[:, left], sems.at[1]),
        pltpu.make_async_copy(up_ref.at[:, right], first.at[:, right], sems.at[2]),
        pltpu.make_async_copy(last_up_ref, last.at[:, left], sems.at[3]),
        pltpu.make_async_copy(last_down_ref, last.at[:, right], sems.at[4]),
    ]
    finish(start_all(copies))
    total = mine[...].astype(F32) + first[...].astype(F32) + last[...].astype(F32)
    out_ref[...] = total.astype(BF16)


class ScatterRing:
    def __init__(self, parts, first, me, count):
        self.parts, self.me, self.count, self.at = parts, me, count, 0
        self.added = first

    def step(self, *others):
        self.at += 1
        if self.count != 8:
            return
        forward, backward = ring_pairs(self.count)
        rows, columns = self.parts.shape[1:]
        if self.at > 1:
            width = columns // 2 if self.at == self.count // 2 else columns
            self.before = self.up, self.down
            self.added = call(
                functools.partial(ring_add_kernel, self.count, self.at),
                [shaped((rows, width), BF16)] * 2,
                [],
                [self.parts, hold(self.up, *others), self.down],
                [self.me],
                [pltpu.VMEM((2, rows, columns), BF16)] + [pltpu.VMEM((rows, columns), BF16)] * 2 + [dma(6)],
            )
        up, down = self.added
        self.up = lax.ppermute(up, "dp", forward)
        self.down = lax.ppermute(down, "dp", backward)

    def sent(self):
        return (self.up, self.down) if self.count == 8 else ()

    def sums(self):
        return tuple(self.added) if self.count == 8 else ()

    def finish(self, *others):
        if self.count != 8:
            return lax.psum_scatter(self.parts, "dp", scatter_dimension=0)
        rows, columns = self.parts.shape[1:]
        return call(
            functools.partial(ring_total_kernel, self.count),
            [shaped((rows, columns), BF16)],
            [],
            [self.parts, *self.before, hold(self.up, *others), self.down],
            [self.me],
            [pltpu.VMEM((rows, columns), BF16)] * 3 + [dma(5)],
        )[0]


def swap(values, bit):
    count = lax.axis_size("sp")
    return lax.ppermute(values, "sp", [(i, i ^ bit) for i in range(count)])


def gather_sp(piece):
    far = swap(piece, 2)
    near = swap(piece, 1)
    return [piece, near, far, swap(far, 1)]


def far_kernel(far_ref, near_ref, out_ref, near, sems):
    finish(start_all([pltpu.make_async_copy(near_ref.at[far_ref.shape[0] :, :], near, sems.at[0])]))
    out_ref[...] = (far_ref[...] + near[...].astype(F32)).astype(BF16)


def add_far(far, near):
    return call(
        far_kernel,
        [shaped(far.shape, BF16)],
        [far],
        [near],
        (),
        [pltpu.VMEM(far.shape, BF16), dma(1)],
    )[0]


def exchange_sp(sends):
    return [swap(send, step) for step, send in enumerate(sends, 1)]


def place(step, size, me_ref):
    return pl.multiple_of((me_ref[0] ^ step) * size, size)


def in_hbm(pieces):
    return [pltpu.with_memory_space_constraint(piece, pltpu.HBM) for piece in pieces]


def start_all(copies):
    for copy in copies:
        copy.start()
    return copies


def finish(copies):
    for copy in copies:
        copy.wait()


def load(pieces, me_ref, count, target, sems, lanes=slice(None)):
    if len(pieces) == 1:
        starts = [0]
    else:
        at = position_of(me_ref[1], count)
        rows = pieces[0].shape[0]
        starts = [rank_at(at + step, count) * rows for step in (0, -1, 1, -2, 2, -3, 3, 4)]
        starts.append(starts[-1] + half_rows(rows))
    copies = []
    for at, (start, piece) in enumerate(zip(starts, pieces)):
        rows = pl.ds(pl.multiple_of(start, 16), piece.shape[0])
        copies.append(pltpu.make_async_copy(piece.at[:, lanes], target.at[rows, :], sems.at[at]))
    return start_all(copies)


def load_rows(pieces, target, sems, me_ref=None, rows=slice(None), lanes=slice(None)):
    copies = []
    for step, piece in enumerate(pieces):
        block = piece.at[rows, lanes]
        size = block.shape[0]
        start = step * size if me_ref is None else place(step, size, me_ref)
        copies.append(pltpu.make_async_copy(block, target.at[pl.ds(start, size), :], sems.at[step]))
    return start_all(copies)


def dma(count):
    return pltpu.SemaphoreType.DMA((count,))


def share(sources, me, plan, rows):
    columns = sum(size for _, _, size, _ in plan)

    def kernel(*refs):
        *inputs, me_ref, target, sems = refs
        copies = []
        for at, (source, start, size, to) in enumerate(plan):
            if start is None:
                block = inputs[source].at[pl.ds(place(0, rows, me_ref), rows), :]
            else:
                block = inputs[source].at[:, pl.ds(start + place(0, size, me_ref), size)]
            copies.append(pltpu.make_async_copy(block, target.at[:, to : to + size], sems.at[at]))
        finish(start_all(copies))

    return call(
        kernel,
        [pltpu.VMEM((rows, columns), BF16)],
        [],
        [pltpu.with_memory_space_constraint(source, pltpu.HBM) for source in sources],
        [me],
        [dma(len(plan))],
    )[0]


def padded(bucket_ref):
    return jnp.concatenate([jnp.full((1, BLOCK), -1, jnp.int32), bucket_ref[...]], axis=1)


def bias_kernel(table_ref, bucket_ref, seg_ref, me_ref, bias_ref, mask_ref):
    heads, diagonals = bias_ref.shape[:2]
    buckets = padded(bucket_ref)
    bucket = lax.broadcasted_iota(jnp.int32, (table_ref.shape[1], buckets.shape[1]), 0)
    chosen = (bucket == buckets).astype(F32)
    rows = exact_dot(table_ref[...], chosen)
    row = lax.broadcasted_iota(jnp.int32, rows.shape, 0)
    for head in range(heads):
        mine = jnp.sum(jnp.where(row == me_ref[0] * heads + head, rows, 0.0), axis=0, keepdims=True)
        for diagonal in range(diagonals):
            part = mine[:, diagonal * BLOCK : (diagonal + 2) * BLOCK]
            spread = jnp.broadcast_to(part, (BLOCK, 2 * BLOCK))
            rolled = pltpu.roll(spread, BLOCK, 1, stride=1, stride_axis=0)
            bias_ref[head, diagonal] = rolled[:, :BLOCK]
    segments = seg_ref[...].astype(F32)
    key = lax.broadcasted_iota(jnp.int32, (BLOCK, BLOCK), 0)
    query = lax.broadcasted_iota(jnp.int32, (BLOCK, BLOCK), 1)
    for block in range(diagonals):
        rows = slice(block * BLOCK, (block + 1) * BLOCK)
        keys = jnp.broadcast_to(segments[:, rows], (BLOCK, BLOCK)).T
        for index in range(block, diagonals):
            same = keys == segments[:, index * BLOCK : (index + 1) * BLOCK]
            if index == block:
                same = same & (query >= key)
            mask_ref[index, rows, :] = jnp.where(same, 0.0, NEG).astype(F32)


def norm_kernel(*refs):
    pieces, (gain_ref, shift_ref), me_ref = refs[2:6], refs[:2], refs[6]
    act_ref, normed_ref, up_ref, tokens, sems, up_sems = refs[7:]
    tok = up_ref.shape[0] // 4
    copies = load_rows(pieces, tokens, sems, me_ref, slice(0, tok))
    up_copies = load_rows(pieces, up_ref, up_sems, None, slice(tok, 2 * tok))
    finish(copies)
    for start in range(0, tokens.shape[0], BLOCK):
        rows = slice(start, start + BLOCK)
        normed, _ = layer_norm(tokens[rows, :].astype(F32))
        act_ref[rows, :] = (normed * gain_ref[0:1, :] + shift_ref[0:1, :]).astype(BF16)
        normed_ref[rows, :] = normed.astype(BF16)
    finish(up_copies)


def split_heads(rows):
    lane = lax.broadcasted_iota(jnp.int32, (1, BLOCK), 1)
    low = (lane < BLOCK // 2).astype(F32).astype(BF16)
    return jnp.concatenate([rows * low, rows * (1 - low)], axis=0)


def join_heads(both):
    half = BLOCK // 2
    return jnp.concatenate([both[:half, :BLOCK], both[half:, BLOCK:]], axis=0).T


def score_block(raw, bias_ref, mask_ref, pair, index, block):
    rows = slice(block * BLOCK, (block + 1) * BLOCK)
    mask = mask_ref[index, rows, :]
    return jnp.concatenate(
        [
            raw[rows, side * BLOCK : (side + 1) * BLOCK] + bias_ref[2 * pair + side, index - block] + mask
            for side in range(2)
        ],
        axis=1,
    )


def attend_kernel(scale, parts, count, *refs):
    act_ref, bias_ref, mask_ref = refs[:3]
    pieces, me_ref = refs[3 : 3 + count], refs[3 + count]
    qkv_ref, attn_ref, log_ref, weight, sems = refs[4 + count :]
    columns = attn_ref.shape[1]
    copies = load(pieces, me_ref, parts, weight, sems, slice(0, 3 * columns))
    finish(copies)
    for start in range(0, 3 * columns, columns):
        lanes = slice(start, start + columns)
        qkv_ref[:, lanes] = dot(act_ref[...], weight[:, lanes]).astype(BF16)
    for index in range(qkv_ref.shape[0] // BLOCK):
        rows = slice(index * BLOCK, (index + 1) * BLOCK)
        width = (index + 1) * BLOCK
        for pair in range(columns // BLOCK):
            lanes = slice(pair * BLOCK, (pair + 1) * BLOCK)
            queries = split_heads(qkv_ref[rows, lanes] * scale)
            keys = qkv_ref[:width, columns + pair * BLOCK : columns + (pair + 1) * BLOCK]
            values = qkv_ref[:width, 2 * columns + pair * BLOCK : 2 * columns + (pair + 1) * BLOCK]
            raw = dot(keys, queries, 1, 1)
            scores = [score_block(raw, bias_ref, mask_ref, pair, index, block) for block in range(index + 1)]
            largest = functools.reduce(
                jnp.maximum, [jnp.max(score, axis=0, keepdims=True) for score in scores]
            )
            weights = [jnp.exp(score - largest) for score in scores]
            total = functools.reduce(jnp.add, [jnp.sum(one, axis=0, keepdims=True) for one in weights])
            mixed = dot(values, jnp.concatenate([one.astype(BF16) for one in weights], axis=0), 0, 0)
            attn_ref[rows, lanes] = join_heads(mixed / total).astype(BF16)
            at = index * (columns // BLOCK) + pair
            log_ref[at : at + 1, :] = largest + jnp.log(total)


def branch_kernel(*refs):
    tokens_ref, gain_ref, shift_ref, attn_refs, weight_refs, me_ref = (*refs[:3], refs[3:7], refs[7:11], refs[11])
    resid_ref, act_ref, weight, own, sems, weight_sems = refs[12:]
    tok = tokens_ref.shape[0]
    part = weight_refs[0].shape[1]
    copies = []
    for step in range(4):
        columns = pl.ds(place(step, part, me_ref), part)
        rows = pl.ds(place(0, tok, me_ref), tok)
        copies.append(pltpu.make_async_copy(attn_refs[step].at[rows, :], own.at[:, columns], sems.at[step]))
        copies.append(pltpu.make_async_copy(weight_refs[step], weight.at[:, columns], weight_sems.at[step]))
    finish(start_all(copies))
    resid = tokens_ref[...].astype(F32) + dot(own[...], weight[...])
    resid_ref[...] = resid
    normed, _ = layer_norm(resid)
    act_ref[...] = (normed * gain_ref[1:2, :] + shift_ref[1:2, :]).astype(BF16)


def outer(left, right, grad_ref):
    parts, rows_here, _ = grad_ref.shape
    for start in range(0, parts * rows_here, 2 * BLOCK):
        block = dot(left[:, start : start + 2 * BLOCK], right[...], 0, 0).astype(BF16)
        for sub in range(2 * BLOCK // rows_here):
            grad_ref[start // rows_here + sub] = block[sub * rows_here : (sub + 1) * rows_here]


def store_shares(total, own_ref, send_refs, columns):
    tok = own_ref.shape[0]
    own_ref[:, columns] = total[:tok]
    for step, send in enumerate(send_refs, 1):
        send[:, columns] = total[step * tok : (step + 1) * tok].astype(BF16)


def store_pairs(total, own_ref, far_ref, send_ref, columns):
    tok = own_ref.shape[0]
    own_ref[:, columns] = total[:tok]
    far_ref[:, columns] = total[2 * tok : 3 * tok].astype(far_ref.dtype)
    send_ref[:tok, columns] = total[tok : 2 * tok].astype(BF16)
    send_ref[tok:, columns] = total[3 * tok :].astype(BF16)


def feed_kernel(parts, count, *refs):
    up_from, act_refs, pieces, me_ref = refs[0], refs[1:5], refs[5 : 5 + count], refs[5 + count]
    grad_ref, up_first, down_first, own_ref, *send_refs, own_out_ref, far_out_ref, send_out_ref = refs[
        6 + count : 16 + count
    ]
    act, up_ref, weight, down, slope, hidden, fed_ref, act_sems, up_sems, sems, down_sems = refs[16 + count :]
    width = weight.shape[1]
    copies = load(pieces, me_ref, parts, weight, sems, slice(0, width)) + load_rows(act_refs, act, act_sems)
    late = load(pieces, me_ref, parts, down, down_sems, slice(width, None))
    late += start_all([pltpu.make_async_copy(up_from, up_ref, up_sems.at[0])])
    finish(copies)
    for start in range(0, width, 2 * BLOCK):
        columns = slice(start, start + 2 * BLOCK)
        units = dot(act[...], weight[:, columns])
        square = units * units
        bend = jnp.tanh(ROOT * units * (1.0 + CUBE * square))
        fed_ref[:, columns] = (0.5 * units * (1.0 + bend)).astype(BF16)
        slope[:, columns] = 0.5 * (1.0 + bend) + 0.5 * units * (1.0 - bend * bend) * ROOT * (
            1.0 + 3.0 * CUBE * square
        )
    finish(late)
    for start in range(0, width, 2 * BLOCK):
        rows = slice(start, start + 2 * BLOCK)
        hidden[:, rows] = (dot(up_ref[...], down[rows, :], 1, 1) * slope[:, rows]).astype(BF16)
    for start in range(0, weight.shape[0], 2 * BLOCK):
        rows = slice(start, start + 2 * BLOCK)
        store_shares(dot(hidden[...], weight[rows, :], 1, 1), own_ref, send_refs, rows)
    for start in range(0, down.shape[1], 2 * BLOCK):
        columns = slice(start, start + 2 * BLOCK)
        store_pairs(dot(fed_ref[...], down[:, columns]), own_out_ref, far_out_ref, send_out_ref, columns)
    rows_here = grad_ref.shape[1]
    for at, (left, right) in enumerate([(act, hidden), (fed_ref, up_ref)]):
        lanes = slice(at * width, (at + 1) * width)
        for start in range(0, parts * rows_here, 2 * BLOCK):
            block = dot(left[:, start : start + 2 * BLOCK], right[...], 0, 0).astype(BF16)
            for sub in range(2 * BLOCK // rows_here):
                grad_ref[start // rows_here + sub, :, lanes] = block[sub * rows_here : (sub + 1) * rows_here]
    if parts == 8:
        store_first(grad_ref, me_ref, up_first, down_first)


def branch_back_kernel(*refs):
    own_ref, resid_ref, up_ref, gain_ref, sent, weight_refs, me_ref = (*refs[:4], refs[4:7], refs[7:11], refs[11])
    grad_ref, sums_ref, *send_refs, branch, grad_attn, rest, weight, sems, weight_sems = refs[12:]
    tok = up_ref.shape[0]
    part = send_refs[0].shape[1] // 2
    copies = load_rows(sent, rest, sems)
    late = []
    for step in range(4):
        columns = pl.ds(place(step, part, me_ref), part)
        late.append(pltpu.make_async_copy(weight_refs[step], weight.at[:, columns], weight_sems.at[step]))
    start_all(late)
    normed, inverse = layer_norm(resid_ref[...])
    finish(copies)
    upstream = own_ref[...]
    for step in range(3):
        upstream += rest[step * tok : (step + 1) * tok, :].astype(F32)
    sums_ref[0:1, :] = jnp.sum(upstream * normed, axis=0, keepdims=True)
    sums_ref[1:2, :] = jnp.sum(upstream, axis=0, keepdims=True)
    sums_ref[2:, :] = jnp.zeros_like(sums_ref[2:, :])
    grad = up_ref[...].astype(F32) + norm_back(upstream, normed, inverse, gain_ref[1:2, :])
    grad_ref[...] = grad
    branch[...] = grad.astype(BF16)
    finish(late)
    grad_attn[...] = dot(branch[...], weight[...], 1, 1).astype(BF16)
    for step, send in enumerate(send_refs):
        columns = pl.ds(place(step, part, me_ref), part)
        send[:, :part] = grad_attn[:, columns]
        send[:, part:] = branch[:, columns]


def attend_back_kernel(scale, dp_count, count, *refs):
    qkv_ref, log_ref, bias_ref, mask_ref, act_ref, normed_ref, sums_ref, bucket_ref = refs[:8]
    far_out_ref, send_out_ref, attn_refs, grad_refs = refs[8], refs[9], refs[10:14], refs[14:18]
    pieces, me_ref = refs[18 : 18 + count], refs[18 + count]
    last_ref, up_first, down_first, small_ref, own_ref, far_ref, send_ref = refs[19 + count : 26 + count]
    grads, branch, attn, grad_qkv, key_acc, value_acc, diagonal_acc, stacked, shares, weight_ref = refs[
        26 + count : 36 + count
    ]
    grad_sems, branch_sems, attn_sems, sems, out_sems = refs[36 + count :]
    seq_len = qkv_ref.shape[0]
    columns = qkv_ref.shape[1] // 3
    heads, diagonals = bias_ref.shape[:2]
    tok = own_ref.shape[0]
    copies = load_rows(grad_refs, grads, grad_sems, me_ref, lanes=slice(0, columns))
    late = load_rows(grad_refs, branch, branch_sems, me_ref, lanes=slice(columns, 2 * columns))
    late += load_rows(attn_refs, attn, attn_sems)
    late += load(pieces, me_ref, dp_count, weight_ref, sems, slice(0, 3 * columns))
    late += start_all(
        [
            pltpu.make_async_copy(far_out_ref, far_ref.at[tok:, :], out_sems.at[0]),
            pltpu.make_async_copy(send_out_ref.at[:tok, :], send_ref.at[tok : 2 * tok, :], out_sems.at[1]),
            pltpu.make_async_copy(send_out_ref.at[tok:, :], send_ref.at[3 * tok :, :], out_sems.at[2]),
        ]
    )
    key_acc[...] = jnp.zeros_like(key_acc)
    value_acc[...] = jnp.zeros_like(value_acc)
    diagonal_acc[...] = jnp.zeros_like(diagonal_acc)
    finish(copies)
    for pair in range(columns // BLOCK):
        lanes = slice(pair * BLOCK, (pair + 1) * BLOCK)
        all_keys = qkv_ref[:, columns + pair * BLOCK : columns + (pair + 1) * BLOCK]
        for index in range(seq_len // BLOCK):
            rows = slice(index * BLOCK, (index + 1) * BLOCK)
            width = (index + 1) * BLOCK
            queries = split_heads(qkv_ref[rows, lanes] * scale)
            grad_rows = split_heads(grads[rows, lanes])
            keys = all_keys[:width]
            values = qkv_ref[:width, 2 * columns + pair * BLOCK : 2 * columns + (pair + 1) * BLOCK]
            at = index * (columns // BLOCK) + pair
            logs = log_ref[at : at + 1, :]
            raw = dot(keys, queries, 1, 1)
            grad_probs = dot(values, grad_rows, 1, 1)
            probs = [
                jnp.exp(score_block(raw, bias_ref, mask_ref, pair, index, block) - logs)
                for block in range(index + 1)
            ]
            products = [
                one * grad_probs[block * BLOCK : (block + 1) * BLOCK] for block, one in enumerate(probs)
            ]
            row_term = functools.reduce(jnp.add, [jnp.sum(one, axis=0, keepdims=True) for one in products])
            grad_scores = [product - one * row_term for product, one in zip(products, probs)]
            for block, one in enumerate(grad_scores):
                diagonal_acc[pair, index - block] += one
            grad_raw = jnp.concatenate([one.astype(BF16) for one in grad_scores], axis=0)
            probs_all = jnp.concatenate([one.astype(BF16) for one in probs], axis=0)
            grad_qkv[rows, lanes] = (join_heads(dot(keys, grad_raw, 0, 0)) * scale).astype(BF16)
            key_acc[:width, lanes] += dot(grad_raw, queries)
            value_acc[:width, lanes] += dot(probs_all, grad_rows)
    grad_qkv[:, columns : 2 * columns] = key_acc[...].astype(BF16)
    grad_qkv[:, 2 * columns :] = value_acc[...].astype(BF16)

    parts, last_rows = last_ref.shape[:2]
    width = act_ref.shape[1]
    rows_here = width // parts
    for start in range(0, width, 2 * BLOCK):
        block = dot(act_ref[:, start : start + 2 * BLOCK], grad_qkv[...], 0, 0).astype(BF16)
        for sub in range(2 * BLOCK // rows_here):
            last_ref[start // rows_here + sub, :rows_here, : 3 * columns] = block[
                sub * rows_here : (sub + 1) * rows_here
            ]
    finish(late)
    for step in range(4):
        block = dot(attn[step * seq_len : (step + 1) * seq_len, :], branch[...], 0, 0).astype(BF16)
        for sub in range(columns // rows_here):
            part = (me_ref[0] ^ step) * (columns // rows_here) + sub
            last_ref[part, :rows_here, 3 * columns :] = block[sub * rows_here : (sub + 1) * rows_here]

    for start in range(0, width, 2 * BLOCK):
        lanes = slice(start, start + 2 * BLOCK)
        share_of = dot(grad_qkv[...], weight_ref[lanes, :], 1, 1)
        small_ref[0:1, lanes] = jnp.sum(share_of * normed_ref[:, lanes].astype(F32), axis=0, keepdims=True)
        small_ref[2:3, lanes] = jnp.sum(share_of, axis=0, keepdims=True)
        shares[:, lanes] = share_of
    for step, (target, to) in enumerate([(own_ref, 0), (send_ref, 0), (far_ref, 0), (send_ref, 2 * tok)]):
        rows = pl.ds(place(step, tok, me_ref), tok)
        target[to : to + tok, :] = shares[rows, :].astype(target.dtype)
    small_ref[1:2, :] = sums_ref[0:1, :]
    small_ref[3:4, :] = sums_ref[1:2, :]

    row = lax.broadcasted_iota(jnp.int32, (BLOCK, BLOCK), 0)
    column = lax.broadcasted_iota(jnp.int32, (BLOCK, BLOCK), 1)
    flip = (row + column == BLOCK - 1).astype(F32)
    stacked[...] = jnp.zeros_like(stacked)
    for pair in range(heads // 2):
        for diagonal in range(diagonals):
            both = exact_dot(flip, diagonal_acc[pair, diagonal])
            at = slice(diagonal * BLOCK, (diagonal + 2) * BLOCK)
            for side in range(2):
                block = both[:, side * BLOCK : (side + 1) * BLOCK]
                wide = jnp.concatenate([block, jnp.zeros_like(block)], axis=1)
                rolled = pltpu.roll(wide, 1, 1, stride=1, stride_axis=0)
                head = 2 * pair + side
                stacked[head : head + 1, at] += jnp.sum(rolled, axis=0, keepdims=True)
    buckets = BLOCK // heads
    distances = padded(bucket_ref)
    bucket = lax.rem(lax.broadcasted_iota(jnp.int32, (BLOCK, distances.shape[1]), 0), buckets)
    chosen = (bucket == distances).astype(F32)
    by_head = exact_dot(stacked[...], chosen, 1, 1)
    row = lax.broadcasted_iota(jnp.int32, by_head.shape, 0)
    column = lax.broadcasted_iota(jnp.int32, by_head.shape, 1)
    table = jnp.sum(jnp.where(lax.div(column, buckets) == row, by_head, 0.0), axis=0, keepdims=True)
    small_ref[4:5, :BLOCK] = table
    if last_rows > rows_here:
        last_ref[:, rows_here:, :] = jnp.zeros_like(last_ref[:, rows_here:, :])
        per = parts // 4
        for part in range(parts):
            for at in range(4):
                last_ref[part, rows_here : rows_here + 1, at * rows_here : (at + 1) * rows_here] = small_ref[
                    at : at + 1, part * rows_here : (part + 1) * rows_here
                ].astype(BF16)
            turned = table if part % per == 0 else pltpu.roll(table, BLOCK - part % per * (BLOCK // per), 1)
            turned = jnp.where(me_ref[0] == part // per, turned, 0.0)
            last_ref[part, rows_here : rows_here + 1, 4 * rows_here : 4 * rows_here + BLOCK] = turned.astype(BF16)
    if parts == 8:
        store_first(last_ref, me_ref, up_first, down_first)


def ends_kernel(own_ref, tokens_ref, grad_resid_ref, gain_ref, own_out_ref, resid_ref, *refs):
    near_ref, far_ref, grad_ref, out_ref, near, far, sems = refs
    copies = start_all(
        [
            pltpu.make_async_copy(near_ref.at[: near.shape[0], :], near, sems.at[0]),
            pltpu.make_async_copy(far_ref, far, sems.at[1]),
        ]
    )
    tok = own_ref.shape[0]
    normed, inverse = layer_norm(tokens_ref[...].astype(F32))
    finish(copies)
    upstream = own_ref[...] + near[:tok, :].astype(F32) + far[:tok, :].astype(F32)
    grad_ref[...] = grad_resid_ref[...] + norm_back(upstream, normed, inverse, gain_ref[0:1, :])
    total = resid_ref[...] + own_out_ref[...] + near[tok:, :].astype(F32) + far[tok:, :].astype(F32)
    out_ref[...] = total.astype(BF16)


def wide_feed_kernel(*refs):
    pieces, me_ref, in_ref, down_ref, both, sems = refs[:4], refs[4], refs[5], refs[6], refs[7], refs[8]
    finish(load_rows(pieces, both, sems))
    rows = in_ref.shape[0]
    width = down_ref.shape[1]
    for step in range(4):
        mine = slice(step * rows, (step + 1) * rows)
        down_ref[pl.ds(place(step, rows, me_ref), rows), :] = both[mine, width:].astype(F32)
        for start in range(0, width, rows):
            at = pl.multiple_of(4 * start + (me_ref[0] ^ step) * rows, rows)
            in_ref[:, pl.ds(at, rows)] = both[mine, start : start + rows].astype(F32)


def wide_last_kernel(*refs):
    pieces, me_ref = refs[:4], refs[4]
    qkv_ref, out_ref, gain_ref, shift_ref, table_ref, last, sems = refs[5:]
    finish(load_rows(pieces, last, sems))
    rows, width = out_ref.shape
    part = width // 4
    whole = rows + SMALL_ROWS
    small = jnp.zeros((1, width), F32)
    for step in range(4):
        start = step * whole
        mine = slice(start, start + rows)
        for third in range(3):
            at = pl.multiple_of(third * width + (me_ref[0] ^ step) * part, part)
            qkv_ref[:, pl.ds(at, part)] = last[mine, third * part : (third + 1) * part].astype(F32)
        out_ref[:, pl.ds(place(step, part, me_ref), part)] = last[mine, 3 * part :].astype(F32)
        small += last[start + rows : start + whole, :].astype(F32)[0:1]
    for at in range(2):
        gain_ref[at : at + 1, :] = small[:, at * rows : (at + 1) * rows]
        shift_ref[at : at + 1, :] = small[:, (2 + at) * rows : (3 + at) * rows]
    table_ref[...] = small[:, 4 * rows : 4 * rows + table_ref.shape[1]]


def stacked_sp(pieces):
    me = lax.axis_index("sp")
    whole = jnp.zeros((len(pieces),) + pieces[0].shape, pieces[0].dtype)
    for step, piece in enumerate(pieces):
        whole = lax.dynamic_update_index_in_dim(whole, piece, me ^ step, 0)
    return whole


def on_device(
    inputs,
    qkv_weight,
    out_weight,
    in_weight,
    down_weight,
    norm_gain,
    norm_shift,
    bias_table,
    segment_ids,
    bucket_index,
    cotangent,
):
    dp_count, sp_count = lax.axis_size("dp"), lax.axis_size("sp")
    me_sp = lax.axis_index("sp")
    me = jnp.stack([me_sp, lax.axis_index("dp")]).astype(jnp.int32)
    tok, width = inputs.shape[1:]
    head_total, bucket_count = bias_table.shape
    heads = head_total // sp_count
    scale = (width // head_total) ** (-0.5)
    seq_len = segment_ids.shape[1]
    rows_here = qkv_weight.shape[0]
    ff = in_weight.shape[1]
    ff_rows = ff // dp_count // sp_count
    ff_part = ff // sp_count
    part = width // sp_count
    diagonals = seq_len // BLOCK
    aligned = ff_rows % BLOCK == 0 and rows_here % BLOCK == 0

    if aligned:
        plan = [(0, third * width, part, third * part) for third in range(3)] + [(1, 0, part, 3 * part)]
        first_part = share([qkv_weight, out_weight], me, plan, rows_here)
        step = sp_count * ff_rows
        plan = [(0, index * step, ff_rows, index * ff_rows) for index in range(dp_count)]
        plan.append((1, None, width, ff_part))
        rest_part = share([hold(in_weight, first_part), down_weight], me, plan, rows_here)
    else:

        def own_sp(stacked, axis):
            return lax.dynamic_index_in_dim(stacked, me_sp, axis, keepdims=False)

        first_part = own_sp(qkv_weight.reshape(rows_here, 3, sp_count, part), 2).reshape(rows_here, 3 * part)
        out_part = own_sp(out_weight.reshape(rows_here, sp_count, part), 1)
        first_part = jnp.concatenate([first_part, out_part], axis=1)
        in_part = own_sp(in_weight.reshape(rows_here, dp_count, sp_count, ff_rows), 2)
        in_part = in_part.reshape(rows_here, ff_part)
        down_part = lax.dynamic_slice_in_dim(down_weight, me_sp * ff_rows, ff_rows, 0)
        rest_part = jnp.concatenate([in_part, down_part], axis=1)
    first_ring = GatherRing(first_part, dp_count)
    rest_ring = GatherRing(rest_part, dp_count)

    tokens = inputs[0]
    first_ring.step()

    buckets = bucket_index[None]
    bias, mask = call(
        bias_kernel,
        [shaped((heads, diagonals, BLOCK, BLOCK), F32), shaped((diagonals, seq_len, BLOCK), F32)],
        [bias_table, hold(buckets, first_part), segment_ids],
        (),
        [me],
        micros=1.2,
    )
    both = jnp.concatenate([hold(tokens, first_part), cotangent[0]], axis=0)
    token_far, token_near = swap(both, 2), swap(both, 1)
    first_ring.step(bias, rest_part)
    token_last = swap(token_far, 1)
    first_ring.step(token_far)
    act_one, normed_one, up_all = call(
        norm_kernel,
        [shaped((seq_len, width), BF16)] * 3,
        [hold(norm_gain, *first_ring.held), norm_shift],
        [both, token_near, token_far, token_last],
        [me],
        [pltpu.VMEM((seq_len, width), BF16), dma(4), dma(4)],
        micros=2.4,
    )
    first_ring.step()
    rest_ring.step(first_ring.up, first_ring.down)
    first_pieces = first_ring.pieces
    count = len(first_pieces)
    if count == 1:
        out_columns = first_pieces[0][:, 3 * part :]
    else:

        def assemble(*refs):
            *pieces, me_ref, target, sems = refs
            finish(load(pieces, me_ref, dp_count, target, sems, slice(3 * part, 4 * part)))

        (out_columns,) = call(
            assemble, [], [], first_pieces, [me], [dma(count)], [shaped((width, part), BF16)]
        )
    out_far, out_near = swap(out_columns, 2), swap(out_columns, 1)
    pairs = heads // 2
    qkv, attn, logs = call(
        functools.partial(attend_kernel, scale, dp_count, count),
        [
            shaped((seq_len, 3 * part), BF16),
            shaped((seq_len, part), BF16),
            shaped((diagonals * pairs, 2 * BLOCK), F32),
        ],
        [hold(act_one, out_columns), bias, mask],
        first_pieces,
        [me],
        [pltpu.VMEM((width, 3 * part), BF16), dma(count)],
        micros=5,
    )
    attn = hold(attn, rest_ring.up, rest_ring.down)
    attn_far, attn_near = swap(attn, 2), swap(attn, 1)
    rest_ring.step(attn)
    attn_last = swap(attn_far, 1)
    out_last = swap(out_far, 1)
    resid, act_two = call(
        branch_kernel,
        [shaped((tok, width), F32), shaped((tok, width), BF16)],
        [tokens, norm_gain, norm_shift],
        [attn, attn_near, attn_far, attn_last, out_columns, out_near, out_far, out_last],
        [me],
        [pltpu.VMEM((width, width), BF16), pltpu.VMEM((tok, width), BF16), dma(4), dma(4)],
        micros=2.4,
    )
    act_two = hold(act_two, rest_ring.up, rest_ring.down)
    act_far, act_near = swap(act_two, 2), swap(act_two, 1)
    rest_ring.step(act_two)
    act_last = swap(act_far, 1)
    rest_ring.step(act_last)
    shares = [shaped((tok, width), F32)] + [shaped((tok, width), BF16)] * 3
    pair_shares = [shaped((tok, width), F32), shaped((tok, width), BF16), shaped((2 * tok, width), BF16)]
    grad_feed, up_first, down_first, own_two, *sends, own_out, far_out, send_out = call(
        functools.partial(feed_kernel, dp_count, count),
        [shaped((dp_count, rows_here, 2 * width), BF16)] + [shaped((rows_here, 2 * width), BF16)] * 2
        + shares + pair_shares,
        [],
        in_hbm([up_all, act_two, act_near, act_far, act_last, *rest_ring.pieces]),
        [me],
        [
            pltpu.VMEM((seq_len, width), BF16),
            pltpu.VMEM((seq_len, width), BF16),
            pltpu.VMEM((width, ff_part), BF16),
            pltpu.VMEM((ff_part, width), BF16),
            pltpu.VMEM((seq_len, ff_part), F32),
            pltpu.VMEM((seq_len, ff_part), BF16),
            pltpu.VMEM((seq_len, ff_part), BF16),
            dma(4),
            dma(1),
            dma(count),
            dma(count),
        ],
        micros=9,
    )

    sent_two = exchange_sp(sends)
    feed_grads = ScatterRing(grad_feed, (up_first, down_first), me, dp_count)
    feed_grads.step()
    feed_grads.step(*sent_two)
    grad_resid, sums_two, *sends = call(
        branch_back_kernel,
        [shaped((tok, width), F32), shaped((8, width), F32)] + [shaped((tok, 2 * part), BF16)] * 4,
        [hold(own_two, *feed_grads.sums()), resid, cotangent[0], norm_gain],
        [*sent_two, out_columns, out_near, out_far, out_last],
        [me],
        [
            pltpu.VMEM((tok, width), BF16),
            pltpu.VMEM((tok, width), BF16),
            pltpu.VMEM((3 * tok, width), BF16),
            pltpu.VMEM((width, width), BF16),
            dma(3),
            dma(4),
        ],
        micros=2.5,
    )
    grad_pieces = [sends[0]] + exchange_sp(sends[1:])
    feed_grads.step(*grad_pieces[1:])
    last_rows = rows_here + SMALL_ROWS if aligned else rows_here
    last, up_first, down_first, small, own_one, far_both, send_both = call(
        functools.partial(attend_back_kernel, scale, dp_count, count),
        [shaped((dp_count, last_rows, 4 * part), BF16)] + [shaped((last_rows, 4 * part), BF16)] * 2
        + [shaped((8, width), F32)]
        + [shaped((tok, width), F32), shaped((2 * tok, width), BF16), shaped((4 * tok, width), BF16)],
        [hold(qkv, *feed_grads.sums()), logs, bias, mask, act_one, normed_one, sums_two, buckets],
        [far_out, send_out, attn, attn_near, attn_far, attn_last, *grad_pieces, *first_pieces],
        [me],
        [
            pltpu.VMEM((seq_len, part), BF16),
            pltpu.VMEM((seq_len, part), BF16),
            pltpu.VMEM((4 * seq_len, part), BF16),
            pltpu.VMEM((seq_len, 3 * part), BF16),
            pltpu.VMEM((seq_len, part), F32),
            pltpu.VMEM((seq_len, part), F32),
            pltpu.VMEM((pairs, diagonals, BLOCK, 2 * BLOCK), F32),
            pltpu.VMEM((heads, seq_len + BLOCK), F32),
            pltpu.VMEM((seq_len, width), F32),
            pltpu.VMEM((width, 3 * part), BF16),
            dma(4),
            dma(4),
            dma(4),
            dma(count),
            dma(3),
        ],
        micros=9.4,
    )
    if not aligned:
        table = jnp.zeros((head_total * bucket_count,), F32)
        table = lax.dynamic_update_slice_in_dim(table, small[4, :BLOCK], me_sp * BLOCK, 0)
        packed = [small[at].reshape(dp_count, -1) for at in range(4)] + [table.reshape(dp_count, -1)]
        packed = jnp.concatenate(packed, axis=1).astype(BF16)
        packed = jnp.pad(packed, ((0, 0), (0, 4 * part - packed.shape[1])))
        packed = jnp.pad(packed[:, None], ((0, 0), (0, SMALL_ROWS - 1), (0, 0)))
        last = jnp.concatenate([last, packed], axis=1)
    last_grads = ScatterRing(last, hold((up_first, down_first), *feed_grads.sent()), me, dp_count)
    last_grads.step()
    near_both = swap(hold(send_both, *feed_grads.sent()), 1)
    feed_grads.step(small)
    last_grads.step(*feed_grads.sums(), near_both)
    sent_both = add_far(hold(far_both, *last_grads.sums()), near_both)
    last_both = swap(sent_both, 2)
    sum_feed = feed_grads.finish(sent_both)
    feed_far, feed_near = swap(sum_feed, 2), swap(sum_feed, 1)
    last_grads.step(sum_feed)
    last_grads.step(last_both)
    sum_last = last_grads.finish()
    grad_input, output = call(
        ends_kernel,
        [shaped((tok, width), F32), shaped((tok, width), BF16)],
        [hold(own_one, sum_last), tokens, grad_resid, norm_gain, own_out, resid],
        [near_both, last_both],
        (),
        [pltpu.VMEM((2 * tok, width), BF16)] * 2 + [dma(2)],
        micros=1.6,
    )

    feed_last = swap(hold(feed_far, sum_last), 1)
    feed_pieces = [sum_feed, feed_near, feed_far, feed_last]
    last_far, last_near = swap(sum_last, 2), swap(sum_last, 1)
    piece = width // dp_count
    table_here = head_total * bucket_count // dp_count
    if aligned:
        out_in, out_down = call(
            wide_feed_kernel,
            [shaped((rows_here, ff), F32), shaped((sp_count * ff_rows, width), F32)],
            [],
            [hold(feed_pieces[0], sum_last)] + feed_pieces[1:],
            [me],
            [pltpu.VMEM((sp_count * rows_here, 2 * width), BF16), dma(4)],
        micros=3,
    )
        last_pieces = [sum_last, last_near, last_far, swap(hold(last_far, out_in, grad_input), 1)]
        out_qkv, out_out, gains, shifts, tables = call(
            wide_last_kernel,
            [
                shaped((rows_here, 3 * width), F32),
                shaped((rows_here, width), F32),
                shaped((2, piece), F32),
                shaped((2, piece), F32),
                shaped((1, table_here), F32),
            ],
            [],
            last_pieces,
            [me],
            [pltpu.VMEM((sp_count * (rows_here + SMALL_ROWS), width), BF16), dma(4)],
        micros=2.3,
    )
        tables = tables[0]
    else:
        all_feed = stacked_sp(feed_pieces).astype(F32)
        out_down = all_feed[:, :, width:].reshape(sp_count * ff_rows, width)
        all_in = all_feed[:, :, :width].reshape(sp_count, rows_here, dp_count, ff_rows)
        out_in = jnp.moveaxis(all_in, 0, 2).reshape(rows_here, ff)
        all_last = stacked_sp([sum_last, last_near, last_far, swap(last_far, 1)]).astype(F32)
        all_qkv = all_last[:, :rows_here, : 3 * part].reshape(sp_count, rows_here, 3, part)
        out_qkv = jnp.moveaxis(all_qkv, 0, 2).reshape(rows_here, 3 * width)
        out_out = jnp.moveaxis(all_last[:, :rows_here, 3 * part :], 0, 1).reshape(rows_here, width)
        small_row = jnp.sum(all_last[:, rows_here:], axis=0)[0]
        gains = small_row[: 2 * piece].reshape(2, piece)
        shifts = small_row[2 * piece : 4 * piece].reshape(2, piece)
        tables = small_row[4 * piece : 4 * piece + table_here]
    return (output[None], grad_input[None], out_qkv, out_out, out_in, out_down, gains, shifts, tables)


def solution(mesh):
    in_specs = (
        P("dp", "sp", None),
        P("dp", None),
        P("dp", None),
        P("dp", None),
        P("dp", None),
        P(),
        P(),
        P(),
        P("dp", None),
        P(),
        P("dp", "sp", None),
    )
    out_specs = (
        P("dp", "sp", None),
        P("dp", "sp", None),
        P("dp", None),
        P("dp", None),
        P("dp", None),
        P("dp", None),
        P(None, "dp"),
        P(None, "dp"),
        P("dp"),
    )
    return jax.shard_map(
        on_device, mesh=mesh, in_specs=in_specs, out_specs=out_specs, check_vma=False
    )
```

```python
import functools

import jax
import jax.numpy as jnp
from jax import lax
from jax.experimental import pallas as pl
from jax.experimental.pallas import tpu as pltpu
from jax.sharding import PartitionSpec as P

BLOCK = 128
SMALL_ROWS = 16
NEG = -1e30
BF16 = jnp.bfloat16
F32 = jnp.float32
VMEM_LIMIT = 24 * 1024 * 1024
ROOT = 0.7978845608028654
CUBE = 0.044715


def dot(left, right, left_dim=1, right_dim=0):
    return lax.dot_general(
        left, right, (((left_dim,), (right_dim,)), ((), ())), preferred_element_type=F32
    )


def exact_dot(left, right, left_dim=1, right_dim=0):
    return lax.dot_general(
        left,
        right,
        (((left_dim,), (right_dim,)), ((), ())),
        precision=lax.Precision.HIGHEST,
        preferred_element_type=F32,
    )


def layer_norm(values):
    average = jnp.mean(values, axis=-1, keepdims=True)
    centred = values - average
    inverse = lax.rsqrt(jnp.mean(centred * centred, axis=-1, keepdims=True) + 1e-05)
    return centred * inverse, inverse


def norm_back(upstream, normed, inverse, gain):
    scaled = upstream * gain
    centre_term = jnp.mean(scaled, axis=-1, keepdims=True)
    slope_term = jnp.mean(scaled * normed, axis=-1, keepdims=True)
    return inverse * (scaled - centre_term - normed * slope_term)


def shaped(shape, dtype):
    return jax.ShapeDtypeStruct(tuple(shape), dtype)


def call(kernel, outs, args=(), hbm_args=(), smem_args=(), scratch=(), hbm_outs=(), micros=1):
    specs = [pl.BlockSpec(memory_space=pltpu.VMEM)] * len(args)
    specs += [pl.BlockSpec(memory_space=pltpu.HBM)] * len(hbm_args)
    specs += [pl.BlockSpec(memory_space=pltpu.SMEM)] * len(smem_args)
    out_specs = [pl.BlockSpec(memory_space=pltpu.VMEM)] * len(outs)
    out_specs += [pl.BlockSpec(memory_space=pltpu.HBM)] * len(hbm_outs)
    return pl.pallas_call(
        kernel,
        out_shape=(*outs, *hbm_outs),
        in_specs=specs,
        out_specs=tuple(out_specs),
        scratch_shapes=list(scratch),
        compiler_params=pltpu.CompilerParams(vmem_limit_bytes=VMEM_LIMIT),
        cost_estimate=pl.CostEstimate(flops=0, bytes_accessed=int(micros * 3.3e6), transcendentals=0),
    )(*args, *hbm_args, *smem_args)


def rank_at(position, count):
    position = lax.rem(position + 2 * count, count)
    return jnp.where(position < count // 2, 2 * position, 2 * (count - 1 - position) + 1)


def position_of(rank, count):
    return jnp.where(lax.rem(rank, 2) == 0, lax.div(rank, 2), count - 1 - lax.div(rank, 2))


def ring_pairs(count):
    order = list(range(0, count, 2)) + list(range(count - 1, 0, -2))
    forward = [(order[i], order[(i + 1) % count]) for i in range(count)]
    return forward, [(b, a) for a, b in forward]


def half_rows(rows):
    return rows // 2 // 16 * 16


def hold(value, *others):
    return lax.optimization_barrier((value, others))[0] if others else value


def halves(up, down):
    rows, columns = up.shape
    half = half_rows(rows)

    def kernel(up_ref, down_ref, upper_ref, lower_ref, sems):
        copies = [
            pltpu.make_async_copy(up_ref.at[:half, :], upper_ref, sems.at[0]),
            pltpu.make_async_copy(down_ref.at[half:, :], lower_ref, sems.at[1]),
        ]
        finish(start_all(copies))

    outs = [shaped((half, columns), up.dtype), shaped((rows - half, columns), up.dtype)]
    return call(kernel, outs, [], [up, down], scratch=[dma(2)])


class GatherRing:
    def __init__(self, shard, count):
        self.shard, self.count, self.at = shard, count, 0
        self.up = self.down = shard
        self.pieces, self.held = [shard], (shard, shard)

    def step(self, *others):
        self.at += 1
        if self.count != 8:
            if self.at == 1:
                self.up = self.down = lax.all_gather(self.shard, "dp", axis=0, tiled=True)
                self.pieces = [self.up]
            return
        forward, backward = ring_pairs(self.count)
        up, down = self.up, self.down
        if self.at == self.count // 2:
            up, down = halves(up, down)
        self.held = up, down
        up, down, *_ = lax.optimization_barrier((up, down, *others))
        self.up = lax.ppermute(up, "dp", forward)
        self.down = lax.ppermute(down, "dp", backward)
        self.pieces += [self.up, self.down]


def target_rows(parts, me_ref, count, step):
    at = position_of(me_ref[1], count)
    near, far = count // 2 - step, count // 2 + 1 - step
    middle = parts.shape[2] // 2
    left, right = slice(0, middle), slice(middle, 2 * middle)
    up = parts.at[rank_at(at + far, count), :, left], parts.at[rank_at(at + near, count), :, right]
    down = parts.at[rank_at(at - near, count), :, left], parts.at[rank_at(at - far, count), :, right]
    return up, down


def store_first(parts, me_ref, up_ref, down_ref):
    middle = parts.shape[2] // 2
    for target, (left, right) in zip((up_ref, down_ref), target_rows(parts, me_ref, parts.shape[0], 1)):
        target[:, :middle] = left[...]
        target[:, middle:] = right[...]


def ring_add_kernel(count, step, *refs):
    parts, up_ref, down_ref, me_ref = refs[:4]
    up_out, down_out, mine, up, down, sems = refs[4:]
    middle = parts.shape[2] // 2
    left, right = slice(0, middle), slice(middle, 2 * middle)
    (up_left, up_right), (down_left, down_right) = target_rows(parts, me_ref, count, step)
    last = step == count // 2
    copies = [
        pltpu.make_async_copy(up_ref.at[:, left if last else slice(None)], up.at[:, left if last else slice(None)], sems.at[0]),
        pltpu.make_async_copy(down_ref.at[:, right if last else slice(None)], down.at[:, right if last else slice(None)], sems.at[1]),
        pltpu.make_async_copy(up_left, mine.at[0, :, left], sems.at[2]),
        pltpu.make_async_copy(down_right, mine.at[1, :, right], sems.at[3]),
    ]
    if not last:
        copies.append(pltpu.make_async_copy(up_right, mine.at[0, :, right], sems.at[4]))
        copies.append(pltpu.make_async_copy(down_left, mine.at[1, :, left], sems.at[5]))
    finish(start_all(copies))
    up_lanes, down_lanes = (left, right) if last else (slice(None), slice(None))
    up_out[...] = (mine[0, :, up_lanes].astype(F32) + up[:, up_lanes].astype(F32)).astype(BF16)
    down_out[...] = (mine[1, :, down_lanes].astype(F32) + down[:, down_lanes].astype(F32)).astype(BF16)


def ring_total_kernel(count, parts, up_ref, down_ref, last_up_ref, last_down_ref, me_ref, out_ref, mine, first, last, sems):
    middle = parts.shape[2] // 2
    left, right = slice(0, middle), slice(middle, 2 * middle)
    copies = [
        pltpu.make_async_copy(parts.at[me_ref[1]], mine, sems.at[0]),
        pltpu.make_async_copy(down_ref.at[:, left], first.at[:, left], sems.at[1]),
        pltpu.make_async_copy(up_ref.at[:, right], first.at[:, right], sems.at[2]),
        pltpu.make_async_copy(last_up_ref, last.at[:, left], sems.at[3]),
        pltpu.make_async_copy(last_down_ref, last.at[:, right], sems.at[4]),
    ]
    finish(start_all(copies))
    total = mine[...].astype(F32) + first[...].astype(F32) + last[...].astype(F32)
    out_ref[...] = total.astype(BF16)


class ScatterRing:
    def __init__(self, parts, first, me, count):
        self.parts, self.me, self.count, self.at = parts, me, count, 0
        self.added = first

    def step(self, *others):
        self.at += 1
        if self.count != 8:
            return
        forward, backward = ring_pairs(self.count)
        rows, columns = self.parts.shape[1:]
        if self.at > 1:
            width = columns // 2 if self.at == self.count // 2 else columns
            self.before = self.up, self.down
            self.added = call(
                functools.partial(ring_add_kernel, self.count, self.at),
                [shaped((rows, width), BF16)] * 2,
                [],
                [self.parts, hold(self.up, *others), self.down],
                [self.me],
                [pltpu.VMEM((2, rows, columns), BF16)] + [pltpu.VMEM((rows, columns), BF16)] * 2 + [dma(6)],
            )
        up, down = self.added
        self.up = lax.ppermute(up, "dp", forward)
        self.down = lax.ppermute(down, "dp", backward)

    def sent(self):
        return (self.up, self.down) if self.count == 8 else ()

    def sums(self):
        return tuple(self.added) if self.count == 8 else ()

    def finish(self, *others):
        if self.count != 8:
            return lax.psum_scatter(self.parts, "dp", scatter_dimension=0)
        rows, columns = self.parts.shape[1:]
        return call(
            functools.partial(ring_total_kernel, self.count),
            [shaped((rows, columns), BF16)],
            [],
            [self.parts, *self.before, hold(self.up, *others), self.down],
            [self.me],
            [pltpu.VMEM((rows, columns), BF16)] * 3 + [dma(5)],
        )[0]


def swap(values, bit):
    count = lax.axis_size("sp")
    return lax.ppermute(values, "sp", [(i, i ^ bit) for i in range(count)])


def gather_sp(piece):
    far = swap(piece, 2)
    near = swap(piece, 1)
    return [piece, near, far, swap(far, 1)]


def far_kernel(far_ref, near_ref, out_ref, near, sems):
    finish(start_all([pltpu.make_async_copy(near_ref.at[far_ref.shape[0] :, :], near, sems.at[0])]))
    out_ref[...] = (far_ref[...] + near[...].astype(F32)).astype(BF16)


def add_far(far, near):
    return call(
        far_kernel,
        [shaped(far.shape, BF16)],
        [far],
        [near],
        (),
        [pltpu.VMEM(far.shape, BF16), dma(1)],
    )[0]


def exchange_sp(sends):
    return [swap(send, step) for step, send in enumerate(sends, 1)]


def place(step, size, me_ref):
    return pl.multiple_of((me_ref[0] ^ step) * size, size)


def in_hbm(pieces):
    return [pltpu.with_memory_space_constraint(piece, pltpu.HBM) for piece in pieces]


def start_all(copies):
    for copy in copies:
        copy.start()
    return copies


def finish(copies):
    for copy in copies:
        copy.wait()


def load(pieces, me_ref, count, target, sems, lanes=slice(None)):
    if len(pieces) == 1:
        starts = [0]
    else:
        at = position_of(me_ref[1], count)
        rows = pieces[0].shape[0]
        starts = [rank_at(at + step, count) * rows for step in (0, -1, 1, -2, 2, -3, 3, 4)]
        starts.append(starts[-1] + half_rows(rows))
    copies = []
    for at, (start, piece) in enumerate(zip(starts, pieces)):
        rows = pl.ds(pl.multiple_of(start, 16), piece.shape[0])
        copies.append(pltpu.make_async_copy(piece.at[:, lanes], target.at[rows, :], sems.at[at]))
    return start_all(copies)


def load_rows(pieces, target, sems, me_ref=None, rows=slice(None), lanes=slice(None)):
    copies = []
    for step, piece in enumerate(pieces):
        block = piece.at[rows, lanes]
        size = block.shape[0]
        start = step * size if me_ref is None else place(step, size, me_ref)
        copies.append(pltpu.make_async_copy(block, target.at[pl.ds(start, size), :], sems.at[step]))
    return start_all(copies)


def dma(count):
    return pltpu.SemaphoreType.DMA((count,))


def share(sources, me, plan, rows):
    columns = sum(size for _, _, size, _ in plan)

    def kernel(*refs):
        *inputs, me_ref, target, sems = refs
        copies = []
        for at, (source, start, size, to) in enumerate(plan):
            if start is None:
                block = inputs[source].at[pl.ds(place(0, rows, me_ref), rows), :]
            else:
                block = inputs[source].at[:, pl.ds(start + place(0, size, me_ref), size)]
            copies.append(pltpu.make_async_copy(block, target.at[:, to : to + size], sems.at[at]))
        finish(start_all(copies))

    return call(
        kernel,
        [pltpu.VMEM((rows, columns), BF16)],
        [],
        [pltpu.with_memory_space_constraint(source, pltpu.HBM) for source in sources],
        [me],
        [dma(len(plan))],
    )[0]


def padded(bucket_ref):
    return jnp.concatenate([jnp.full((1, BLOCK), -1, jnp.int32), bucket_ref[...]], axis=1)


def bias_kernel(table_ref, bucket_ref, seg_ref, me_ref, bias_ref, mask_ref):
    heads, diagonals = bias_ref.shape[:2]
    buckets = padded(bucket_ref)
    bucket = lax.broadcasted_iota(jnp.int32, (table_ref.shape[1], buckets.shape[1]), 0)
    chosen = (bucket == buckets).astype(F32)
    rows = exact_dot(table_ref[...], chosen)
    row = lax.broadcasted_iota(jnp.int32, rows.shape, 0)
    for head in range(heads):
        mine = jnp.sum(jnp.where(row == me_ref[0] * heads + head, rows, 0.0), axis=0, keepdims=True)
        for diagonal in range(diagonals):
            part = mine[:, diagonal * BLOCK : (diagonal + 2) * BLOCK]
            spread = jnp.broadcast_to(part, (BLOCK, 2 * BLOCK))
            rolled = pltpu.roll(spread, BLOCK, 1, stride=1, stride_axis=0)
            bias_ref[head, diagonal] = rolled[:, :BLOCK]
    segments = seg_ref[...].astype(F32)
    key = lax.broadcasted_iota(jnp.int32, (BLOCK, BLOCK), 0)
    query = lax.broadcasted_iota(jnp.int32, (BLOCK, BLOCK), 1)
    for block in range(diagonals):
        rows = slice(block * BLOCK, (block + 1) * BLOCK)
        keys = jnp.broadcast_to(segments[:, rows], (BLOCK, BLOCK)).T
        for index in range(block, diagonals):
            same = keys == segments[:, index * BLOCK : (index + 1) * BLOCK]
            if index == block:
                same = same & (query >= key)
            mask_ref[index, rows, :] = jnp.where(same, 0.0, NEG).astype(F32)


def norm_kernel(*refs):
    pieces, (gain_ref, shift_ref), me_ref = refs[2:6], refs[:2], refs[6]
    act_ref, normed_ref, up_ref, tokens, sems, up_sems = refs[7:]
    tok = up_ref.shape[0] // 4
    copies = load_rows(pieces, tokens, sems, me_ref, slice(0, tok))
    up_copies = load_rows(pieces, up_ref, up_sems, None, slice(tok, 2 * tok))
    finish(copies)
    for start in range(0, tokens.shape[0], BLOCK):
        rows = slice(start, start + BLOCK)
        normed, _ = layer_norm(tokens[rows, :].astype(F32))
        act_ref[rows, :] = (normed * gain_ref[0:1, :] + shift_ref[0:1, :]).astype(BF16)
        normed_ref[rows, :] = normed.astype(BF16)
    finish(up_copies)


def split_heads(rows):
    lane = lax.broadcasted_iota(jnp.int32, (1, BLOCK), 1)
    low = (lane < BLOCK // 2).astype(F32).astype(BF16)
    return jnp.concatenate([rows * low, rows * (1 - low)], axis=0)


def join_heads(both):
    half = BLOCK // 2
    return jnp.concatenate([both[:half, :BLOCK], both[half:, BLOCK:]], axis=0).T


def score_block(raw, bias_ref, mask_ref, pair, index, block):
    rows = slice(block * BLOCK, (block + 1) * BLOCK)
    mask = mask_ref[index, rows, :]
    return jnp.concatenate(
        [
            raw[rows, side * BLOCK : (side + 1) * BLOCK] + bias_ref[2 * pair + side, index - block] + mask
            for side in range(2)
        ],
        axis=1,
    )


def attend_kernel(scale, parts, count, *refs):
    act_ref, bias_ref, mask_ref = refs[:3]
    pieces, me_ref = refs[3 : 3 + count], refs[3 + count]
    qkv_ref, attn_ref, log_ref, weight, sems = refs[4 + count :]
    columns = attn_ref.shape[1]
    copies = load(pieces, me_ref, parts, weight, sems, slice(0, 3 * columns))
    finish(copies)
    for start in range(0, 3 * columns, columns):
        lanes = slice(start, start + columns)
        qkv_ref[:, lanes] = dot(act_ref[...], weight[:, lanes]).astype(BF16)
    for index in range(qkv_ref.shape[0] // BLOCK):
        rows = slice(index * BLOCK, (index + 1) * BLOCK)
        width = (index + 1) * BLOCK
        for pair in range(columns // BLOCK):
            lanes = slice(pair * BLOCK, (pair + 1) * BLOCK)
            queries = split_heads(qkv_ref[rows, lanes] * scale)
            keys = qkv_ref[:width, columns + pair * BLOCK : columns + (pair + 1) * BLOCK]
            values = qkv_ref[:width, 2 * columns + pair * BLOCK : 2 * columns + (pair + 1) * BLOCK]
            raw = dot(keys, queries, 1, 1)
            scores = [score_block(raw, bias_ref, mask_ref, pair, index, block) for block in range(index + 1)]
            largest = functools.reduce(
                jnp.maximum, [jnp.max(score, axis=0, keepdims=True) for score in scores]
            )
            weights = [jnp.exp(score - largest) for score in scores]
            total = functools.reduce(jnp.add, [jnp.sum(one, axis=0, keepdims=True) for one in weights])
            mixed = dot(values, jnp.concatenate([one.astype(BF16) for one in weights], axis=0), 0, 0)
            attn_ref[rows, lanes] = join_heads(mixed / total).astype(BF16)
            at = index * (columns // BLOCK) + pair
            log_ref[at : at + 1, :] = largest + jnp.log(total)


def branch_kernel(*refs):
    tokens_ref, gain_ref, shift_ref, attn_refs, weight_refs, me_ref = (*refs[:3], refs[3:7], refs[7:11], refs[11])
    resid_ref, act_ref, weight, own, sems, weight_sems = refs[12:]
    tok = tokens_ref.shape[0]
    part = weight_refs[0].shape[1]
    copies = []
    for step in range(4):
        columns = pl.ds(place(step, part, me_ref), part)
        rows = pl.ds(place(0, tok, me_ref), tok)
        copies.append(pltpu.make_async_copy(attn_refs[step].at[rows, :], own.at[:, columns], sems.at[step]))
        copies.append(pltpu.make_async_copy(weight_refs[step], weight.at[:, columns], weight_sems.at[step]))
    finish(start_all(copies))
    resid = tokens_ref[...].astype(F32) + dot(own[...], weight[...])
    resid_ref[...] = resid
    normed, _ = layer_norm(resid)
    act_ref[...] = (normed * gain_ref[1:2, :] + shift_ref[1:2, :]).astype(BF16)


def outer(left, right, grad_ref):
    parts, rows_here, _ = grad_ref.shape
    for start in range(0, parts * rows_here, 2 * BLOCK):
        block = dot(left[:, start : start + 2 * BLOCK], right[...], 0, 0).astype(BF16)
        for sub in range(2 * BLOCK // rows_here):
            grad_ref[start // rows_here + sub] = block[sub * rows_here : (sub + 1) * rows_here]


def feed_kernel(parts, count, *refs):
    up_from, act_refs, pieces, me_ref = refs[0], refs[1:5], refs[5 : 5 + count], refs[5 + count]
    grad_ref, up_first, down_first, own_ref, far_ref, send_ref, fed_ref = refs[6 + count : 13 + count]
    act, up_ref, weight, down, slope, hidden, act_sems, up_sems, sems, down_sems = refs[13 + count :]
    tok = own_ref.shape[0]
    width = weight.shape[1]
    copies = load(pieces, me_ref, parts, weight, sems, slice(0, width)) + load_rows(act_refs, act, act_sems)
    finish(copies)
    late = load(pieces, me_ref, parts, down, down_sems, slice(width, None))
    late += start_all([pltpu.make_async_copy(up_from, up_ref, up_sems.at[0])])
    for start in range(0, width, 2 * BLOCK):
        columns = slice(start, start + 2 * BLOCK)
        units = dot(act[...], weight[:, columns])
        square = units * units
        bend = jnp.tanh(ROOT * units * (1.0 + CUBE * square))
        fed_ref[:, columns] = (0.5 * units * (1.0 + bend)).astype(BF16)
        slope[:, columns] = 0.5 * (1.0 + bend) + 0.5 * units * (1.0 - bend * bend) * ROOT * (
            1.0 + 3.0 * CUBE * square
        )
    finish(late)
    for start in range(0, width, 2 * BLOCK):
        rows = slice(start, start + 2 * BLOCK)
        hidden[:, rows] = (dot(up_ref[...], down[rows, :], 1, 1) * slope[:, rows]).astype(BF16)
    for start in range(0, weight.shape[0], 2 * BLOCK):
        rows = slice(start, start + 2 * BLOCK)
        share_of = dot(hidden[...], weight[rows, :], 1, 1)
        own_ref[:, rows] = share_of[:tok]
        far_ref[:, rows] = share_of[2 * tok : 3 * tok]
        send_ref[:tok, rows] = share_of[tok : 2 * tok].astype(BF16)
        send_ref[tok:, rows] = share_of[3 * tok :].astype(BF16)
    rows_here = grad_ref.shape[1]
    for at, (left, right) in enumerate([(act, hidden), (fed_ref, up_ref)]):
        lanes = slice(at * width, (at + 1) * width)
        for start in range(0, parts * rows_here, 2 * BLOCK):
            block = dot(left[:, start : start + 2 * BLOCK], right[...], 0, 0).astype(BF16)
            for sub in range(2 * BLOCK // rows_here):
                grad_ref[start // rows_here + sub, :, lanes] = block[sub * rows_here : (sub + 1) * rows_here]
    if parts == 8:
        store_first(grad_ref, me_ref, up_first, down_first)


def branch_back_kernel(*refs):
    own_ref, resid_ref, up_ref, gain_ref, near_ref, far_ref, weight_refs, me_ref = (*refs[:6], refs[6:10], refs[10])
    grad_ref, sums_ref, *send_refs, branch, grad_attn, near, far, weight, sems, weight_sems = refs[11:]
    tok = up_ref.shape[0]
    part = send_refs[0].shape[1] // 2
    copies = start_all(
        [
            pltpu.make_async_copy(near_ref.at[:tok, :], near, sems.at[0]),
            pltpu.make_async_copy(far_ref, far, sems.at[1]),
        ]
    )
    late = []
    for step in range(4):
        columns = pl.ds(place(step, part, me_ref), part)
        late.append(pltpu.make_async_copy(weight_refs[step], weight.at[:, columns], weight_sems.at[step]))
    start_all(late)
    normed, inverse = layer_norm(resid_ref[...])
    finish(copies)
    upstream = own_ref[...] + near[...].astype(F32) + far[...].astype(F32)
    sums_ref[0:1, :] = jnp.sum(upstream * normed, axis=0, keepdims=True)
    sums_ref[1:2, :] = jnp.sum(upstream, axis=0, keepdims=True)
    sums_ref[2:, :] = jnp.zeros_like(sums_ref[2:, :])
    grad = up_ref[...].astype(F32) + norm_back(upstream, normed, inverse, gain_ref[1:2, :])
    grad_ref[...] = grad
    branch[...] = grad.astype(BF16)
    finish(late)
    grad_attn[...] = dot(branch[...], weight[...], 1, 1).astype(BF16)
    for step, send in enumerate(send_refs):
        columns = pl.ds(place(step, part, me_ref), part)
        send[:, :part] = grad_attn[:, columns]
        send[:, part:] = branch[:, columns]


def attend_back_kernel(scale, dp_count, count, rest_count, *refs):
    qkv_ref, log_ref, bias_ref, mask_ref, act_ref, normed_ref, sums_ref, bucket_ref = refs[:8]
    fed_from, attn_refs, grad_refs, pieces = refs[8], refs[9:13], refs[13:17], refs[17 : 17 + count]
    down_refs, me_ref, refs = refs[17 + count : 17 + count + rest_count], refs[17 + count + rest_count], refs[18 + count + rest_count :]
    last_ref, up_first, down_first, small_ref, own_ref, own_out_ref, far_ref, send_ref = refs[:8]
    grads, branch, attn, grad_qkv, key_acc, value_acc, diagonal_acc, stacked, rolled, rolled_high, shares, weight_ref, fed_ref, down = refs[
        8:22
    ]
    grad_sems, branch_sems, attn_sems, sems, fed_sems, down_sems = refs[22:]
    seq_len = qkv_ref.shape[0]
    columns = qkv_ref.shape[1] // 3
    heads, diagonals = bias_ref.shape[:2]
    tok = own_ref.shape[0]
    copies = load_rows(grad_refs, grads, grad_sems, me_ref, lanes=slice(0, columns))
    late = load_rows(grad_refs, branch, branch_sems, me_ref, lanes=slice(columns, 2 * columns))
    late += load_rows(attn_refs, attn, attn_sems)
    late += load(pieces, me_ref, dp_count, weight_ref, sems, slice(0, 3 * columns))
    late += load(down_refs, me_ref, dp_count, down, down_sems, slice(act_ref.shape[1], None))
    late += start_all([pltpu.make_async_copy(fed_from, fed_ref, fed_sems.at[0])])
    key_acc[...] = jnp.zeros_like(key_acc)
    value_acc[...] = jnp.zeros_like(value_acc)
    diagonal_acc[...] = jnp.zeros_like(diagonal_acc)
    finish(copies)
    for pair in range(columns // BLOCK):
        lanes = slice(pair * BLOCK, (pair + 1) * BLOCK)
        all_keys = qkv_ref[:, columns + pair * BLOCK : columns + (pair + 1) * BLOCK]
        for index in range(seq_len // BLOCK):
            rows = slice(index * BLOCK, (index + 1) * BLOCK)
            width = (index + 1) * BLOCK
            queries = split_heads(qkv_ref[rows, lanes] * scale)
            grad_rows = split_heads(grads[rows, lanes])
            keys = all_keys[:width]
            values = qkv_ref[:width, 2 * columns + pair * BLOCK : 2 * columns + (pair + 1) * BLOCK]
            at = index * (columns // BLOCK) + pair
            logs = log_ref[at : at + 1, :]
            raw = dot(keys, queries, 1, 1)
            grad_probs = dot(values, grad_rows, 1, 1)
            probs = [
                jnp.exp(score_block(raw, bias_ref, mask_ref, pair, index, block) - logs)
                for block in range(index + 1)
            ]
            products = [
                one * grad_probs[block * BLOCK : (block + 1) * BLOCK] for block, one in enumerate(probs)
            ]
            row_term = functools.reduce(jnp.add, [jnp.sum(one, axis=0, keepdims=True) for one in products])
            grad_scores = [product - one * row_term for product, one in zip(products, probs)]
            for block, one in enumerate(grad_scores):
                diagonal_acc[pair, index - block] += one
            grad_raw = jnp.concatenate([one.astype(BF16) for one in grad_scores], axis=0)
            probs_all = jnp.concatenate([one.astype(BF16) for one in probs], axis=0)
            grad_qkv[rows, lanes] = (join_heads(dot(keys, grad_raw, 0, 0)) * scale).astype(BF16)
            key_acc[:width, lanes] += dot(grad_raw, queries)
            value_acc[:width, lanes] += dot(probs_all, grad_rows)
    grad_qkv[:, columns : 2 * columns] = key_acc[...].astype(BF16)
    grad_qkv[:, 2 * columns :] = value_acc[...].astype(BF16)

    parts, last_rows = last_ref.shape[:2]
    width = act_ref.shape[1]
    rows_here = width // parts
    for start in range(0, width, 2 * BLOCK):
        block = dot(act_ref[:, start : start + 2 * BLOCK], grad_qkv[...], 0, 0).astype(BF16)
        for sub in range(2 * BLOCK // rows_here):
            last_ref[start // rows_here + sub, :rows_here, : 3 * columns] = block[
                sub * rows_here : (sub + 1) * rows_here
            ]
    finish(late)
    for step in range(4):
        block = dot(attn[step * seq_len : (step + 1) * seq_len, :], branch[...], 0, 0).astype(BF16)
        for sub in range(columns // rows_here):
            part = (me_ref[0] ^ step) * (columns // rows_here) + sub
            last_ref[part, :rows_here, 3 * columns :] = block[sub * rows_here : (sub + 1) * rows_here]

    for start in range(0, width, 2 * BLOCK):
        lanes = slice(start, start + 2 * BLOCK)
        share_of = dot(grad_qkv[...], weight_ref[lanes, :], 1, 1)
        small_ref[0:1, lanes] = jnp.sum(share_of * normed_ref[:, lanes].astype(F32), axis=0, keepdims=True)
        small_ref[2:3, lanes] = jnp.sum(share_of, axis=0, keepdims=True)
        shares[:, lanes] = share_of
    for start in range(0, width, 2 * BLOCK):
        lanes = slice(start, start + 2 * BLOCK)
        share_of = dot(fed_ref[...], down[:, lanes])
        own_out_ref[:, lanes] = share_of[:tok]
        send_ref[tok : 2 * tok, lanes] = share_of[tok : 2 * tok].astype(BF16)
        far_ref[tok:, lanes] = share_of[2 * tok : 3 * tok].astype(BF16)
        send_ref[3 * tok :, lanes] = share_of[3 * tok :].astype(BF16)
    for step, (target, to) in enumerate([(own_ref, 0), (send_ref, 0), (far_ref, 0), (send_ref, 2 * tok)]):
        rows = pl.ds(place(step, tok, me_ref), tok)
        target[to : to + tok, :] = shares[rows, :].astype(target.dtype)
    small_ref[1:2, :] = sums_ref[0:1, :]
    small_ref[3:4, :] = sums_ref[1:2, :]

    for pair in range(heads // 2):
        for diagonal in range(diagonals):
            for side in range(2):
                total = jnp.zeros((8, 2 * BLOCK), F32)
                for start in range(0, BLOCK, 8):
                    some = diagonal_acc[pair, diagonal, start : start + 8, side * BLOCK : (side + 1) * BLOCK]
                    wide = jnp.concatenate([some, jnp.zeros_like(some)], axis=1)
                    total += wide if start == 0 else pltpu.roll(wide, 2 * BLOCK - start, 1)
                at = ((2 * pair + side) * diagonals + diagonal) * 8
                rolled[at : at + 8, :] = total[:, :BLOCK]
                rolled_high[at : at + 8, :] = total[:, BLOCK:]
    turned = jnp.zeros((heads * diagonals, 2 * BLOCK), F32)
    for start in range(8):
        rows = pl.ds(start, heads * diagonals, stride=8)
        both = jnp.concatenate([rolled[rows, :], rolled_high[rows, :]], axis=1)
        turned += pltpu.roll(both, BLOCK - start, 1)
    stacked[...] = jnp.zeros_like(stacked)
    for head in range(heads):
        for diagonal in range(diagonals):
            at = head * diagonals + diagonal
            stacked[head : head + 1, diagonal * BLOCK : (diagonal + 2) * BLOCK] += turned[at : at + 1, :]
    buckets = BLOCK // heads
    distances = padded(bucket_ref)
    bucket = lax.rem(lax.broadcasted_iota(jnp.int32, (BLOCK, distances.shape[1]), 0), buckets)
    chosen = (bucket == distances).astype(F32)
    by_head = exact_dot(stacked[...], chosen, 1, 1)
    row = lax.broadcasted_iota(jnp.int32, by_head.shape, 0)
    column = lax.broadcasted_iota(jnp.int32, by_head.shape, 1)
    table = jnp.sum(jnp.where(lax.div(column, buckets) == row, by_head, 0.0), axis=0, keepdims=True)
    small_ref[4:5, :BLOCK] = table
    if last_rows > rows_here:
        last_ref[:, rows_here:, :] = jnp.zeros_like(last_ref[:, rows_here:, :])
        per = parts // 4
        for part in range(parts):
            for at in range(4):
                last_ref[part, rows_here : rows_here + 1, at * rows_here : (at + 1) * rows_here] = small_ref[
                    at : at + 1, part * rows_here : (part + 1) * rows_here
                ].astype(BF16)
            turned = table if part % per == 0 else pltpu.roll(table, BLOCK - part % per * (BLOCK // per), 1)
            turned = jnp.where(me_ref[0] == part // per, turned, 0.0)
            last_ref[part, rows_here : rows_here + 1, 4 * rows_here : 4 * rows_here + BLOCK] = turned.astype(BF16)
    if parts == 8:
        store_first(last_ref, me_ref, up_first, down_first)


def ends_kernel(own_ref, tokens_ref, grad_resid_ref, gain_ref, own_out_ref, resid_ref, *refs):
    near_ref, far_ref, grad_ref, out_ref, near, far, sems = refs
    copies = start_all(
        [
            pltpu.make_async_copy(near_ref.at[: near.shape[0], :], near, sems.at[0]),
            pltpu.make_async_copy(far_ref, far, sems.at[1]),
        ]
    )
    tok = own_ref.shape[0]
    normed, inverse = layer_norm(tokens_ref[...].astype(F32))
    finish(copies)
    upstream = own_ref[...] + near[:tok, :].astype(F32) + far[:tok, :].astype(F32)
    grad_ref[...] = grad_resid_ref[...] + norm_back(upstream, normed, inverse, gain_ref[0:1, :])
    total = resid_ref[...] + own_out_ref[...] + near[tok:, :].astype(F32) + far[tok:, :].astype(F32)
    out_ref[...] = total.astype(BF16)


def wide_feed_kernel(*refs):
    pieces, me_ref, in_ref, down_ref, both, sems = refs[:4], refs[4], refs[5], refs[6], refs[7], refs[8]
    finish(load_rows(pieces, both, sems))
    rows = in_ref.shape[0]
    width = down_ref.shape[1]
    for step in range(4):
        mine = slice(step * rows, (step + 1) * rows)
        down_ref[pl.ds(place(step, rows, me_ref), rows), :] = both[mine, width:].astype(F32)
        for start in range(0, width, rows):
            at = pl.multiple_of(4 * start + (me_ref[0] ^ step) * rows, rows)
            in_ref[:, pl.ds(at, rows)] = both[mine, start : start + rows].astype(F32)


def wide_last_kernel(*refs):
    pieces, me_ref = refs[:4], refs[4]
    qkv_ref, out_ref, gain_ref, shift_ref, table_ref, last, sems = refs[5:]
    finish(load_rows(pieces, last, sems))
    rows, width = out_ref.shape
    part = width // 4
    whole = rows + SMALL_ROWS
    small = jnp.zeros((1, width), F32)
    for step in range(4):
        start = step * whole
        mine = slice(start, start + rows)
        for third in range(3):
            at = pl.multiple_of(third * width + (me_ref[0] ^ step) * part, part)
            qkv_ref[:, pl.ds(at, part)] = last[mine, third * part : (third + 1) * part].astype(F32)
        out_ref[:, pl.ds(place(step, part, me_ref), part)] = last[mine, 3 * part :].astype(F32)
        small += last[start + rows : start + whole, :].astype(F32)[0:1]
    for at in range(2):
        gain_ref[at : at + 1, :] = small[:, at * rows : (at + 1) * rows]
        shift_ref[at : at + 1, :] = small[:, (2 + at) * rows : (3 + at) * rows]
    table_ref[...] = small[:, 4 * rows : 4 * rows + table_ref.shape[1]]


def stacked_sp(pieces):
    me = lax.axis_index("sp")
    whole = jnp.zeros((len(pieces),) + pieces[0].shape, pieces[0].dtype)
    for step, piece in enumerate(pieces):
        whole = lax.dynamic_update_index_in_dim(whole, piece, me ^ step, 0)
    return whole


def on_device(
    inputs,
    qkv_weight,
    out_weight,
    in_weight,
    down_weight,
    norm_gain,
    norm_shift,
    bias_table,
    segment_ids,
    bucket_index,
    cotangent,
):
    dp_count, sp_count = lax.axis_size("dp"), lax.axis_size("sp")
    me_sp = lax.axis_index("sp")
    me = jnp.stack([me_sp, lax.axis_index("dp")]).astype(jnp.int32)
    tok, width = inputs.shape[1:]
    head_total, bucket_count = bias_table.shape
    heads = head_total // sp_count
    scale = (width // head_total) ** (-0.5)
    seq_len = segment_ids.shape[1]
    rows_here = qkv_weight.shape[0]
    ff = in_weight.shape[1]
    ff_rows = ff // dp_count // sp_count
    ff_part = ff // sp_count
    part = width // sp_count
    diagonals = seq_len // BLOCK
    aligned = ff_rows % BLOCK == 0 and rows_here % BLOCK == 0

    if aligned:
        plan = [(0, third * width, part, third * part) for third in range(3)] + [(1, 0, part, 3 * part)]
        first_part = share([qkv_weight, out_weight], me, plan, rows_here)
        step = sp_count * ff_rows
        plan = [(0, index * step, ff_rows, index * ff_rows) for index in range(dp_count)]
        plan.append((1, None, width, ff_part))
        rest_part = share([hold(in_weight, first_part), down_weight], me, plan, rows_here)
    else:

        def own_sp(stacked, axis):
            return lax.dynamic_index_in_dim(stacked, me_sp, axis, keepdims=False)

        first_part = own_sp(qkv_weight.reshape(rows_here, 3, sp_count, part), 2).reshape(rows_here, 3 * part)
        out_part = own_sp(out_weight.reshape(rows_here, sp_count, part), 1)
        first_part = jnp.concatenate([first_part, out_part], axis=1)
        in_part = own_sp(in_weight.reshape(rows_here, dp_count, sp_count, ff_rows), 2)
        in_part = in_part.reshape(rows_here, ff_part)
        down_part = lax.dynamic_slice_in_dim(down_weight, me_sp * ff_rows, ff_rows, 0)
        rest_part = jnp.concatenate([in_part, down_part], axis=1)
    first_ring = GatherRing(first_part, dp_count)
    rest_ring = GatherRing(rest_part, dp_count)

    tokens = inputs[0]
    first_ring.step()

    buckets = bucket_index[None]
    bias, mask = call(
        bias_kernel,
        [shaped((heads, diagonals, BLOCK, BLOCK), F32), shaped((diagonals, seq_len, BLOCK), F32)],
        [bias_table, hold(buckets, first_part), segment_ids],
        (),
        [me],
        micros=1.2,
    )
    both = jnp.concatenate([hold(tokens, first_part), cotangent[0]], axis=0)
    token_far, token_near = swap(both, 2), swap(both, 1)
    first_ring.step(bias, rest_part)
    token_last = swap(token_far, 1)
    first_ring.step(token_far)
    act_one, normed_one, up_all = call(
        norm_kernel,
        [shaped((seq_len, width), BF16)] * 3,
        [hold(norm_gain, *first_ring.held), norm_shift],
        [both, token_near, token_far, token_last],
        [me],
        [pltpu.VMEM((seq_len, width), BF16), dma(4), dma(4)],
        micros=2.4,
    )
    first_ring.step()
    rest_ring.step(first_ring.up, first_ring.down)
    first_pieces = first_ring.pieces
    count = len(first_pieces)
    if count == 1:
        out_columns = first_pieces[0][:, 3 * part :]
    else:

        def assemble(*refs):
            *pieces, me_ref, target, sems = refs
            finish(load(pieces, me_ref, dp_count, target, sems, slice(3 * part, 4 * part)))

        (out_columns,) = call(
            assemble, [], [], first_pieces, [me], [dma(count)], [shaped((width, part), BF16)]
        )
    out_far, out_near = swap(out_columns, 2), swap(out_columns, 1)
    pairs = heads // 2
    qkv, attn, logs = call(
        functools.partial(attend_kernel, scale, dp_count, count),
        [
            shaped((seq_len, 3 * part), BF16),
            shaped((seq_len, part), BF16),
            shaped((diagonals * pairs, 2 * BLOCK), F32),
        ],
        [hold(act_one, out_columns), bias, mask],
        first_pieces,
        [me],
        [pltpu.VMEM((width, 3 * part), BF16), dma(count)],
        micros=5,
    )
    attn = hold(attn, rest_ring.up, rest_ring.down)
    attn_far, attn_near = swap(attn, 2), swap(attn, 1)
    rest_ring.step(attn)
    attn_last = swap(attn_far, 1)
    out_last = swap(out_far, 1)
    resid, act_two = call(
        branch_kernel,
        [shaped((tok, width), F32), shaped((tok, width), BF16)],
        [tokens, norm_gain, norm_shift],
        [attn, attn_near, attn_far, attn_last, out_columns, out_near, out_far, out_last],
        [me],
        [pltpu.VMEM((width, width), BF16), pltpu.VMEM((tok, width), BF16), dma(4), dma(4)],
        micros=2.4,
    )
    act_two = hold(act_two, rest_ring.up, rest_ring.down)
    act_far, act_near = swap(act_two, 2), swap(act_two, 1)
    rest_ring.step(act_two)
    act_last = swap(act_far, 1)
    rest_ring.step(act_last)
    grad_feed, up_first, down_first, own_two, far_two, send_two, fed = call(
        functools.partial(feed_kernel, dp_count, count),
        [shaped((dp_count, rows_here, 2 * width), BF16)] + [shaped((rows_here, 2 * width), BF16)] * 2
        + [shaped((tok, width), F32)] * 2
        + [shaped((2 * tok, width), BF16), shaped((seq_len, ff_part), BF16)],
        [],
        in_hbm([up_all, act_two, act_near, act_far, act_last, *rest_ring.pieces]),
        [me],
        [
            pltpu.VMEM((seq_len, width), BF16),
            pltpu.VMEM((seq_len, width), BF16),
            pltpu.VMEM((width, ff_part), BF16),
            pltpu.VMEM((ff_part, width), BF16),
            pltpu.VMEM((seq_len, ff_part), F32),
            pltpu.VMEM((seq_len, ff_part), BF16),
            dma(4),
            dma(1),
            dma(count),
            dma(count),
        ],
        micros=9,
    )

    near_two = swap(send_two, 1)
    last_two = swap(add_far(far_two, near_two), 2)
    feed_grads = ScatterRing(grad_feed, (up_first, down_first), me, dp_count)
    feed_grads.step()
    feed_grads.step(last_two)
    grad_resid, sums_two, *sends = call(
        branch_back_kernel,
        [shaped((tok, width), F32), shaped((8, width), F32)] + [shaped((tok, 2 * part), BF16)] * 4,
        [hold(own_two, *feed_grads.sums()), resid, cotangent[0], norm_gain],
        [near_two, last_two, out_columns, out_near, out_far, out_last],
        [me],
        [
            *[pltpu.VMEM((tok, width), BF16)] * 4,
            pltpu.VMEM((width, width), BF16),
            dma(2),
            dma(4),
        ],
        micros=2.5,
    )
    grad_pieces = [sends[0]] + exchange_sp(sends[1:])
    feed_grads.step(*grad_pieces[1:])
    last_rows = rows_here + SMALL_ROWS if aligned else rows_here
    last, up_first, down_first, small, own_one, own_out, far_both, send_both = call(
        functools.partial(attend_back_kernel, scale, dp_count, count, len(rest_ring.pieces)),
        [shaped((dp_count, last_rows, 4 * part), BF16)] + [shaped((last_rows, 4 * part), BF16)] * 2
        + [shaped((8, width), F32)]
        + [shaped((tok, width), F32)] * 2
        + [shaped((2 * tok, width), BF16), shaped((4 * tok, width), BF16)],
        [hold(qkv, *feed_grads.sums()), logs, bias, mask, act_one, normed_one, sums_two, buckets],
        [fed, attn, attn_near, attn_far, attn_last, *grad_pieces, *first_pieces, *in_hbm(rest_ring.pieces)],
        [me],
        [
            pltpu.VMEM((seq_len, part), BF16),
            pltpu.VMEM((seq_len, part), BF16),
            pltpu.VMEM((4 * seq_len, part), BF16),
            pltpu.VMEM((seq_len, 3 * part), BF16),
            pltpu.VMEM((seq_len, part), F32),
            pltpu.VMEM((seq_len, part), F32),
            pltpu.VMEM((pairs, diagonals, BLOCK, 2 * BLOCK), F32),
            pltpu.VMEM((heads, seq_len + BLOCK), F32),
            pltpu.VMEM((8 * heads * diagonals, BLOCK), F32),
            pltpu.VMEM((8 * heads * diagonals, BLOCK), F32),
            pltpu.VMEM((seq_len, width), F32),
            pltpu.VMEM((width, 3 * part), BF16),
            pltpu.VMEM((seq_len, ff_part), BF16),
            pltpu.VMEM((ff_part, width), BF16),
            dma(4),
            dma(4),
            dma(4),
            dma(count),
            dma(1),
            dma(count),
        ],
        micros=9.4,
    )
    if not aligned:
        table = jnp.zeros((head_total * bucket_count,), F32)
        table = lax.dynamic_update_slice_in_dim(table, small[4, :BLOCK], me_sp * BLOCK, 0)
        packed = [small[at].reshape(dp_count, -1) for at in range(4)] + [table.reshape(dp_count, -1)]
        packed = jnp.concatenate(packed, axis=1).astype(BF16)
        packed = jnp.pad(packed, ((0, 0), (0, 4 * part - packed.shape[1])))
        packed = jnp.pad(packed[:, None], ((0, 0), (0, SMALL_ROWS - 1), (0, 0)))
        last = jnp.concatenate([last, packed], axis=1)
    last_grads = ScatterRing(last, hold((up_first, down_first), *feed_grads.sent()), me, dp_count)
    last_grads.step()
    near_both = swap(hold(send_both, *feed_grads.sent()), 1)
    feed_grads.step(small)
    last_grads.step(*feed_grads.sums(), near_both)
    sent_both = add_far(hold(far_both, *last_grads.sums()), near_both)
    last_both = swap(sent_both, 2)
    sum_feed = feed_grads.finish(sent_both)
    feed_far, feed_near = swap(sum_feed, 2), swap(sum_feed, 1)
    last_grads.step(sum_feed)
    last_grads.step(last_both)
    sum_last = last_grads.finish()
    grad_input, output = call(
        ends_kernel,
        [shaped((tok, width), F32), shaped((tok, width), BF16)],
        [hold(own_one, sum_last), tokens, grad_resid, norm_gain, own_out, resid],
        [near_both, last_both],
        (),
        [pltpu.VMEM((2 * tok, width), BF16)] * 2 + [dma(2)],
        micros=1.6,
    )

    feed_last = swap(hold(feed_far, sum_last), 1)
    feed_pieces = [sum_feed, feed_near, feed_far, feed_last]
    last_far, last_near = swap(sum_last, 2), swap(sum_last, 1)
    piece = width // dp_count
    table_here = head_total * bucket_count // dp_count
    if aligned:
        out_in, out_down = call(
            wide_feed_kernel,
            [shaped((rows_here, ff), F32), shaped((sp_count * ff_rows, width), F32)],
            [],
            [hold(feed_pieces[0], sum_last)] + feed_pieces[1:],
            [me],
            [pltpu.VMEM((sp_count * rows_here, 2 * width), BF16), dma(4)],
        micros=3,
    )
        last_pieces = [sum_last, last_near, last_far, swap(hold(last_far, out_in, grad_input), 1)]
        out_qkv, out_out, gains, shifts, tables = call(
            wide_last_kernel,
            [
                shaped((rows_here, 3 * width), F32),
                shaped((rows_here, width), F32),
                shaped((2, piece), F32),
                shaped((2, piece), F32),
                shaped((1, table_here), F32),
            ],
            [],
            last_pieces,
            [me],
            [pltpu.VMEM((sp_count * (rows_here + SMALL_ROWS), width), BF16), dma(4)],
        micros=2.3,
    )
        tables = tables[0]
    else:
        all_feed = stacked_sp(feed_pieces).astype(F32)
        out_down = all_feed[:, :, width:].reshape(sp_count * ff_rows, width)
        all_in = all_feed[:, :, :width].reshape(sp_count, rows_here, dp_count, ff_rows)
        out_in = jnp.moveaxis(all_in, 0, 2).reshape(rows_here, ff)
        all_last = stacked_sp([sum_last, last_near, last_far, swap(last_far, 1)]).astype(F32)
        all_qkv = all_last[:, :rows_here, : 3 * part].reshape(sp_count, rows_here, 3, part)
        out_qkv = jnp.moveaxis(all_qkv, 0, 2).reshape(rows_here, 3 * width)
        out_out = jnp.moveaxis(all_last[:, :rows_here, 3 * part :], 0, 1).reshape(rows_here, width)
        small_row = jnp.sum(all_last[:, rows_here:], axis=0)[0]
        gains = small_row[: 2 * piece].reshape(2, piece)
        shifts = small_row[2 * piece : 4 * piece].reshape(2, piece)
        tables = small_row[4 * piece : 4 * piece + table_here]
    return (output[None], grad_input[None], out_qkv, out_out, out_in, out_down, gains, shifts, tables)


def solution(mesh):
    in_specs = (
        P("dp", "sp", None),
        P("dp", None),
        P("dp", None),
        P("dp", None),
        P("dp", None),
        P(),
        P(),
        P(),
        P("dp", None),
        P(),
        P("dp", "sp", None),
    )
    out_specs = (
        P("dp", "sp", None),
        P("dp", "sp", None),
        P("dp", None),
        P("dp", None),
        P("dp", None),
        P("dp", None),
        P(None, "dp"),
        P(None, "dp"),
        P("dp"),
    )
    return jax.shard_map(
        on_device, mesh=mesh, in_specs=in_specs, out_specs=out_specs, check_vma=False
    )
```

```python
import functools

import jax
import jax.numpy as jnp
from jax import lax
from jax.experimental import pallas as pl
from jax.experimental.pallas import tpu as pltpu
from jax.sharding import PartitionSpec as P

BLOCK = 128
SMALL_ROWS = 16
NEG = -1e30
BF16 = jnp.bfloat16
F32 = jnp.float32
VMEM_LIMIT = 24 * 1024 * 1024
ROOT = 0.7978845608028654
CUBE = 0.044715


def dot(left, right, left_dim=1, right_dim=0):
    return lax.dot_general(
        left, right, (((left_dim,), (right_dim,)), ((), ())), preferred_element_type=F32
    )


def exact_dot(left, right, left_dim=1, right_dim=0):
    return lax.dot_general(
        left,
        right,
        (((left_dim,), (right_dim,)), ((), ())),
        precision=lax.Precision.HIGHEST,
        preferred_element_type=F32,
    )


def layer_norm(values):
    average = jnp.mean(values, axis=-1, keepdims=True)
    centred = values - average
    inverse = lax.rsqrt(jnp.mean(centred * centred, axis=-1, keepdims=True) + 1e-05)
    return centred * inverse, inverse


def norm_back(upstream, normed, inverse, gain):
    scaled = upstream * gain
    centre_term = jnp.mean(scaled, axis=-1, keepdims=True)
    slope_term = jnp.mean(scaled * normed, axis=-1, keepdims=True)
    return inverse * (scaled - centre_term - normed * slope_term)


def shaped(shape, dtype):
    return jax.ShapeDtypeStruct(tuple(shape), dtype)


def call(kernel, outs, args=(), hbm_args=(), smem_args=(), scratch=(), hbm_outs=(), micros=1):
    specs = [pl.BlockSpec(memory_space=pltpu.VMEM)] * len(args)
    specs += [pl.BlockSpec(memory_space=pltpu.HBM)] * len(hbm_args)
    specs += [pl.BlockSpec(memory_space=pltpu.SMEM)] * len(smem_args)
    out_specs = [pl.BlockSpec(memory_space=pltpu.VMEM)] * len(outs)
    out_specs += [pl.BlockSpec(memory_space=pltpu.HBM)] * len(hbm_outs)
    return pl.pallas_call(
        kernel,
        out_shape=(*outs, *hbm_outs),
        in_specs=specs,
        out_specs=tuple(out_specs),
        scratch_shapes=list(scratch),
        compiler_params=pltpu.CompilerParams(vmem_limit_bytes=VMEM_LIMIT),
        cost_estimate=pl.CostEstimate(flops=0, bytes_accessed=int(micros * 3.3e6), transcendentals=0),
    )(*args, *hbm_args, *smem_args)


def rank_at(position, count):
    position = lax.rem(position + 2 * count, count)
    return jnp.where(position < count // 2, 2 * position, 2 * (count - 1 - position) + 1)


def position_of(rank, count):
    return jnp.where(lax.rem(rank, 2) == 0, lax.div(rank, 2), count - 1 - lax.div(rank, 2))


def ring_pairs(count):
    order = list(range(0, count, 2)) + list(range(count - 1, 0, -2))
    forward = [(order[i], order[(i + 1) % count]) for i in range(count)]
    return forward, [(b, a) for a, b in forward]


def half_rows(rows):
    return rows // 2 // 16 * 16


def hold(value, *others):
    return lax.optimization_barrier((value, others))[0] if others else value


def halves(up, down):
    rows, columns = up.shape
    half = half_rows(rows)

    def kernel(up_ref, down_ref, upper_ref, lower_ref, sems):
        copies = [
            pltpu.make_async_copy(up_ref.at[:half, :], upper_ref, sems.at[0]),
            pltpu.make_async_copy(down_ref.at[half:, :], lower_ref, sems.at[1]),
        ]
        finish(start_all(copies))

    outs = [shaped((half, columns), up.dtype), shaped((rows - half, columns), up.dtype)]
    return call(kernel, outs, [], [up, down], scratch=[dma(2)])


class GatherRing:
    def __init__(self, shard, count):
        self.shard, self.count, self.at = shard, count, 0
        self.up = self.down = shard
        self.pieces, self.held = [shard], (shard, shard)

    def step(self, *others):
        self.at += 1
        if self.count != 8:
            if self.at == 1:
                self.up = self.down = lax.all_gather(self.shard, "dp", axis=0, tiled=True)
                self.pieces = [self.up]
            return
        forward, backward = ring_pairs(self.count)
        up, down = self.up, self.down
        if self.at == self.count // 2:
            up, down = halves(up, down)
        self.held = up, down
        up, down, *_ = lax.optimization_barrier((up, down, *others))
        self.up = lax.ppermute(up, "dp", forward)
        self.down = lax.ppermute(down, "dp", backward)
        self.pieces += [self.up, self.down]


def target_rows(parts, me_ref, count, step):
    at = position_of(me_ref[1], count)
    near, far = count // 2 - step, count // 2 + 1 - step
    middle = parts.shape[2] // 2
    left, right = slice(0, middle), slice(middle, 2 * middle)
    up = parts.at[rank_at(at + far, count), :, left], parts.at[rank_at(at + near, count), :, right]
    down = parts.at[rank_at(at - near, count), :, left], parts.at[rank_at(at - far, count), :, right]
    return up, down


def store_first(parts, me_ref, up_ref, down_ref):
    middle = parts.shape[2] // 2
    for target, (left, right) in zip((up_ref, down_ref), target_rows(parts, me_ref, parts.shape[0], 1)):
        target[:, :middle] = left[...]
        target[:, middle:] = right[...]


def ring_add_kernel(count, step, *refs):
    parts, up_ref, down_ref, me_ref = refs[:4]
    up_out, down_out, mine, up, down, sems = refs[4:]
    middle = parts.shape[2] // 2
    left, right = slice(0, middle), slice(middle, 2 * middle)
    (up_left, up_right), (down_left, down_right) = target_rows(parts, me_ref, count, step)
    last = step == count // 2
    copies = [
        pltpu.make_async_copy(up_ref.at[:, left if last else slice(None)], up.at[:, left if last else slice(None)], sems.at[0]),
        pltpu.make_async_copy(down_ref.at[:, right if last else slice(None)], down.at[:, right if last else slice(None)], sems.at[1]),
        pltpu.make_async_copy(up_left, mine.at[0, :, left], sems.at[2]),
        pltpu.make_async_copy(down_right, mine.at[1, :, right], sems.at[3]),
    ]
    if not last:
        copies.append(pltpu.make_async_copy(up_right, mine.at[0, :, right], sems.at[4]))
        copies.append(pltpu.make_async_copy(down_left, mine.at[1, :, left], sems.at[5]))
    finish(start_all(copies))
    up_lanes, down_lanes = (left, right) if last else (slice(None), slice(None))
    up_out[...] = (mine[0, :, up_lanes].astype(F32) + up[:, up_lanes].astype(F32)).astype(BF16)
    down_out[...] = (mine[1, :, down_lanes].astype(F32) + down[:, down_lanes].astype(F32)).astype(BF16)


def ring_total_kernel(count, parts, up_ref, down_ref, last_up_ref, last_down_ref, me_ref, out_ref, mine, first, last, sems):
    middle = parts.shape[2] // 2
    left, right = slice(0, middle), slice(middle, 2 * middle)
    copies = [
        pltpu.make_async_copy(parts.at[me_ref[1]], mine, sems.at[0]),
        pltpu.make_async_copy(down_ref.at[:, left], first.at[:, left], sems.at[1]),
        pltpu.make_async_copy(up_ref.at[:, right], first.at[:, right], sems.at[2]),
        pltpu.make_async_copy(last_up_ref, last.at[:, left], sems.at[3]),
        pltpu.make_async_copy(last_down_ref, last.at[:, right], sems.at[4]),
    ]
    finish(start_all(copies))
    total = mine[...].astype(F32) + first[...].astype(F32) + last[...].astype(F32)
    out_ref[...] = total.astype(BF16)


class ScatterRing:
    def __init__(self, parts, first, me, count):
        self.parts, self.me, self.count, self.at = parts, me, count, 0
        self.added = first

    def step(self, *others):
        self.at += 1
        if self.count != 8:
            return
        forward, backward = ring_pairs(self.count)
        rows, columns = self.parts.shape[1:]
        if self.at > 1:
            width = columns // 2 if self.at == self.count // 2 else columns
            self.before = self.up, self.down
            self.added = call(
                functools.partial(ring_add_kernel, self.count, self.at),
                [shaped((rows, width), BF16)] * 2,
                [],
                [self.parts, hold(self.up, *others), self.down],
                [self.me],
                [pltpu.VMEM((2, rows, columns), BF16)] + [pltpu.VMEM((rows, columns), BF16)] * 2 + [dma(6)],
            )
        up, down = self.added
        self.up = lax.ppermute(up, "dp", forward)
        self.down = lax.ppermute(down, "dp", backward)

    def sent(self):
        return (self.up, self.down) if self.count == 8 else ()

    def sums(self):
        return tuple(self.added) if self.count == 8 else ()

    def finish(self, *others):
        if self.count != 8:
            return lax.psum_scatter(self.parts, "dp", scatter_dimension=0)
        rows, columns = self.parts.shape[1:]
        return call(
            functools.partial(ring_total_kernel, self.count),
            [shaped((rows, columns), BF16)],
            [],
            [self.parts, *self.before, hold(self.up, *others), self.down],
            [self.me],
            [pltpu.VMEM((rows, columns), BF16)] * 3 + [dma(5)],
        )[0]


def swap(values, bit):
    count = lax.axis_size("sp")
    return lax.ppermute(values, "sp", [(i, i ^ bit) for i in range(count)])


def gather_sp(piece):
    far = swap(piece, 2)
    near = swap(piece, 1)
    return [piece, near, far, swap(far, 1)]


def far_kernel(far_ref, near_ref, out_ref, near, sems):
    finish(start_all([pltpu.make_async_copy(near_ref.at[far_ref.shape[0] :, :], near, sems.at[0])]))
    out_ref[...] = (far_ref[...] + near[...].astype(F32)).astype(BF16)


def add_far(far, near):
    return call(
        far_kernel,
        [shaped(far.shape, BF16)],
        [far],
        [near],
        (),
        [pltpu.VMEM(far.shape, BF16), dma(1)],
    )[0]


def exchange_sp(sends):
    return [swap(send, step) for step, send in enumerate(sends, 1)]


def place(step, size, me_ref):
    return pl.multiple_of((me_ref[0] ^ step) * size, size)


def in_hbm(pieces):
    return [pltpu.with_memory_space_constraint(piece, pltpu.HBM) for piece in pieces]


def start_all(copies):
    for copy in copies:
        copy.start()
    return copies


def finish(copies):
    for copy in copies:
        copy.wait()


def load(pieces, me_ref, count, target, sems, lanes=slice(None)):
    if len(pieces) == 1:
        starts = [0]
    else:
        at = position_of(me_ref[1], count)
        rows = pieces[0].shape[0]
        starts = [rank_at(at + step, count) * rows for step in (0, -1, 1, -2, 2, -3, 3, 4)]
        starts.append(starts[-1] + half_rows(rows))
    copies = []
    for at, (start, piece) in enumerate(zip(starts, pieces)):
        rows = pl.ds(pl.multiple_of(start, 16), piece.shape[0])
        copies.append(pltpu.make_async_copy(piece.at[:, lanes], target.at[rows, :], sems.at[at]))
    return start_all(copies)


def load_rows(pieces, target, sems, me_ref=None, rows=slice(None), lanes=slice(None)):
    copies = []
    for step, piece in enumerate(pieces):
        block = piece.at[rows, lanes]
        size = block.shape[0]
        start = step * size if me_ref is None else place(step, size, me_ref)
        copies.append(pltpu.make_async_copy(block, target.at[pl.ds(start, size), :], sems.at[step]))
    return start_all(copies)


def dma(count):
    return pltpu.SemaphoreType.DMA((count,))


def share(sources, me, plan, rows):
    columns = sum(size for _, _, size, _ in plan)

    def kernel(*refs):
        *inputs, me_ref, target, sems = refs
        copies = []
        for at, (source, start, size, to) in enumerate(plan):
            if start is None:
                block = inputs[source].at[pl.ds(place(0, rows, me_ref), rows), :]
            else:
                block = inputs[source].at[:, pl.ds(start + place(0, size, me_ref), size)]
            copies.append(pltpu.make_async_copy(block, target.at[:, to : to + size], sems.at[at]))
        finish(start_all(copies))

    return call(
        kernel,
        [pltpu.VMEM((rows, columns), BF16)],
        [],
        [pltpu.with_memory_space_constraint(source, pltpu.HBM) for source in sources],
        [me],
        [dma(len(plan))],
    )[0]


def padded(bucket_ref):
    return jnp.concatenate([jnp.full((1, BLOCK), -1, jnp.int32), bucket_ref[...]], axis=1)


def bias_kernel(table_ref, bucket_ref, seg_ref, me_ref, bias_ref, mask_ref):
    heads, diagonals = bias_ref.shape[:2]
    buckets = padded(bucket_ref)
    bucket = lax.broadcasted_iota(jnp.int32, (table_ref.shape[1], buckets.shape[1]), 0)
    chosen = (bucket == buckets).astype(F32)
    rows = exact_dot(table_ref[...], chosen)
    row = lax.broadcasted_iota(jnp.int32, rows.shape, 0)
    for head in range(heads):
        mine = jnp.sum(jnp.where(row == me_ref[0] * heads + head, rows, 0.0), axis=0, keepdims=True)
        for diagonal in range(diagonals):
            part = mine[:, diagonal * BLOCK : (diagonal + 2) * BLOCK]
            spread = jnp.broadcast_to(part, (BLOCK, 2 * BLOCK))
            rolled = pltpu.roll(spread, BLOCK, 1, stride=1, stride_axis=0)
            bias_ref[head, diagonal] = rolled[:, :BLOCK]
    segments = seg_ref[...].astype(F32)
    key = lax.broadcasted_iota(jnp.int32, (BLOCK, BLOCK), 0)
    query = lax.broadcasted_iota(jnp.int32, (BLOCK, BLOCK), 1)
    for block in range(diagonals):
        rows = slice(block * BLOCK, (block + 1) * BLOCK)
        keys = jnp.broadcast_to(segments[:, rows], (BLOCK, BLOCK)).T
        for index in range(block, diagonals):
            same = keys == segments[:, index * BLOCK : (index + 1) * BLOCK]
            if index == block:
                same = same & (query >= key)
            mask_ref[index, rows, :] = jnp.where(same, 0.0, NEG).astype(F32)


def norm_kernel(*refs):
    pieces, (gain_ref, shift_ref), me_ref = refs[2:6], refs[:2], refs[6]
    act_ref, normed_ref, up_ref, tokens, sems, up_sems = refs[7:]
    tok = up_ref.shape[0] // 4
    copies = load_rows(pieces, tokens, sems, me_ref, slice(0, tok))
    up_copies = load_rows(pieces, up_ref, up_sems, None, slice(tok, 2 * tok))
    finish(copies)
    for start in range(0, tokens.shape[0], BLOCK):
        rows = slice(start, start + BLOCK)
        normed, _ = layer_norm(tokens[rows, :].astype(F32))
        act_ref[rows, :] = (normed * gain_ref[0:1, :] + shift_ref[0:1, :]).astype(BF16)
        normed_ref[rows, :] = normed.astype(BF16)
    finish(up_copies)


def split_heads(rows):
    lane = lax.broadcasted_iota(jnp.int32, (1, BLOCK), 1)
    low = (lane < BLOCK // 2).astype(F32).astype(BF16)
    return jnp.concatenate([rows * low, rows * (1 - low)], axis=0)


def join_heads(both):
    half = BLOCK // 2
    return jnp.concatenate([both[:half, :BLOCK], both[half:, BLOCK:]], axis=0).T


def score_block(raw, bias_ref, mask_ref, pair, index, block):
    rows = slice(block * BLOCK, (block + 1) * BLOCK)
    mask = mask_ref[index, rows, :]
    return jnp.concatenate(
        [
            raw[rows, side * BLOCK : (side + 1) * BLOCK] + bias_ref[2 * pair + side, index - block] + mask
            for side in range(2)
        ],
        axis=1,
    )


def attend_kernel(scale, parts, count, *refs):
    act_ref, bias_ref, mask_ref = refs[:3]
    pieces, me_ref = refs[3 : 3 + count], refs[3 + count]
    qkv_ref, attn_ref, log_ref, weight, sems = refs[4 + count :]
    columns = attn_ref.shape[1]
    copies = load(pieces, me_ref, parts, weight, sems, slice(0, 3 * columns))
    finish(copies)
    for start in range(0, 3 * columns, columns):
        lanes = slice(start, start + columns)
        qkv_ref[:, lanes] = dot(act_ref[...], weight[:, lanes]).astype(BF16)
    for index in range(qkv_ref.shape[0] // BLOCK):
        rows = slice(index * BLOCK, (index + 1) * BLOCK)
        width = (index + 1) * BLOCK
        for pair in range(columns // BLOCK):
            lanes = slice(pair * BLOCK, (pair + 1) * BLOCK)
            queries = split_heads(qkv_ref[rows, lanes] * scale)
            keys = qkv_ref[:width, columns + pair * BLOCK : columns + (pair + 1) * BLOCK]
            values = qkv_ref[:width, 2 * columns + pair * BLOCK : 2 * columns + (pair + 1) * BLOCK]
            raw = dot(keys, queries, 1, 1)
            scores = [score_block(raw, bias_ref, mask_ref, pair, index, block) for block in range(index + 1)]
            largest = functools.reduce(
                jnp.maximum, [jnp.max(score, axis=0, keepdims=True) for score in scores]
            )
            weights = [jnp.exp(score - largest) for score in scores]
            total = functools.reduce(jnp.add, [jnp.sum(one, axis=0, keepdims=True) for one in weights])
            mixed = dot(values, jnp.concatenate([one.astype(BF16) for one in weights], axis=0), 0, 0)
            attn_ref[rows, lanes] = join_heads(mixed / total).astype(BF16)
            at = index * (columns // BLOCK) + pair
            log_ref[at : at + 1, :] = largest + jnp.log(total)


def branch_kernel(*refs):
    tokens_ref, gain_ref, shift_ref, attn_refs, weight_refs, me_ref = (*refs[:3], refs[3:7], refs[7:11], refs[11])
    resid_ref, act_ref, weight, own, sems, weight_sems = refs[12:]
    tok = tokens_ref.shape[0]
    part = weight_refs[0].shape[1]
    copies = []
    for step in range(4):
        columns = pl.ds(place(step, part, me_ref), part)
        rows = pl.ds(place(0, tok, me_ref), tok)
        copies.append(pltpu.make_async_copy(attn_refs[step].at[rows, :], own.at[:, columns], sems.at[step]))
        copies.append(pltpu.make_async_copy(weight_refs[step], weight.at[:, columns], weight_sems.at[step]))
    finish(start_all(copies))
    resid = tokens_ref[...].astype(F32) + dot(own[...], weight[...])
    resid_ref[...] = resid
    normed, _ = layer_norm(resid)
    act_ref[...] = (normed * gain_ref[1:2, :] + shift_ref[1:2, :]).astype(BF16)


def outer(left, right, grad_ref):
    parts, rows_here, _ = grad_ref.shape
    for start in range(0, parts * rows_here, 2 * BLOCK):
        block = dot(left[:, start : start + 2 * BLOCK], right[...], 0, 0).astype(BF16)
        for sub in range(2 * BLOCK // rows_here):
            grad_ref[start // rows_here + sub] = block[sub * rows_here : (sub + 1) * rows_here]


def feed_kernel(parts, count, *refs):
    up_from, act_refs, pieces, me_ref = refs[0], refs[1:5], refs[5 : 5 + count], refs[5 + count]
    up_first, down_first, own_ref, far_ref, send_ref, fed_ref, hidden = refs[6 + count : 13 + count]
    act, up_ref, weight, down, slope, act_sems, up_sems, sems, down_sems = refs[13 + count :]
    tok = own_ref.shape[0]
    width = weight.shape[1]
    copies = load(pieces, me_ref, parts, weight, sems, slice(0, width)) + load_rows(act_refs, act, act_sems)
    finish(copies)
    late = load(pieces, me_ref, parts, down, down_sems, slice(width, None))
    late += start_all([pltpu.make_async_copy(up_from, up_ref, up_sems.at[0])])
    for start in range(0, width, 2 * BLOCK):
        columns = slice(start, start + 2 * BLOCK)
        units = dot(act[...], weight[:, columns])
        square = units * units
        bend = jnp.tanh(ROOT * units * (1.0 + CUBE * square))
        fed_ref[:, columns] = (0.5 * units * (1.0 + bend)).astype(BF16)
        slope[:, columns] = 0.5 * (1.0 + bend) + 0.5 * units * (1.0 - bend * bend) * ROOT * (
            1.0 + 3.0 * CUBE * square
        )
    finish(late)
    for start in range(0, width, 2 * BLOCK):
        rows = slice(start, start + 2 * BLOCK)
        hidden[:, rows] = (dot(up_ref[...], down[rows, :], 1, 1) * slope[:, rows]).astype(BF16)
    for start in range(0, weight.shape[0], 2 * BLOCK):
        rows = slice(start, start + 2 * BLOCK)
        share_of = dot(hidden[...], weight[rows, :], 1, 1)
        own_ref[:, rows] = share_of[:tok]
        far_ref[:, rows] = share_of[2 * tok : 3 * tok]
        send_ref[:tok, rows] = share_of[tok : 2 * tok].astype(BF16)
        send_ref[tok:, rows] = share_of[3 * tok :].astype(BF16)
    if parts == 8:
        rows_here = up_first.shape[0]
        at = position_of(me_ref[1], parts)
        far, near = parts // 2, parts // 2 - 1
        for side, (left, right, up_to, down_to) in enumerate(
            [(act, hidden, at + far, at - near), (fed_ref, up_ref, at + near, at - far)]
        ):
            some = [
                left[:, pl.ds(pl.multiple_of(rank_at(target, parts) * rows_here, rows_here), rows_here)]
                for target in (up_to, down_to)
            ]
            block = dot(jnp.concatenate(some, axis=1), right[...], 0, 0).astype(BF16)
            up_first[:, side * width : (side + 1) * width] = block[:rows_here]
            down_first[:, side * width : (side + 1) * width] = block[rows_here:]


def feed_grad_kernel(*refs):
    hidden_ref, fed_ref, up_from, act_refs, grad_ref, act, up_ref, act_sems, up_sems = (
        *refs[:3],
        refs[3:7],
        *refs[7:],
    )
    late = start_all([pltpu.make_async_copy(up_from, up_ref, up_sems.at[0])])
    finish(load_rows(act_refs, act, act_sems) + late)
    parts, rows_here, wide = grad_ref.shape
    for at, (left, right) in enumerate([(act, hidden_ref), (fed_ref, up_ref)]):
        lanes = slice(at * wide // 2, (at + 1) * wide // 2)
        for start in range(0, parts * rows_here, 2 * BLOCK):
            block = dot(left[:, start : start + 2 * BLOCK], right[...], 0, 0).astype(BF16)
            for sub in range(2 * BLOCK // rows_here):
                grad_ref[start // rows_here + sub, :, lanes] = block[sub * rows_here : (sub + 1) * rows_here]


def branch_back_kernel(*refs):
    own_ref, resid_ref, up_ref, gain_ref, near_ref, far_ref, weight_refs, me_ref = (*refs[:6], refs[6:10], refs[10])
    grad_ref, sums_ref, *send_refs, branch, grad_attn, near, far, weight, sems, weight_sems = refs[11:]
    tok = up_ref.shape[0]
    part = send_refs[0].shape[1] // 2
    copies = start_all(
        [
            pltpu.make_async_copy(near_ref.at[:tok, :], near, sems.at[0]),
            pltpu.make_async_copy(far_ref, far, sems.at[1]),
        ]
    )
    late = []
    for step in range(4):
        columns = pl.ds(place(step, part, me_ref), part)
        late.append(pltpu.make_async_copy(weight_refs[step], weight.at[:, columns], weight_sems.at[step]))
    start_all(late)
    normed, inverse = layer_norm(resid_ref[...])
    finish(copies)
    upstream = own_ref[...] + near[...].astype(F32) + far[...].astype(F32)
    sums_ref[0:1, :] = jnp.sum(upstream * normed, axis=0, keepdims=True)
    sums_ref[1:2, :] = jnp.sum(upstream, axis=0, keepdims=True)
    sums_ref[2:, :] = jnp.zeros_like(sums_ref[2:, :])
    grad = up_ref[...].astype(F32) + norm_back(upstream, normed, inverse, gain_ref[1:2, :])
    grad_ref[...] = grad
    branch[...] = grad.astype(BF16)
    finish(late)
    grad_attn[...] = dot(branch[...], weight[...], 1, 1).astype(BF16)
    for step, send in enumerate(send_refs):
        columns = pl.ds(place(step, part, me_ref), part)
        send[:, :part] = grad_attn[:, columns]
        send[:, part:] = branch[:, columns]


def attend_back_kernel(scale, dp_count, count, rest_count, *refs):
    qkv_ref, log_ref, bias_ref, mask_ref, act_ref, normed_ref, sums_ref, bucket_ref = refs[:8]
    fed_from, attn_refs, grad_refs, pieces = refs[8], refs[9:13], refs[13:17], refs[17 : 17 + count]
    down_refs, me_ref, refs = refs[17 + count : 17 + count + rest_count], refs[17 + count + rest_count], refs[18 + count + rest_count :]
    last_ref, up_first, down_first, small_ref, own_ref, own_out_ref, far_ref, send_ref = refs[:8]
    grads, branch, attn, grad_qkv, key_acc, value_acc, diagonal_acc, stacked, rolled, rolled_high, shares, weight_ref, fed_ref, down = refs[
        8:22
    ]
    grad_sems, branch_sems, attn_sems, sems, fed_sems, down_sems = refs[22:]
    seq_len = qkv_ref.shape[0]
    columns = qkv_ref.shape[1] // 3
    heads, diagonals = bias_ref.shape[:2]
    tok = own_ref.shape[0]
    copies = load_rows(grad_refs, grads, grad_sems, me_ref, lanes=slice(0, columns))
    late = load_rows(grad_refs, branch, branch_sems, me_ref, lanes=slice(columns, 2 * columns))
    late += load_rows(attn_refs, attn, attn_sems)
    late += load(pieces, me_ref, dp_count, weight_ref, sems, slice(0, 3 * columns))
    late += load(down_refs, me_ref, dp_count, down, down_sems, slice(act_ref.shape[1], None))
    late += start_all([pltpu.make_async_copy(fed_from, fed_ref, fed_sems.at[0])])
    key_acc[...] = jnp.zeros_like(key_acc)
    value_acc[...] = jnp.zeros_like(value_acc)
    diagonal_acc[...] = jnp.zeros_like(diagonal_acc)
    finish(copies)
    for pair in range(columns // BLOCK):
        lanes = slice(pair * BLOCK, (pair + 1) * BLOCK)
        all_keys = qkv_ref[:, columns + pair * BLOCK : columns + (pair + 1) * BLOCK]
        for index in range(seq_len // BLOCK):
            rows = slice(index * BLOCK, (index + 1) * BLOCK)
            width = (index + 1) * BLOCK
            queries = split_heads(qkv_ref[rows, lanes] * scale)
            grad_rows = split_heads(grads[rows, lanes])
            keys = all_keys[:width]
            values = qkv_ref[:width, 2 * columns + pair * BLOCK : 2 * columns + (pair + 1) * BLOCK]
            at = index * (columns // BLOCK) + pair
            logs = log_ref[at : at + 1, :]
            raw = dot(keys, queries, 1, 1)
            grad_probs = dot(values, grad_rows, 1, 1)
            probs = [
                jnp.exp(score_block(raw, bias_ref, mask_ref, pair, index, block) - logs)
                for block in range(index + 1)
            ]
            products = [
                one * grad_probs[block * BLOCK : (block + 1) * BLOCK] for block, one in enumerate(probs)
            ]
            row_term = functools.reduce(jnp.add, [jnp.sum(one, axis=0, keepdims=True) for one in products])
            grad_scores = [product - one * row_term for product, one in zip(products, probs)]
            for block, one in enumerate(grad_scores):
                diagonal_acc[pair, index - block] += one
            grad_raw = jnp.concatenate([one.astype(BF16) for one in grad_scores], axis=0)
            probs_all = jnp.concatenate([one.astype(BF16) for one in probs], axis=0)
            grad_qkv[rows, lanes] = (join_heads(dot(keys, grad_raw, 0, 0)) * scale).astype(BF16)
            key_acc[:width, lanes] += dot(grad_raw, queries)
            value_acc[:width, lanes] += dot(probs_all, grad_rows)
    grad_qkv[:, columns : 2 * columns] = key_acc[...].astype(BF16)
    grad_qkv[:, 2 * columns :] = value_acc[...].astype(BF16)

    parts, last_rows = last_ref.shape[:2]
    width = act_ref.shape[1]
    rows_here = width // parts
    for start in range(0, width, 2 * BLOCK):
        block = dot(act_ref[:, start : start + 2 * BLOCK], grad_qkv[...], 0, 0).astype(BF16)
        for sub in range(2 * BLOCK // rows_here):
            last_ref[start // rows_here + sub, :rows_here, : 3 * columns] = block[
                sub * rows_here : (sub + 1) * rows_here
            ]
    finish(late)
    for step in range(4):
        block = dot(attn[step * seq_len : (step + 1) * seq_len, :], branch[...], 0, 0).astype(BF16)
        for sub in range(columns // rows_here):
            part = (me_ref[0] ^ step) * (columns // rows_here) + sub
            last_ref[part, :rows_here, 3 * columns :] = block[sub * rows_here : (sub + 1) * rows_here]

    for start in range(0, width, 2 * BLOCK):
        lanes = slice(start, start + 2 * BLOCK)
        share_of = dot(grad_qkv[...], weight_ref[lanes, :], 1, 1)
        small_ref[0:1, lanes] = jnp.sum(share_of * normed_ref[:, lanes].astype(F32), axis=0, keepdims=True)
        small_ref[2:3, lanes] = jnp.sum(share_of, axis=0, keepdims=True)
        shares[:, lanes] = share_of
    for start in range(0, width, 2 * BLOCK):
        lanes = slice(start, start + 2 * BLOCK)
        share_of = dot(fed_ref[...], down[:, lanes])
        own_out_ref[:, lanes] = share_of[:tok]
        send_ref[tok : 2 * tok, lanes] = share_of[tok : 2 * tok].astype(BF16)
        far_ref[tok:, lanes] = share_of[2 * tok : 3 * tok].astype(BF16)
        send_ref[3 * tok :, lanes] = share_of[3 * tok :].astype(BF16)
    for step, (target, to) in enumerate([(own_ref, 0), (send_ref, 0), (far_ref, 0), (send_ref, 2 * tok)]):
        rows = pl.ds(place(step, tok, me_ref), tok)
        target[to : to + tok, :] = shares[rows, :].astype(target.dtype)
    small_ref[1:2, :] = sums_ref[0:1, :]
    small_ref[3:4, :] = sums_ref[1:2, :]

    for pair in range(heads // 2):
        for diagonal in range(diagonals):
            for side in range(2):
                total = jnp.zeros((8, 2 * BLOCK), F32)
                for start in range(0, BLOCK, 8):
                    some = diagonal_acc[pair, diagonal, start : start + 8, side * BLOCK : (side + 1) * BLOCK]
                    wide = jnp.concatenate([some, jnp.zeros_like(some)], axis=1)
                    total += wide if start == 0 else pltpu.roll(wide, 2 * BLOCK - start, 1)
                at = ((2 * pair + side) * diagonals + diagonal) * 8
                rolled[at : at + 8, :] = total[:, :BLOCK]
                rolled_high[at : at + 8, :] = total[:, BLOCK:]
    turned = jnp.zeros((heads * diagonals, 2 * BLOCK), F32)
    for start in range(8):
        rows = pl.ds(start, heads * diagonals, stride=8)
        both = jnp.concatenate([rolled[rows, :], rolled_high[rows, :]], axis=1)
        turned += pltpu.roll(both, BLOCK - start, 1)
    stacked[...] = jnp.zeros_like(stacked)
    for head in range(heads):
        for diagonal in range(diagonals):
            at = head * diagonals + diagonal
            stacked[head : head + 1, diagonal * BLOCK : (diagonal + 2) * BLOCK] += turned[at : at + 1, :]
    buckets = BLOCK // heads
    distances = padded(bucket_ref)
    bucket = lax.rem(lax.broadcasted_iota(jnp.int32, (BLOCK, distances.shape[1]), 0), buckets)
    chosen = (bucket == distances).astype(F32)
    by_head = exact_dot(stacked[...], chosen, 1, 1)
    row = lax.broadcasted_iota(jnp.int32, by_head.shape, 0)
    column = lax.broadcasted_iota(jnp.int32, by_head.shape, 1)
    table = jnp.sum(jnp.where(lax.div(column, buckets) == row, by_head, 0.0), axis=0, keepdims=True)
    small_ref[4:5, :BLOCK] = table
    if last_rows > rows_here:
        last_ref[:, rows_here:, :] = jnp.zeros_like(last_ref[:, rows_here:, :])
        per = parts // 4
        for part in range(parts):
            for at in range(4):
                last_ref[part, rows_here : rows_here + 1, at * rows_here : (at + 1) * rows_here] = small_ref[
                    at : at + 1, part * rows_here : (part + 1) * rows_here
                ].astype(BF16)
            turned = table if part % per == 0 else pltpu.roll(table, BLOCK - part % per * (BLOCK // per), 1)
            turned = jnp.where(me_ref[0] == part // per, turned, 0.0)
            last_ref[part, rows_here : rows_here + 1, 4 * rows_here : 4 * rows_here + BLOCK] = turned.astype(BF16)
    if parts == 8:
        store_first(last_ref, me_ref, up_first, down_first)


def ends_kernel(own_ref, tokens_ref, grad_resid_ref, gain_ref, own_out_ref, resid_ref, *refs):
    near_ref, far_ref, grad_ref, out_ref, near, far, sems = refs
    copies = start_all(
        [
            pltpu.make_async_copy(near_ref.at[: near.shape[0], :], near, sems.at[0]),
            pltpu.make_async_copy(far_ref, far, sems.at[1]),
        ]
    )
    tok = own_ref.shape[0]
    normed, inverse = layer_norm(tokens_ref[...].astype(F32))
    finish(copies)
    upstream = own_ref[...] + near[:tok, :].astype(F32) + far[:tok, :].astype(F32)
    grad_ref[...] = grad_resid_ref[...] + norm_back(upstream, normed, inverse, gain_ref[0:1, :])
    total = resid_ref[...] + own_out_ref[...] + near[tok:, :].astype(F32) + far[tok:, :].astype(F32)
    out_ref[...] = total.astype(BF16)


def wide_feed_kernel(*refs):
    pieces, me_ref, in_ref, down_ref, both, sems = refs[:4], refs[4], refs[5], refs[6], refs[7], refs[8]
    finish(load_rows(pieces, both, sems))
    rows = in_ref.shape[0]
    width = down_ref.shape[1]
    for step in range(4):
        mine = slice(step * rows, (step + 1) * rows)
        down_ref[pl.ds(place(step, rows, me_ref), rows), :] = both[mine, width:].astype(F32)
        for start in range(0, width, rows):
            at = pl.multiple_of(4 * start + (me_ref[0] ^ step) * rows, rows)
            in_ref[:, pl.ds(at, rows)] = both[mine, start : start + rows].astype(F32)


def wide_last_kernel(*refs):
    pieces, me_ref = refs[:4], refs[4]
    qkv_ref, out_ref, gain_ref, shift_ref, table_ref, last, sems = refs[5:]
    finish(load_rows(pieces, last, sems))
    rows, width = out_ref.shape
    part = width // 4
    whole = rows + SMALL_ROWS
    small = jnp.zeros((1, width), F32)
    for step in range(4):
        start = step * whole
        mine = slice(start, start + rows)
        for third in range(3):
            at = pl.multiple_of(third * width + (me_ref[0] ^ step) * part, part)
            qkv_ref[:, pl.ds(at, part)] = last[mine, third * part : (third + 1) * part].astype(F32)
        out_ref[:, pl.ds(place(step, part, me_ref), part)] = last[mine, 3 * part :].astype(F32)
        small += last[start + rows : start + whole, :].astype(F32)[0:1]
    for at in range(2):
        gain_ref[at : at + 1, :] = small[:, at * rows : (at + 1) * rows]
        shift_ref[at : at + 1, :] = small[:, (2 + at) * rows : (3 + at) * rows]
    table_ref[...] = small[:, 4 * rows : 4 * rows + table_ref.shape[1]]


def stacked_sp(pieces):
    me = lax.axis_index("sp")
    whole = jnp.zeros((len(pieces),) + pieces[0].shape, pieces[0].dtype)
    for step, piece in enumerate(pieces):
        whole = lax.dynamic_update_index_in_dim(whole, piece, me ^ step, 0)
    return whole


def on_device(
    inputs,
    qkv_weight,
    out_weight,
    in_weight,
    down_weight,
    norm_gain,
    norm_shift,
    bias_table,
    segment_ids,
    bucket_index,
    cotangent,
):
    dp_count, sp_count = lax.axis_size("dp"), lax.axis_size("sp")
    me_sp = lax.axis_index("sp")
    me = jnp.stack([me_sp, lax.axis_index("dp")]).astype(jnp.int32)
    tok, width = inputs.shape[1:]
    head_total, bucket_count = bias_table.shape
    heads = head_total // sp_count
    scale = (width // head_total) ** (-0.5)
    seq_len = segment_ids.shape[1]
    rows_here = qkv_weight.shape[0]
    ff = in_weight.shape[1]
    ff_rows = ff // dp_count // sp_count
    ff_part = ff // sp_count
    part = width // sp_count
    diagonals = seq_len // BLOCK
    aligned = ff_rows % BLOCK == 0 and rows_here % BLOCK == 0

    if aligned:
        plan = [(0, third * width, part, third * part) for third in range(3)] + [(1, 0, part, 3 * part)]
        first_part = share([qkv_weight, out_weight], me, plan, rows_here)
        step = sp_count * ff_rows
        plan = [(0, index * step, ff_rows, index * ff_rows) for index in range(dp_count)]
        plan.append((1, None, width, ff_part))
        rest_part = share([hold(in_weight, first_part), down_weight], me, plan, rows_here)
    else:

        def own_sp(stacked, axis):
            return lax.dynamic_index_in_dim(stacked, me_sp, axis, keepdims=False)

        first_part = own_sp(qkv_weight.reshape(rows_here, 3, sp_count, part), 2).reshape(rows_here, 3 * part)
        out_part = own_sp(out_weight.reshape(rows_here, sp_count, part), 1)
        first_part = jnp.concatenate([first_part, out_part], axis=1)
        in_part = own_sp(in_weight.reshape(rows_here, dp_count, sp_count, ff_rows), 2)
        in_part = in_part.reshape(rows_here, ff_part)
        down_part = lax.dynamic_slice_in_dim(down_weight, me_sp * ff_rows, ff_rows, 0)
        rest_part = jnp.concatenate([in_part, down_part], axis=1)
    first_ring = GatherRing(first_part, dp_count)
    rest_ring = GatherRing(rest_part, dp_count)

    tokens = inputs[0]
    first_ring.step()

    buckets = bucket_index[None]
    bias, mask = call(
        bias_kernel,
        [shaped((heads, diagonals, BLOCK, BLOCK), F32), shaped((diagonals, seq_len, BLOCK), F32)],
        [bias_table, hold(buckets, first_part), segment_ids],
        (),
        [me],
        micros=1.2,
    )
    both = jnp.concatenate([hold(tokens, first_part), cotangent[0]], axis=0)
    token_far, token_near = swap(both, 2), swap(both, 1)
    first_ring.step(bias, rest_part)
    token_last = swap(token_far, 1)
    first_ring.step(token_far)
    act_one, normed_one, up_all = call(
        norm_kernel,
        [shaped((seq_len, width), BF16)] * 3,
        [hold(norm_gain, *first_ring.held), norm_shift],
        [both, token_near, token_far, token_last],
        [me],
        [pltpu.VMEM((seq_len, width), BF16), dma(4), dma(4)],
        micros=2.4,
    )
    first_ring.step()
    rest_ring.step(first_ring.up, first_ring.down)
    first_pieces = first_ring.pieces
    count = len(first_pieces)
    if count == 1:
        out_columns = first_pieces[0][:, 3 * part :]
    else:

        def assemble(*refs):
            *pieces, me_ref, target, sems = refs
            finish(load(pieces, me_ref, dp_count, target, sems, slice(3 * part, 4 * part)))

        (out_columns,) = call(
            assemble, [], [], first_pieces, [me], [dma(count)], [shaped((width, part), BF16)]
        )
    out_far, out_near = swap(out_columns, 2), swap(out_columns, 1)
    pairs = heads // 2
    qkv, attn, logs = call(
        functools.partial(attend_kernel, scale, dp_count, count),
        [
            shaped((seq_len, 3 * part), BF16),
            shaped((seq_len, part), BF16),
            shaped((diagonals * pairs, 2 * BLOCK), F32),
        ],
        [hold(act_one, out_columns), bias, mask],
        first_pieces,
        [me],
        [pltpu.VMEM((width, 3 * part), BF16), dma(count)],
        micros=5,
    )
    attn = hold(attn, rest_ring.up, rest_ring.down)
    attn_far, attn_near = swap(attn, 2), swap(attn, 1)
    rest_ring.step(attn)
    attn_last = swap(attn_far, 1)
    out_last = swap(out_far, 1)
    resid, act_two = call(
        branch_kernel,
        [shaped((tok, width), F32), shaped((tok, width), BF16)],
        [tokens, norm_gain, norm_shift],
        [attn, attn_near, attn_far, attn_last, out_columns, out_near, out_far, out_last],
        [me],
        [pltpu.VMEM((width, width), BF16), pltpu.VMEM((tok, width), BF16), dma(4), dma(4)],
        micros=2.4,
    )
    act_far, act_near = swap(act_two, 2), swap(act_two, 1)
    rest_ring.step(act_two)
    act_last = swap(act_far, 1)
    rest_ring.step(act_last)
    up_first, down_first, own_two, far_two, send_two, fed, grad_hidden = call(
        functools.partial(feed_kernel, dp_count, count),
        [shaped((rows_here, 2 * width), BF16)] * 2
        + [shaped((tok, width), F32)] * 2
        + [shaped((2 * tok, width), BF16)]
        + [shaped((seq_len, ff_part), BF16)] * 2,
        [],
        in_hbm([up_all, act_two, act_near, act_far, act_last, *rest_ring.pieces]),
        [me],
        [
            pltpu.VMEM((seq_len, width), BF16),
            pltpu.VMEM((seq_len, width), BF16),
            pltpu.VMEM((width, ff_part), BF16),
            pltpu.VMEM((ff_part, width), BF16),
            pltpu.VMEM((seq_len, ff_part), F32),
            dma(4),
            dma(1),
            dma(count),
            dma(count),
        ],
        micros=7,
    )

    near_two = swap(send_two, 1)
    (grad_feed,) = call(
        feed_grad_kernel,
        [shaped((dp_count, rows_here, 2 * width), BF16)],
        [grad_hidden, fed],
        in_hbm([up_all, act_two, act_near, act_far, act_last]),
        (),
        [pltpu.VMEM((seq_len, width), BF16)] * 2 + [dma(4), dma(1)],
        micros=3,
    )
    last_two = swap(add_far(far_two, near_two), 2)
    feed_grads = ScatterRing(grad_feed, (up_first, down_first), me, dp_count)
    feed_grads.step()
    feed_grads.step(last_two)
    grad_resid, sums_two, *sends = call(
        branch_back_kernel,
        [shaped((tok, width), F32), shaped((8, width), F32)] + [shaped((tok, 2 * part), BF16)] * 4,
        [hold(own_two, *feed_grads.sums()), resid, cotangent[0], norm_gain],
        [near_two, last_two, out_columns, out_near, out_far, out_last],
        [me],
        [
            *[pltpu.VMEM((tok, width), BF16)] * 4,
            pltpu.VMEM((width, width), BF16),
            dma(2),
            dma(4),
        ],
        micros=2.5,
    )
    grad_pieces = [sends[0]] + exchange_sp(sends[1:])
    feed_grads.step(*grad_pieces[1:])
    last_rows = rows_here + SMALL_ROWS if aligned else rows_here
    last, up_first, down_first, small, own_one, own_out, far_both, send_both = call(
        functools.partial(attend_back_kernel, scale, dp_count, count, len(rest_ring.pieces)),
        [shaped((dp_count, last_rows, 4 * part), BF16)] + [shaped((last_rows, 4 * part), BF16)] * 2
        + [shaped((8, width), F32)]
        + [shaped((tok, width), F32)] * 2
        + [shaped((2 * tok, width), BF16), shaped((4 * tok, width), BF16)],
        [hold(qkv, *feed_grads.sums()), logs, bias, mask, act_one, normed_one, sums_two, buckets],
        [fed, attn, attn_near, attn_far, attn_last, *grad_pieces, *first_pieces, *in_hbm(rest_ring.pieces)],
        [me],
        [
            pltpu.VMEM((seq_len, part), BF16),
            pltpu.VMEM((seq_len, part), BF16),
            pltpu.VMEM((4 * seq_len, part), BF16),
            pltpu.VMEM((seq_len, 3 * part), BF16),
            pltpu.VMEM((seq_len, part), F32),
            pltpu.VMEM((seq_len, part), F32),
            pltpu.VMEM((pairs, diagonals, BLOCK, 2 * BLOCK), F32),
            pltpu.VMEM((heads, seq_len + BLOCK), F32),
            pltpu.VMEM((8 * heads * diagonals, BLOCK), F32),
            pltpu.VMEM((8 * heads * diagonals, BLOCK), F32),
            pltpu.VMEM((seq_len, width), F32),
            pltpu.VMEM((width, 3 * part), BF16),
            pltpu.VMEM((seq_len, ff_part), BF16),
            pltpu.VMEM((ff_part, width), BF16),
            dma(4),
            dma(4),
            dma(4),
            dma(count),
            dma(1),
            dma(count),
        ],
        micros=9.4,
    )
    if not aligned:
        table = jnp.zeros((head_total * bucket_count,), F32)
        table = lax.dynamic_update_slice_in_dim(table, small[4, :BLOCK], me_sp * BLOCK, 0)
        packed = [small[at].reshape(dp_count, -1) for at in range(4)] + [table.reshape(dp_count, -1)]
        packed = jnp.concatenate(packed, axis=1).astype(BF16)
        packed = jnp.pad(packed, ((0, 0), (0, 4 * part - packed.shape[1])))
        packed = jnp.pad(packed[:, None], ((0, 0), (0, SMALL_ROWS - 1), (0, 0)))
        last = jnp.concatenate([last, packed], axis=1)
    last_grads = ScatterRing(last, hold((up_first, down_first), *feed_grads.sent()), me, dp_count)
    last_grads.step()
    near_both = swap(hold(send_both, *feed_grads.sent()), 1)
    feed_grads.step(small)
    last_grads.step(*feed_grads.sums(), near_both)
    sent_both = add_far(hold(far_both, *last_grads.sums()), near_both)
    last_both = swap(sent_both, 2)
    sum_feed = feed_grads.finish(sent_both)
    feed_far, feed_near = swap(sum_feed, 2), swap(sum_feed, 1)
    last_grads.step(sum_feed)
    last_grads.step(last_both)
    sum_last = last_grads.finish()
    grad_input, output = call(
        ends_kernel,
        [shaped((tok, width), F32), shaped((tok, width), BF16)],
        [hold(own_one, sum_last), tokens, grad_resid, norm_gain, own_out, resid],
        [near_both, last_both],
        (),
        [pltpu.VMEM((2 * tok, width), BF16)] * 2 + [dma(2)],
        micros=1.6,
    )

    feed_last = swap(hold(feed_far, sum_last), 1)
    feed_pieces = [sum_feed, feed_near, feed_far, feed_last]
    last_far, last_near = swap(sum_last, 2), swap(sum_last, 1)
    piece = width // dp_count
    table_here = head_total * bucket_count // dp_count
    if aligned:
        out_in, out_down = call(
            wide_feed_kernel,
            [shaped((rows_here, ff), F32), shaped((sp_count * ff_rows, width), F32)],
            [],
            [hold(feed_pieces[0], sum_last)] + feed_pieces[1:],
            [me],
            [pltpu.VMEM((sp_count * rows_here, 2 * width), BF16), dma(4)],
        micros=3,
    )
        last_pieces = [sum_last, last_near, last_far, swap(hold(last_far, out_in, grad_input), 1)]
        out_qkv, out_out, gains, shifts, tables = call(
            wide_last_kernel,
            [
                shaped((rows_here, 3 * width), F32),
                shaped((rows_here, width), F32),
                shaped((2, piece), F32),
                shaped((2, piece), F32),
                shaped((1, table_here), F32),
            ],
            [],
            last_pieces,
            [me],
            [pltpu.VMEM((sp_count * (rows_here + SMALL_ROWS), width), BF16), dma(4)],
        micros=2.3,
    )
        tables = tables[0]
    else:
        all_feed = stacked_sp(feed_pieces).astype(F32)
        out_down = all_feed[:, :, width:].reshape(sp_count * ff_rows, width)
        all_in = all_feed[:, :, :width].reshape(sp_count, rows_here, dp_count, ff_rows)
        out_in = jnp.moveaxis(all_in, 0, 2).reshape(rows_here, ff)
        all_last = stacked_sp([sum_last, last_near, last_far, swap(last_far, 1)]).astype(F32)
        all_qkv = all_last[:, :rows_here, : 3 * part].reshape(sp_count, rows_here, 3, part)
        out_qkv = jnp.moveaxis(all_qkv, 0, 2).reshape(rows_here, 3 * width)
        out_out = jnp.moveaxis(all_last[:, :rows_here, 3 * part :], 0, 1).reshape(rows_here, width)
        small_row = jnp.sum(all_last[:, rows_here:], axis=0)[0]
        gains = small_row[: 2 * piece].reshape(2, piece)
        shifts = small_row[2 * piece : 4 * piece].reshape(2, piece)
        tables = small_row[4 * piece : 4 * piece + table_here]
    return (output[None], grad_input[None], out_qkv, out_out, out_in, out_down, gains, shifts, tables)


def solution(mesh):
    in_specs = (
        P("dp", "sp", None),
        P("dp", None),
        P("dp", None),
        P("dp", None),
        P("dp", None),
        P(),
        P(),
        P(),
        P("dp", None),
        P(),
        P("dp", "sp", None),
    )
    out_specs = (
        P("dp", "sp", None),
        P("dp", "sp", None),
        P("dp", None),
        P("dp", None),
        P("dp", None),
        P("dp", None),
        P(None, "dp"),
        P(None, "dp"),
        P("dp"),
    )
    return jax.shard_map(
        on_device, mesh=mesh, in_specs=in_specs, out_specs=out_specs, check_vma=False
    )
```

```python
import functools

import jax
import jax.numpy as jnp
from jax import lax
from jax.experimental import pallas as pl
from jax.experimental.pallas import tpu as pltpu
from jax.sharding import PartitionSpec as P

BLOCK = 128
SMALL_ROWS = 16
NEG = -1e30
BF16 = jnp.bfloat16
F32 = jnp.float32
VMEM_LIMIT = 24 * 1024 * 1024
ROOT = 0.7978845608028654
CUBE = 0.044715


def dot(left, right, left_dim=1, right_dim=0):
    return lax.dot_general(
        left, right, (((left_dim,), (right_dim,)), ((), ())), preferred_element_type=F32
    )


def exact_dot(left, right, left_dim=1, right_dim=0):
    return lax.dot_general(
        left,
        right,
        (((left_dim,), (right_dim,)), ((), ())),
        precision=lax.Precision.HIGHEST,
        preferred_element_type=F32,
    )


def layer_norm(values):
    average = jnp.mean(values, axis=-1, keepdims=True)
    centred = values - average
    inverse = lax.rsqrt(jnp.mean(centred * centred, axis=-1, keepdims=True) + 1e-05)
    return centred * inverse, inverse


def norm_back(upstream, normed, inverse, gain):
    scaled = upstream * gain
    centre_term = jnp.mean(scaled, axis=-1, keepdims=True)
    slope_term = jnp.mean(scaled * normed, axis=-1, keepdims=True)
    return inverse * (scaled - centre_term - normed * slope_term)


def shaped(shape, dtype):
    return jax.ShapeDtypeStruct(tuple(shape), dtype)


def call(kernel, outs, args=(), hbm_args=(), smem_args=(), scratch=(), hbm_outs=(), micros=1):
    specs = [pl.BlockSpec(memory_space=pltpu.VMEM)] * len(args)
    specs += [pl.BlockSpec(memory_space=pltpu.HBM)] * len(hbm_args)
    specs += [pl.BlockSpec(memory_space=pltpu.SMEM)] * len(smem_args)
    out_specs = [pl.BlockSpec(memory_space=pltpu.VMEM)] * len(outs)
    out_specs += [pl.BlockSpec(memory_space=pltpu.HBM)] * len(hbm_outs)
    return pl.pallas_call(
        kernel,
        out_shape=(*outs, *hbm_outs),
        in_specs=specs,
        out_specs=tuple(out_specs),
        scratch_shapes=list(scratch),
        compiler_params=pltpu.CompilerParams(vmem_limit_bytes=VMEM_LIMIT),
        cost_estimate=pl.CostEstimate(flops=0, bytes_accessed=int(micros * 3.3e6), transcendentals=0),
    )(*args, *hbm_args, *smem_args)


def rank_at(position, count):
    position = lax.rem(position + 2 * count, count)
    return jnp.where(position < count // 2, 2 * position, 2 * (count - 1 - position) + 1)


def position_of(rank, count):
    return jnp.where(lax.rem(rank, 2) == 0, lax.div(rank, 2), count - 1 - lax.div(rank, 2))


def ring_pairs(count):
    order = list(range(0, count, 2)) + list(range(count - 1, 0, -2))
    forward = [(order[i], order[(i + 1) % count]) for i in range(count)]
    return forward, [(b, a) for a, b in forward]


def half_rows(rows):
    return rows // 2 // 16 * 16


def hold(value, *others):
    return lax.optimization_barrier((value, others))[0] if others else value


def halves(up, down):
    rows, columns = up.shape
    half = half_rows(rows)

    def kernel(up_ref, down_ref, upper_ref, lower_ref, sems):
        copies = [
            pltpu.make_async_copy(up_ref.at[:half, :], upper_ref, sems.at[0]),
            pltpu.make_async_copy(down_ref.at[half:, :], lower_ref, sems.at[1]),
        ]
        finish(start_all(copies))

    outs = [shaped((half, columns), up.dtype), shaped((rows - half, columns), up.dtype)]
    return call(kernel, outs, [], [up, down], scratch=[dma(2)])


class GatherRing:
    def __init__(self, shard, count):
        self.shard, self.count, self.at = shard, count, 0
        self.up = self.down = shard
        self.pieces, self.held = [shard], (shard, shard)

    def step(self, *others):
        self.at += 1
        if self.count != 8:
            if self.at == 1:
                self.up = self.down = lax.all_gather(self.shard, "dp", axis=0, tiled=True)
                self.pieces = [self.up]
            return
        forward, backward = ring_pairs(self.count)
        up, down = self.up, self.down
        if self.at == self.count // 2:
            up, down = halves(up, down)
        self.held = up, down
        up, down, *_ = lax.optimization_barrier((up, down, *others))
        self.up = lax.ppermute(up, "dp", forward)
        self.down = lax.ppermute(down, "dp", backward)
        self.pieces += [self.up, self.down]


def target_rows(parts, me_ref, count, step):
    at = position_of(me_ref[1], count)
    near, far = count // 2 - step, count // 2 + 1 - step
    middle = parts.shape[2] // 2
    left, right = slice(0, middle), slice(middle, 2 * middle)
    up = parts.at[rank_at(at + far, count), :, left], parts.at[rank_at(at + near, count), :, right]
    down = parts.at[rank_at(at - near, count), :, left], parts.at[rank_at(at - far, count), :, right]
    return up, down


def store_first(parts, me_ref, up_ref, down_ref):
    middle = parts.shape[2] // 2
    for target, (left, right) in zip((up_ref, down_ref), target_rows(parts, me_ref, parts.shape[0], 1)):
        target[:, :middle] = left[...]
        target[:, middle:] = right[...]


def ring_add_kernel(count, step, up_ref, down_ref, parts, me_ref, up_out, down_out, mine, sems):
    middle = parts.shape[2] // 2
    left, right = slice(0, middle), slice(middle, 2 * middle)
    (up_left, up_right), (down_left, down_right) = target_rows(parts, me_ref, count, step)
    copies = [
        pltpu.make_async_copy(up_left, mine.at[0, :, left], sems.at[0]),
        pltpu.make_async_copy(down_right, mine.at[1, :, right], sems.at[1]),
    ]
    up_lanes, down_lanes = left, right
    if step < count // 2:
        copies.append(pltpu.make_async_copy(up_right, mine.at[0, :, right], sems.at[2]))
        copies.append(pltpu.make_async_copy(down_left, mine.at[1, :, left], sems.at[3]))
        up_lanes = down_lanes = slice(0, 2 * middle)
    finish(start_all(copies))
    up_out[...] = (mine[0, :, up_lanes].astype(F32) + up_ref[:, up_lanes].astype(F32)).astype(BF16)
    down_out[...] = (mine[1, :, down_lanes].astype(F32) + down_ref[:, down_lanes].astype(F32)).astype(BF16)


def ring_total_kernel(count, up_ref, down_ref, last_up_ref, last_down_ref, parts, me_ref, out_ref, mine, sems):
    middle = parts.shape[2] // 2
    left, right = slice(0, middle), slice(middle, 2 * middle)
    finish(start_all([pltpu.make_async_copy(parts.at[me_ref[1]], mine, sems.at[0])]))
    for lanes, first, last in ((left, down_ref, last_up_ref), (right, up_ref, last_down_ref)):
        total = mine[:, lanes].astype(F32) + first[:, lanes].astype(F32) + last[...].astype(F32)
        out_ref[:, lanes] = total.astype(BF16)


class ScatterRing:
    def __init__(self, parts, first, me, count):
        self.parts, self.me, self.count, self.at = parts, me, count, 0
        self.added = first

    def step(self, *others):
        self.at += 1
        if self.count != 8:
            return
        forward, backward = ring_pairs(self.count)
        rows, columns = self.parts.shape[1:]
        if self.at > 1:
            width = columns // 2 if self.at == self.count // 2 else columns
            self.before = self.up, self.down
            self.added = call(
                functools.partial(ring_add_kernel, self.count, self.at),
                [shaped((rows, width), BF16)] * 2,
                [hold(self.up, *others), self.down],
                [self.parts],
                [self.me],
                [pltpu.VMEM((2, rows, columns), BF16), dma(4)],
            )
        up, down = self.added
        self.up = lax.ppermute(up, "dp", forward)
        self.down = lax.ppermute(down, "dp", backward)

    def sent(self):
        return (self.up, self.down) if self.count == 8 else ()

    def sums(self):
        return tuple(self.added) if self.count == 8 else ()

    def finish(self, *others):
        if self.count != 8:
            return lax.psum_scatter(self.parts, "dp", scatter_dimension=0)
        rows, columns = self.parts.shape[1:]
        return call(
            functools.partial(ring_total_kernel, self.count),
            [shaped((rows, columns), BF16)],
            [*self.before, hold(self.up, *others), self.down],
            [self.parts],
            [self.me],
            [pltpu.VMEM((rows, columns), BF16), dma(1)],
        )[0]


def swap(values, bit):
    count = lax.axis_size("sp")
    return lax.ppermute(values, "sp", [(i, i ^ bit) for i in range(count)])


def gather_sp(piece):
    far = swap(piece, 2)
    near = swap(piece, 1)
    return [piece, near, far, swap(far, 1)]


def far_kernel(far_ref, near_ref, out_ref, near, sems):
    finish(start_all([pltpu.make_async_copy(near_ref.at[far_ref.shape[0] :, :], near, sems.at[0])]))
    out_ref[...] = (far_ref[...] + near[...].astype(F32)).astype(BF16)


def add_far(far, near):
    return call(
        far_kernel,
        [shaped(far.shape, BF16)],
        [far],
        [near],
        (),
        [pltpu.VMEM(far.shape, BF16), dma(1)],
    )[0]


def exchange_sp(sends):
    return [swap(send, step) for step, send in enumerate(sends, 1)]


def place(step, size, me_ref):
    return pl.multiple_of((me_ref[0] ^ step) * size, size)


def in_hbm(pieces):
    return [pltpu.with_memory_space_constraint(piece, pltpu.HBM) for piece in pieces]


def start_all(copies):
    for copy in copies:
        copy.start()
    return copies


def finish(copies):
    for copy in copies:
        copy.wait()


def load(pieces, me_ref, count, target, sems, lanes=slice(None)):
    if len(pieces) == 1:
        starts = [0]
    else:
        at = position_of(me_ref[1], count)
        rows = pieces[0].shape[0]
        starts = [rank_at(at + step, count) * rows for step in (0, -1, 1, -2, 2, -3, 3, 4)]
        starts.append(starts[-1] + half_rows(rows))
    copies = []
    for at, (start, piece) in enumerate(zip(starts, pieces)):
        rows = pl.ds(pl.multiple_of(start, 16), piece.shape[0])
        copies.append(pltpu.make_async_copy(piece.at[:, lanes], target.at[rows, :], sems.at[at]))
    return start_all(copies)


def load_rows(pieces, target, sems, me_ref=None, rows=slice(None), lanes=slice(None)):
    copies = []
    for step, piece in enumerate(pieces):
        block = piece.at[rows, lanes]
        size = block.shape[0]
        start = step * size if me_ref is None else place(step, size, me_ref)
        copies.append(pltpu.make_async_copy(block, target.at[pl.ds(start, size), :], sems.at[step]))
    return start_all(copies)


def dma(count):
    return pltpu.SemaphoreType.DMA((count,))


def share(sources, me, plan, rows):
    columns = sum(size for _, _, size, _ in plan)

    def kernel(*refs):
        *inputs, me_ref, target, sems = refs
        copies = []
        for at, (source, start, size, to) in enumerate(plan):
            if start is None:
                block = inputs[source].at[pl.ds(place(0, rows, me_ref), rows), :]
            else:
                block = inputs[source].at[:, pl.ds(start + place(0, size, me_ref), size)]
            copies.append(pltpu.make_async_copy(block, target.at[:, to : to + size], sems.at[at]))
        finish(start_all(copies))

    return call(
        kernel,
        [pltpu.VMEM((rows, columns), BF16)],
        [],
        [pltpu.with_memory_space_constraint(source, pltpu.HBM) for source in sources],
        [me],
        [dma(len(plan))],
    )[0]


def padded(bucket_ref):
    return jnp.concatenate([jnp.full((1, BLOCK), -1, jnp.int32), bucket_ref[...]], axis=1)


def bias_kernel(table_ref, bucket_ref, seg_ref, me_ref, bias_ref, mask_ref):
    heads, diagonals = bias_ref.shape[:2]
    buckets = padded(bucket_ref)
    bucket = lax.broadcasted_iota(jnp.int32, (table_ref.shape[1], buckets.shape[1]), 0)
    chosen = (bucket == buckets).astype(F32)
    rows = exact_dot(table_ref[...], chosen)
    row = lax.broadcasted_iota(jnp.int32, rows.shape, 0)
    for head in range(heads):
        mine = jnp.sum(jnp.where(row == me_ref[0] * heads + head, rows, 0.0), axis=0, keepdims=True)
        for diagonal in range(diagonals):
            part = mine[:, diagonal * BLOCK : (diagonal + 2) * BLOCK]
            spread = jnp.broadcast_to(part, (BLOCK, 2 * BLOCK))
            rolled = pltpu.roll(spread, BLOCK, 1, stride=1, stride_axis=0)
            bias_ref[head, diagonal] = rolled[:, :BLOCK]
    segments = seg_ref[...].astype(F32)
    key = lax.broadcasted_iota(jnp.int32, (BLOCK, BLOCK), 0)
    query = lax.broadcasted_iota(jnp.int32, (BLOCK, BLOCK), 1)
    for block in range(diagonals):
        rows = slice(block * BLOCK, (block + 1) * BLOCK)
        keys = jnp.broadcast_to(segments[:, rows], (BLOCK, BLOCK)).T
        for index in range(block, diagonals):
            same = keys == segments[:, index * BLOCK : (index + 1) * BLOCK]
            if index == block:
                same = same & (query >= key)
            mask_ref[index, rows, :] = jnp.where(same, 0.0, NEG).astype(F32)


def norm_kernel(*refs):
    pieces, (gain_ref, shift_ref), me_ref = refs[2:6], refs[:2], refs[6]
    act_ref, normed_ref, up_ref, tokens, sems, up_sems = refs[7:]
    tok = up_ref.shape[0] // 4
    copies = load_rows(pieces, tokens, sems, me_ref, slice(0, tok))
    up_copies = load_rows(pieces, up_ref, up_sems, None, slice(tok, 2 * tok))
    finish(copies)
    for start in range(0, tokens.shape[0], BLOCK):
        rows = slice(start, start + BLOCK)
        normed, _ = layer_norm(tokens[rows, :].astype(F32))
        act_ref[rows, :] = (normed * gain_ref[0:1, :] + shift_ref[0:1, :]).astype(BF16)
        normed_ref[rows, :] = normed.astype(BF16)
    finish(up_copies)


def split_heads(rows):
    lane = lax.broadcasted_iota(jnp.int32, (1, BLOCK), 1)
    low = (lane < BLOCK // 2).astype(F32).astype(BF16)
    return jnp.concatenate([rows * low, rows * (1 - low)], axis=0)


def join_heads(both):
    half = BLOCK // 2
    return jnp.concatenate([both[:half, :BLOCK], both[half:, BLOCK:]], axis=0).T


def score_block(raw, bias_ref, mask_ref, pair, index, block):
    rows = slice(block * BLOCK, (block + 1) * BLOCK)
    mask = mask_ref[index, rows, :]
    return jnp.concatenate(
        [
            raw[rows, side * BLOCK : (side + 1) * BLOCK] + bias_ref[2 * pair + side, index - block] + mask
            for side in range(2)
        ],
        axis=1,
    )


def attend_kernel(scale, parts, count, *refs):
    act_ref, bias_ref, mask_ref = refs[:3]
    pieces, me_ref = refs[3 : 3 + count], refs[3 + count]
    qkv_ref, attn_ref, log_ref, weight, sems = refs[4 + count :]
    columns = attn_ref.shape[1]
    copies = load(pieces, me_ref, parts, weight, sems, slice(0, 3 * columns))
    finish(copies)
    for start in range(0, 3 * columns, columns):
        lanes = slice(start, start + columns)
        qkv_ref[:, lanes] = dot(act_ref[...], weight[:, lanes]).astype(BF16)
    for index in range(qkv_ref.shape[0] // BLOCK):
        rows = slice(index * BLOCK, (index + 1) * BLOCK)
        width = (index + 1) * BLOCK
        for pair in range(columns // BLOCK):
            lanes = slice(pair * BLOCK, (pair + 1) * BLOCK)
            queries = split_heads(qkv_ref[rows, lanes] * scale)
            keys = qkv_ref[:width, columns + pair * BLOCK : columns + (pair + 1) * BLOCK]
            values = qkv_ref[:width, 2 * columns + pair * BLOCK : 2 * columns + (pair + 1) * BLOCK]
            raw = dot(keys, queries, 1, 1)
            scores = [score_block(raw, bias_ref, mask_ref, pair, index, block) for block in range(index + 1)]
            largest = functools.reduce(
                jnp.maximum, [jnp.max(score, axis=0, keepdims=True) for score in scores]
            )
            weights = [jnp.exp(score - largest) for score in scores]
            total = functools.reduce(jnp.add, [jnp.sum(one, axis=0, keepdims=True) for one in weights])
            mixed = dot(values, jnp.concatenate([one.astype(BF16) for one in weights], axis=0), 0, 0)
            attn_ref[rows, lanes] = join_heads(mixed / total).astype(BF16)
            at = index * (columns // BLOCK) + pair
            log_ref[at : at + 1, :] = largest + jnp.log(total)


def branch_kernel(*refs):
    tokens_ref, gain_ref, shift_ref, attn_refs, weight_refs, me_ref = (*refs[:3], refs[3:7], refs[7:11], refs[11])
    resid_ref, act_ref, weight, own, sems, weight_sems = refs[12:]
    tok = tokens_ref.shape[0]
    part = weight_refs[0].shape[1]
    copies = []
    for step in range(4):
        columns = pl.ds(place(step, part, me_ref), part)
        rows = pl.ds(place(0, tok, me_ref), tok)
        copies.append(pltpu.make_async_copy(attn_refs[step].at[rows, :], own.at[:, columns], sems.at[step]))
        copies.append(pltpu.make_async_copy(weight_refs[step], weight.at[:, columns], weight_sems.at[step]))
    finish(start_all(copies))
    resid = tokens_ref[...].astype(F32) + dot(own[...], weight[...])
    resid_ref[...] = resid
    normed, _ = layer_norm(resid)
    act_ref[...] = (normed * gain_ref[1:2, :] + shift_ref[1:2, :]).astype(BF16)


def outer(left, right, grad_ref):
    parts, rows_here, _ = grad_ref.shape
    for start in range(0, parts * rows_here, 2 * BLOCK):
        block = dot(left[:, start : start + 2 * BLOCK], right[...], 0, 0).astype(BF16)
        for sub in range(2 * BLOCK // rows_here):
            grad_ref[start // rows_here + sub] = block[sub * rows_here : (sub + 1) * rows_here]


def feed_kernel(parts, count, *refs):
    up_from, act_refs, pieces, me_ref = refs[0], refs[1:5], refs[5 : 5 + count], refs[5 + count]
    up_first, down_first, own_ref, far_ref, send_ref, fed_ref, hidden = refs[6 + count : 13 + count]
    act, up_ref, weight, down, slope, act_sems, up_sems, sems, down_sems = refs[13 + count :]
    tok = own_ref.shape[0]
    width = weight.shape[1]
    copies = load(pieces, me_ref, parts, weight, sems, slice(0, width)) + load_rows(act_refs, act, act_sems)
    finish(copies)
    late = load(pieces, me_ref, parts, down, down_sems, slice(width, None))
    late += start_all([pltpu.make_async_copy(up_from, up_ref, up_sems.at[0])])
    for start in range(0, width, 2 * BLOCK):
        columns = slice(start, start + 2 * BLOCK)
        units = dot(act[...], weight[:, columns])
        square = units * units
        bend = jnp.tanh(ROOT * units * (1.0 + CUBE * square))
        fed_ref[:, columns] = (0.5 * units * (1.0 + bend)).astype(BF16)
        slope[:, columns] = 0.5 * (1.0 + bend) + 0.5 * units * (1.0 - bend * bend) * ROOT * (
            1.0 + 3.0 * CUBE * square
        )
    finish(late)
    for start in range(0, width, 2 * BLOCK):
        rows = slice(start, start + 2 * BLOCK)
        hidden[:, rows] = (dot(up_ref[...], down[rows, :], 1, 1) * slope[:, rows]).astype(BF16)
    for start in range(0, weight.shape[0], 2 * BLOCK):
        rows = slice(start, start + 2 * BLOCK)
        share_of = dot(hidden[...], weight[rows, :], 1, 1)
        own_ref[:, rows] = share_of[:tok]
        far_ref[:, rows] = share_of[2 * tok : 3 * tok]
        send_ref[:tok, rows] = share_of[tok : 2 * tok].astype(BF16)
        send_ref[tok:, rows] = share_of[3 * tok :].astype(BF16)
    if parts == 8:
        rows_here = up_first.shape[0]
        at = position_of(me_ref[1], parts)
        far, near = parts // 2, parts // 2 - 1
        for side, (left, right, up_to, down_to) in enumerate(
            [(act, hidden, at + far, at - near), (fed_ref, up_ref, at + near, at - far)]
        ):
            some = [
                left[:, pl.ds(pl.multiple_of(rank_at(target, parts) * rows_here, rows_here), rows_here)]
                for target in (up_to, down_to)
            ]
            block = dot(jnp.concatenate(some, axis=1), right[...], 0, 0).astype(BF16)
            up_first[:, side * width : (side + 1) * width] = block[:rows_here]
            down_first[:, side * width : (side + 1) * width] = block[rows_here:]


def feed_grad_kernel(*refs):
    hidden_ref, fed_ref, up_from, act_refs, grad_ref, act, up_ref, act_sems, up_sems = (
        *refs[:3],
        refs[3:7],
        *refs[7:],
    )
    late = start_all([pltpu.make_async_copy(up_from, up_ref, up_sems.at[0])])
    finish(load_rows(act_refs, act, act_sems) + late)
    parts, rows_here, wide = grad_ref.shape
    for at, (left, right) in enumerate([(act, hidden_ref), (fed_ref, up_ref)]):
        lanes = slice(at * wide // 2, (at + 1) * wide // 2)
        for start in range(0, parts * rows_here, 2 * BLOCK):
            block = dot(left[:, start : start + 2 * BLOCK], right[...], 0, 0).astype(BF16)
            for sub in range(2 * BLOCK // rows_here):
                grad_ref[start // rows_here + sub, :, lanes] = block[sub * rows_here : (sub + 1) * rows_here]


def branch_back_kernel(*refs):
    own_ref, resid_ref, up_ref, gain_ref, near_ref, far_ref, weight_refs, me_ref = (*refs[:6], refs[6:10], refs[10])
    grad_ref, sums_ref, *send_refs, branch, grad_attn, near, far, weight, sems, weight_sems = refs[11:]
    tok = up_ref.shape[0]
    part = send_refs[0].shape[1] // 2
    copies = start_all(
        [
            pltpu.make_async_copy(near_ref.at[:tok, :], near, sems.at[0]),
            pltpu.make_async_copy(far_ref, far, sems.at[1]),
        ]
    )
    late = []
    for step in range(4):
        columns = pl.ds(place(step, part, me_ref), part)
        late.append(pltpu.make_async_copy(weight_refs[step], weight.at[:, columns], weight_sems.at[step]))
    start_all(late)
    normed, inverse = layer_norm(resid_ref[...])
    finish(copies)
    upstream = own_ref[...] + near[...].astype(F32) + far[...].astype(F32)
    sums_ref[0:1, :] = jnp.sum(upstream * normed, axis=0, keepdims=True)
    sums_ref[1:2, :] = jnp.sum(upstream, axis=0, keepdims=True)
    sums_ref[2:, :] = jnp.zeros_like(sums_ref[2:, :])
    grad = up_ref[...].astype(F32) + norm_back(upstream, normed, inverse, gain_ref[1:2, :])
    grad_ref[...] = grad
    branch[...] = grad.astype(BF16)
    finish(late)
    grad_attn[...] = dot(branch[...], weight[...], 1, 1).astype(BF16)
    for step, send in enumerate(send_refs):
        columns = pl.ds(place(step, part, me_ref), part)
        send[:, :part] = grad_attn[:, columns]
        send[:, part:] = branch[:, columns]


def attend_back_kernel(scale, dp_count, count, rest_count, *refs):
    qkv_ref, log_ref, bias_ref, mask_ref, act_ref, normed_ref, sums_ref, bucket_ref = refs[:8]
    fed_from, attn_refs, grad_refs, pieces = refs[8], refs[9:13], refs[13:17], refs[17 : 17 + count]
    down_refs, me_ref, refs = refs[17 + count : 17 + count + rest_count], refs[17 + count + rest_count], refs[18 + count + rest_count :]
    last_ref, up_first, down_first, small_ref, own_ref, own_out_ref, far_ref, send_ref = refs[:8]
    grads, branch, attn, grad_qkv, key_acc, value_acc, diagonal_acc, stacked, rolled, rolled_high, shares, weight_ref, fed_ref, down = refs[
        8:22
    ]
    grad_sems, branch_sems, attn_sems, sems, fed_sems, down_sems = refs[22:]
    seq_len = qkv_ref.shape[0]
    columns = qkv_ref.shape[1] // 3
    heads, diagonals = bias_ref.shape[:2]
    tok = own_ref.shape[0]
    copies = load_rows(grad_refs, grads, grad_sems, me_ref, lanes=slice(0, columns))
    late = load_rows(grad_refs, branch, branch_sems, me_ref, lanes=slice(columns, 2 * columns))
    late += load_rows(attn_refs, attn, attn_sems)
    late += load(pieces, me_ref, dp_count, weight_ref, sems, slice(0, 3 * columns))
    late += load(down_refs, me_ref, dp_count, down, down_sems, slice(act_ref.shape[1], None))
    late += start_all([pltpu.make_async_copy(fed_from, fed_ref, fed_sems.at[0])])
    key_acc[...] = jnp.zeros_like(key_acc)
    value_acc[...] = jnp.zeros_like(value_acc)
    diagonal_acc[...] = jnp.zeros_like(diagonal_acc)
    finish(copies)
    for pair in range(columns // BLOCK):
        lanes = slice(pair * BLOCK, (pair + 1) * BLOCK)
        all_keys = qkv_ref[:, columns + pair * BLOCK : columns + (pair + 1) * BLOCK]
        for index in range(seq_len // BLOCK):
            rows = slice(index * BLOCK, (index + 1) * BLOCK)
            width = (index + 1) * BLOCK
            queries = split_heads(qkv_ref[rows, lanes] * scale)
            grad_rows = split_heads(grads[rows, lanes])
            keys = all_keys[:width]
            values = qkv_ref[:width, 2 * columns + pair * BLOCK : 2 * columns + (pair + 1) * BLOCK]
            at = index * (columns // BLOCK) + pair
            logs = log_ref[at : at + 1, :]
            raw = dot(keys, queries, 1, 1)
            grad_probs = dot(values, grad_rows, 1, 1)
            probs = [
                jnp.exp(score_block(raw, bias_ref, mask_ref, pair, index, block) - logs)
                for block in range(index + 1)
            ]
            products = [
                one * grad_probs[block * BLOCK : (block + 1) * BLOCK] for block, one in enumerate(probs)
            ]
            row_term = functools.reduce(jnp.add, [jnp.sum(one, axis=0, keepdims=True) for one in products])
            grad_scores = [product - one * row_term for product, one in zip(products, probs)]
            for block, one in enumerate(grad_scores):
                diagonal_acc[pair, index - block] += one
            grad_raw = jnp.concatenate([one.astype(BF16) for one in grad_scores], axis=0)
            probs_all = jnp.concatenate([one.astype(BF16) for one in probs], axis=0)
            grad_qkv[rows, lanes] = (join_heads(dot(keys, grad_raw, 0, 0)) * scale).astype(BF16)
            key_acc[:width, lanes] += dot(grad_raw, queries)
            value_acc[:width, lanes] += dot(probs_all, grad_rows)
    grad_qkv[:, columns : 2 * columns] = key_acc[...].astype(BF16)
    grad_qkv[:, 2 * columns :] = value_acc[...].astype(BF16)

    parts, last_rows = last_ref.shape[:2]
    width = act_ref.shape[1]
    rows_here = width // parts
    for start in range(0, width, 2 * BLOCK):
        block = dot(act_ref[:, start : start + 2 * BLOCK], grad_qkv[...], 0, 0).astype(BF16)
        for sub in range(2 * BLOCK // rows_here):
            last_ref[start // rows_here + sub, :rows_here, : 3 * columns] = block[
                sub * rows_here : (sub + 1) * rows_here
            ]
    finish(late)
    for step in range(4):
        block = dot(attn[step * seq_len : (step + 1) * seq_len, :], branch[...], 0, 0).astype(BF16)
        for sub in range(columns // rows_here):
            part = (me_ref[0] ^ step) * (columns // rows_here) + sub
            last_ref[part, :rows_here, 3 * columns :] = block[sub * rows_here : (sub + 1) * rows_here]

    for start in range(0, width, 2 * BLOCK):
        lanes = slice(start, start + 2 * BLOCK)
        share_of = dot(grad_qkv[...], weight_ref[lanes, :], 1, 1)
        small_ref[0:1, lanes] = jnp.sum(share_of * normed_ref[:, lanes].astype(F32), axis=0, keepdims=True)
        small_ref[2:3, lanes] = jnp.sum(share_of, axis=0, keepdims=True)
        shares[:, lanes] = share_of
    for start in range(0, width, 2 * BLOCK):
        lanes = slice(start, start + 2 * BLOCK)
        share_of = dot(fed_ref[...], down[:, lanes])
        own_out_ref[:, lanes] = share_of[:tok]
        send_ref[tok : 2 * tok, lanes] = share_of[tok : 2 * tok].astype(BF16)
        far_ref[tok:, lanes] = share_of[2 * tok : 3 * tok].astype(BF16)
        send_ref[3 * tok :, lanes] = share_of[3 * tok :].astype(BF16)
    for step, (target, to) in enumerate([(own_ref, 0), (send_ref, 0), (far_ref, 0), (send_ref, 2 * tok)]):
        rows = pl.ds(place(step, tok, me_ref), tok)
        target[to : to + tok, :] = shares[rows, :].astype(target.dtype)
    small_ref[1:2, :] = sums_ref[0:1, :]
    small_ref[3:4, :] = sums_ref[1:2, :]

    for pair in range(heads // 2):
        for diagonal in range(diagonals):
            for side in range(2):
                total = jnp.zeros((8, 2 * BLOCK), F32)
                for start in range(0, BLOCK, 8):
                    some = diagonal_acc[pair, diagonal, start : start + 8, side * BLOCK : (side + 1) * BLOCK]
                    wide = jnp.concatenate([some, jnp.zeros_like(some)], axis=1)
                    total += wide if start == 0 else pltpu.roll(wide, 2 * BLOCK - start, 1)
                at = ((2 * pair + side) * diagonals + diagonal) * 8
                rolled[at : at + 8, :] = total[:, :BLOCK]
                rolled_high[at : at + 8, :] = total[:, BLOCK:]
    turned = jnp.zeros((heads * diagonals, 2 * BLOCK), F32)
    for start in range(8):
        rows = pl.ds(start, heads * diagonals, stride=8)
        both = jnp.concatenate([rolled[rows, :], rolled_high[rows, :]], axis=1)
        turned += pltpu.roll(both, BLOCK - start, 1)
    stacked[...] = jnp.zeros_like(stacked)
    for head in range(heads):
        for diagonal in range(diagonals):
            at = head * diagonals + diagonal
            stacked[head : head + 1, diagonal * BLOCK : (diagonal + 2) * BLOCK] += turned[at : at + 1, :]
    buckets = BLOCK // heads
    distances = padded(bucket_ref)
    bucket = lax.rem(lax.broadcasted_iota(jnp.int32, (BLOCK, distances.shape[1]), 0), buckets)
    chosen = (bucket == distances).astype(F32)
    by_head = exact_dot(stacked[...], chosen, 1, 1)
    row = lax.broadcasted_iota(jnp.int32, by_head.shape, 0)
    column = lax.broadcasted_iota(jnp.int32, by_head.shape, 1)
    table = jnp.sum(jnp.where(lax.div(column, buckets) == row, by_head, 0.0), axis=0, keepdims=True)
    small_ref[4:5, :BLOCK] = table
    if last_rows > rows_here:
        last_ref[:, rows_here:, :] = jnp.zeros_like(last_ref[:, rows_here:, :])
        per = parts // 4
        for part in range(parts):
            for at in range(4):
                last_ref[part, rows_here : rows_here + 1, at * rows_here : (at + 1) * rows_here] = small_ref[
                    at : at + 1, part * rows_here : (part + 1) * rows_here
                ].astype(BF16)
            turned = table if part % per == 0 else pltpu.roll(table, BLOCK - part % per * (BLOCK // per), 1)
            turned = jnp.where(me_ref[0] == part // per, turned, 0.0)
            last_ref[part, rows_here : rows_here + 1, 4 * rows_here : 4 * rows_here + BLOCK] = turned.astype(BF16)
    if parts == 8:
        store_first(last_ref, me_ref, up_first, down_first)


def ends_kernel(own_ref, tokens_ref, grad_resid_ref, gain_ref, own_out_ref, resid_ref, *refs):
    near_ref, far_ref, grad_ref, out_ref, near, far, sems = refs
    copies = start_all(
        [
            pltpu.make_async_copy(near_ref.at[: near.shape[0], :], near, sems.at[0]),
            pltpu.make_async_copy(far_ref, far, sems.at[1]),
        ]
    )
    tok = own_ref.shape[0]
    normed, inverse = layer_norm(tokens_ref[...].astype(F32))
    finish(copies)
    upstream = own_ref[...] + near[:tok, :].astype(F32) + far[:tok, :].astype(F32)
    grad_ref[...] = grad_resid_ref[...] + norm_back(upstream, normed, inverse, gain_ref[0:1, :])
    total = resid_ref[...] + own_out_ref[...] + near[tok:, :].astype(F32) + far[tok:, :].astype(F32)
    out_ref[...] = total.astype(BF16)


def wide_feed_kernel(*refs):
    pieces, me_ref, in_ref, down_ref, both, sems = refs[:4], refs[4], refs[5], refs[6], refs[7], refs[8]
    finish(load_rows(pieces, both, sems))
    rows = in_ref.shape[0]
    width = down_ref.shape[1]
    for step in range(4):
        mine = slice(step * rows, (step + 1) * rows)
        down_ref[pl.ds(place(step, rows, me_ref), rows), :] = both[mine, width:].astype(F32)
        for start in range(0, width, rows):
            at = pl.multiple_of(4 * start + (me_ref[0] ^ step) * rows, rows)
            in_ref[:, pl.ds(at, rows)] = both[mine, start : start + rows].astype(F32)


def wide_last_kernel(*refs):
    pieces, me_ref = refs[:4], refs[4]
    qkv_ref, out_ref, gain_ref, shift_ref, table_ref, last, sems = refs[5:]
    finish(load_rows(pieces, last, sems))
    rows, width = out_ref.shape
    part = width // 4
    whole = rows + SMALL_ROWS
    small = jnp.zeros((1, width), F32)
    for step in range(4):
        start = step * whole
        mine = slice(start, start + rows)
        for third in range(3):
            at = pl.multiple_of(third * width + (me_ref[0] ^ step) * part, part)
            qkv_ref[:, pl.ds(at, part)] = last[mine, third * part : (third + 1) * part].astype(F32)
        out_ref[:, pl.ds(place(step, part, me_ref), part)] = last[mine, 3 * part :].astype(F32)
        small += last[start + rows : start + whole, :].astype(F32)[0:1]
    for at in range(2):
        gain_ref[at : at + 1, :] = small[:, at * rows : (at + 1) * rows]
        shift_ref[at : at + 1, :] = small[:, (2 + at) * rows : (3 + at) * rows]
    table_ref[...] = small[:, 4 * rows : 4 * rows + table_ref.shape[1]]


def stacked_sp(pieces):
    me = lax.axis_index("sp")
    whole = jnp.zeros((len(pieces),) + pieces[0].shape, pieces[0].dtype)
    for step, piece in enumerate(pieces):
        whole = lax.dynamic_update_index_in_dim(whole, piece, me ^ step, 0)
    return whole


def on_device(
    inputs,
    qkv_weight,
    out_weight,
    in_weight,
    down_weight,
    norm_gain,
    norm_shift,
    bias_table,
    segment_ids,
    bucket_index,
    cotangent,
):
    dp_count, sp_count = lax.axis_size("dp"), lax.axis_size("sp")
    me_sp = lax.axis_index("sp")
    me = jnp.stack([me_sp, lax.axis_index("dp")]).astype(jnp.int32)
    tok, width = inputs.shape[1:]
    head_total, bucket_count = bias_table.shape
    heads = head_total // sp_count
    scale = (width // head_total) ** (-0.5)
    seq_len = segment_ids.shape[1]
    rows_here = qkv_weight.shape[0]
    ff = in_weight.shape[1]
    ff_rows = ff // dp_count // sp_count
    ff_part = ff // sp_count
    part = width // sp_count
    diagonals = seq_len // BLOCK
    aligned = ff_rows % BLOCK == 0 and rows_here % BLOCK == 0

    if aligned:
        plan = [(0, third * width, part, third * part) for third in range(3)] + [(1, 0, part, 3 * part)]
        first_part = share([qkv_weight, out_weight], me, plan, rows_here)
        step = sp_count * ff_rows
        plan = [(0, index * step, ff_rows, index * ff_rows) for index in range(dp_count)]
        plan.append((1, None, width, ff_part))
        rest_part = share([hold(in_weight, first_part), down_weight], me, plan, rows_here)
    else:

        def own_sp(stacked, axis):
            return lax.dynamic_index_in_dim(stacked, me_sp, axis, keepdims=False)

        first_part = own_sp(qkv_weight.reshape(rows_here, 3, sp_count, part), 2).reshape(rows_here, 3 * part)
        out_part = own_sp(out_weight.reshape(rows_here, sp_count, part), 1)
        first_part = jnp.concatenate([first_part, out_part], axis=1)
        in_part = own_sp(in_weight.reshape(rows_here, dp_count, sp_count, ff_rows), 2)
        in_part = in_part.reshape(rows_here, ff_part)
        down_part = lax.dynamic_slice_in_dim(down_weight, me_sp * ff_rows, ff_rows, 0)
        rest_part = jnp.concatenate([in_part, down_part], axis=1)
    first_ring = GatherRing(first_part, dp_count)
    rest_ring = GatherRing(rest_part, dp_count)

    tokens = inputs[0]
    first_ring.step()

    buckets = bucket_index[None]
    bias, mask = call(
        bias_kernel,
        [shaped((heads, diagonals, BLOCK, BLOCK), F32), shaped((diagonals, seq_len, BLOCK), F32)],
        [bias_table, hold(buckets, first_part), segment_ids],
        (),
        [me],
        micros=1.2,
    )
    both = jnp.concatenate([hold(tokens, first_part), cotangent[0]], axis=0)
    token_far, token_near = swap(both, 2), swap(both, 1)
    first_ring.step(bias, rest_part)
    token_last = swap(token_far, 1)
    first_ring.step(token_far)
    act_one, normed_one, up_all = call(
        norm_kernel,
        [shaped((seq_len, width), BF16)] * 3,
        [hold(norm_gain, *first_ring.held), norm_shift],
        [both, token_near, token_far, token_last],
        [me],
        [pltpu.VMEM((seq_len, width), BF16), dma(4), dma(4)],
        micros=2.4,
    )
    first_ring.step()
    rest_ring.step(first_ring.up, first_ring.down)
    first_pieces = first_ring.pieces
    count = len(first_pieces)
    if count == 1:
        out_columns = first_pieces[0][:, 3 * part :]
    else:

        def assemble(*refs):
            *pieces, me_ref, target, sems = refs
            finish(load(pieces, me_ref, dp_count, target, sems, slice(3 * part, 4 * part)))

        (out_columns,) = call(
            assemble, [], [], first_pieces, [me], [dma(count)], [shaped((width, part), BF16)]
        )
    out_far, out_near = swap(out_columns, 2), swap(out_columns, 1)
    pairs = heads // 2
    qkv, attn, logs = call(
        functools.partial(attend_kernel, scale, dp_count, count),
        [
            shaped((seq_len, 3 * part), BF16),
            shaped((seq_len, part), BF16),
            shaped((diagonals * pairs, 2 * BLOCK), F32),
        ],
        [hold(act_one, out_columns), bias, mask],
        first_pieces,
        [me],
        [pltpu.VMEM((width, 3 * part), BF16), dma(count)],
        micros=5,
    )
    attn = hold(attn, rest_ring.up, rest_ring.down)
    attn_far, attn_near = swap(attn, 2), swap(attn, 1)
    rest_ring.step(attn)
    attn_last = swap(attn_far, 1)
    out_last = swap(out_far, 1)
    resid, act_two = call(
        branch_kernel,
        [shaped((tok, width), F32), shaped((tok, width), BF16)],
        [tokens, norm_gain, norm_shift],
        [attn, attn_near, attn_far, attn_last, out_columns, out_near, out_far, out_last],
        [me],
        [pltpu.VMEM((width, width), BF16), pltpu.VMEM((tok, width), BF16), dma(4), dma(4)],
        micros=2.4,
    )
    act_far, act_near = swap(act_two, 2), swap(act_two, 1)
    rest_ring.step(act_two)
    act_last = swap(act_far, 1)
    rest_ring.step(act_last)
    up_first, down_first, own_two, far_two, send_two, fed, grad_hidden = call(
        functools.partial(feed_kernel, dp_count, count),
        [shaped((rows_here, 2 * width), BF16)] * 2
        + [shaped((tok, width), F32)] * 2
        + [shaped((2 * tok, width), BF16)]
        + [shaped((seq_len, ff_part), BF16)] * 2,
        [],
        in_hbm([up_all, act_two, act_near, act_far, act_last, *rest_ring.pieces]),
        [me],
        [
            pltpu.VMEM((seq_len, width), BF16),
            pltpu.VMEM((seq_len, width), BF16),
            pltpu.VMEM((width, ff_part), BF16),
            pltpu.VMEM((ff_part, width), BF16),
            pltpu.VMEM((seq_len, ff_part), F32),
            dma(4),
            dma(1),
            dma(count),
            dma(count),
        ],
        micros=7,
    )

    near_two = swap(send_two, 1)
    (grad_feed,) = call(
        feed_grad_kernel,
        [shaped((dp_count, rows_here, 2 * width), BF16)],
        [grad_hidden, fed],
        in_hbm([up_all, act_two, act_near, act_far, act_last]),
        (),
        [pltpu.VMEM((seq_len, width), BF16)] * 2 + [dma(4), dma(1)],
        micros=3,
    )
    last_two = swap(add_far(far_two, near_two), 2)
    feed_grads = ScatterRing(grad_feed, (up_first, down_first), me, dp_count)
    feed_grads.step()
    feed_grads.step(last_two)
    grad_resid, sums_two, *sends = call(
        branch_back_kernel,
        [shaped((tok, width), F32), shaped((8, width), F32)] + [shaped((tok, 2 * part), BF16)] * 4,
        [own_two, resid, cotangent[0], norm_gain],
        [near_two, last_two, out_columns, out_near, out_far, out_last],
        [me],
        [
            *[pltpu.VMEM((tok, width), BF16)] * 4,
            pltpu.VMEM((width, width), BF16),
            dma(2),
            dma(4),
        ],
        micros=2.5,
    )
    grad_pieces = [sends[0]] + exchange_sp(sends[1:])
    feed_grads.step(*grad_pieces[1:])
    last_rows = rows_here + SMALL_ROWS if aligned else rows_here
    last, up_first, down_first, small, own_one, own_out, far_both, send_both = call(
        functools.partial(attend_back_kernel, scale, dp_count, count, len(rest_ring.pieces)),
        [shaped((dp_count, last_rows, 4 * part), BF16)] + [shaped((last_rows, 4 * part), BF16)] * 2
        + [shaped((8, width), F32)]
        + [shaped((tok, width), F32)] * 2
        + [shaped((2 * tok, width), BF16), shaped((4 * tok, width), BF16)],
        [hold(qkv, *feed_grads.sums()), logs, bias, mask, act_one, normed_one, sums_two, buckets],
        [fed, attn, attn_near, attn_far, attn_last, *grad_pieces, *first_pieces, *in_hbm(rest_ring.pieces)],
        [me],
        [
            pltpu.VMEM((seq_len, part), BF16),
            pltpu.VMEM((seq_len, part), BF16),
            pltpu.VMEM((4 * seq_len, part), BF16),
            pltpu.VMEM((seq_len, 3 * part), BF16),
            pltpu.VMEM((seq_len, part), F32),
            pltpu.VMEM((seq_len, part), F32),
            pltpu.VMEM((pairs, diagonals, BLOCK, 2 * BLOCK), F32),
            pltpu.VMEM((heads, seq_len + BLOCK), F32),
            pltpu.VMEM((8 * heads * diagonals, BLOCK), F32),
            pltpu.VMEM((8 * heads * diagonals, BLOCK), F32),
            pltpu.VMEM((seq_len, width), F32),
            pltpu.VMEM((width, 3 * part), BF16),
            pltpu.VMEM((seq_len, ff_part), BF16),
            pltpu.VMEM((ff_part, width), BF16),
            dma(4),
            dma(4),
            dma(4),
            dma(count),
            dma(1),
            dma(count),
        ],
        micros=9.4,
    )
    if not aligned:
        table = jnp.zeros((head_total * bucket_count,), F32)
        table = lax.dynamic_update_slice_in_dim(table, small[4, :BLOCK], me_sp * BLOCK, 0)
        packed = [small[at].reshape(dp_count, -1) for at in range(4)] + [table.reshape(dp_count, -1)]
        packed = jnp.concatenate(packed, axis=1).astype(BF16)
        packed = jnp.pad(packed, ((0, 0), (0, 4 * part - packed.shape[1])))
        packed = jnp.pad(packed[:, None], ((0, 0), (0, SMALL_ROWS - 1), (0, 0)))
        last = jnp.concatenate([last, packed], axis=1)
    last_grads = ScatterRing(last, hold((up_first, down_first), *feed_grads.sent()), me, dp_count)
    last_grads.step()
    near_both = swap(hold(send_both, *feed_grads.sent()), 1)
    feed_grads.step(small)
    last_grads.step(*feed_grads.sums(), near_both)
    sent_both = add_far(hold(far_both, *last_grads.sums()), near_both)
    last_both = swap(sent_both, 2)
    sum_feed = feed_grads.finish(sent_both)
    feed_far, feed_near = swap(sum_feed, 2), swap(sum_feed, 1)
    last_grads.step(sum_feed)
    last_grads.step(last_both)
    sum_last = last_grads.finish()
    grad_input, output = call(
        ends_kernel,
        [shaped((tok, width), F32), shaped((tok, width), BF16)],
        [hold(own_one, sum_last), tokens, grad_resid, norm_gain, own_out, resid],
        [near_both, last_both],
        (),
        [pltpu.VMEM((2 * tok, width), BF16)] * 2 + [dma(2)],
        micros=1.6,
    )

    feed_last = swap(hold(feed_far, sum_last), 1)
    feed_pieces = [sum_feed, feed_near, feed_far, feed_last]
    last_far, last_near = swap(sum_last, 2), swap(sum_last, 1)
    piece = width // dp_count
    table_here = head_total * bucket_count // dp_count
    if aligned:
        out_in, out_down = call(
            wide_feed_kernel,
            [shaped((rows_here, ff), F32), shaped((sp_count * ff_rows, width), F32)],
            [],
            [hold(feed_pieces[0], sum_last)] + feed_pieces[1:],
            [me],
            [pltpu.VMEM((sp_count * rows_here, 2 * width), BF16), dma(4)],
        micros=3,
    )
        last_pieces = [sum_last, last_near, last_far, swap(hold(last_far, out_in, grad_input), 1)]
        out_qkv, out_out, gains, shifts, tables = call(
            wide_last_kernel,
            [
                shaped((rows_here, 3 * width), F32),
                shaped((rows_here, width), F32),
                shaped((2, piece), F32),
                shaped((2, piece), F32),
                shaped((1, table_here), F32),
            ],
            [],
            last_pieces,
            [me],
            [pltpu.VMEM((sp_count * (rows_here + SMALL_ROWS), width), BF16), dma(4)],
        micros=2.3,
    )
        tables = tables[0]
    else:
        all_feed = stacked_sp(feed_pieces).astype(F32)
        out_down = all_feed[:, :, width:].reshape(sp_count * ff_rows, width)
        all_in = all_feed[:, :, :width].reshape(sp_count, rows_here, dp_count, ff_rows)
        out_in = jnp.moveaxis(all_in, 0, 2).reshape(rows_here, ff)
        all_last = stacked_sp([sum_last, last_near, last_far, swap(last_far, 1)]).astype(F32)
        all_qkv = all_last[:, :rows_here, : 3 * part].reshape(sp_count, rows_here, 3, part)
        out_qkv = jnp.moveaxis(all_qkv, 0, 2).reshape(rows_here, 3 * width)
        out_out = jnp.moveaxis(all_last[:, :rows_here, 3 * part :], 0, 1).reshape(rows_here, width)
        small_row = jnp.sum(all_last[:, rows_here:], axis=0)[0]
        gains = small_row[: 2 * piece].reshape(2, piece)
        shifts = small_row[2 * piece : 4 * piece].reshape(2, piece)
        tables = small_row[4 * piece : 4 * piece + table_here]
    return (output[None], grad_input[None], out_qkv, out_out, out_in, out_down, gains, shifts, tables)


def solution(mesh):
    in_specs = (
        P("dp", "sp", None),
        P("dp", None),
        P("dp", None),
        P("dp", None),
        P("dp", None),
        P(),
        P(),
        P(),
        P("dp", None),
        P(),
        P("dp", "sp", None),
    )
    out_specs = (
        P("dp", "sp", None),
        P("dp", "sp", None),
        P("dp", None),
        P("dp", None),
        P("dp", None),
        P("dp", None),
        P(None, "dp"),
        P(None, "dp"),
        P("dp"),
    )
    return jax.shard_map(
        on_device, mesh=mesh, in_specs=in_specs, out_specs=out_specs, check_vma=False
    )
```
